32 devices in a mesh: dp: 4 (over z), expert: 8 (over y, x, core).
Axes of the slice: x: 2, y: 2, z: 4, core: 2. Of those that a mesh axis runs over, the one named last changes fastest.
Arguments:
- inputs: bfloat16 [8, 1024, 1536], P('dp', 'expert'), may hold values from -6 to 6
- cotangent: bfloat16 [8, 1024, 1536], P('dp', 'expert'), may hold values from -6 to 6
- routes: int32 [32, 256, 4], P(('dp', 'expert')), may hold values from 0 to 7, all different within a row; in each aligned block of 256 rows (0 to 255, 256 to 511, ..., all dimensions but the last counted through in order) at most 256 rows name the same one
- project_weight: float32 [1536, 2048], P(('dp', 'expert')), may hold values from -0.21875 to 0.21875
- project_moment: float32 [1536, 2048], P(('dp', 'expert')), may hold values from -64 to 64
- project_square: float32 [1536, 2048], P(('dp', 'expert')), may hold values from 215.57895 to 3449.2632
- output_weight: float32 [1536, 1536], P(('dp', 'expert')), may hold values from -0.875 to 0.875
- output_moment: float32 [1536, 1536], P(('dp', 'expert')), may hold values from -8 to 8
- output_square: float32 [1536, 1536], P(('dp', 'expert')), may hold values from 4.8188233 to 77.28302
- router_weight: float32 [1536, 8], P(('dp', 'expert')), may hold values from -0.078125 to 0.078125
- router_moment: float32 [1536, 8], P(('dp', 'expert')), may hold values from -1024 to 1024
- router_square: float32 [1536, 8], P(('dp', 'expert')), may hold values from 57344 to 913408
- norm_gains: float32 [2, 1536], P(None, ('dp', 'expert')), may hold values from 0.5 to 1.5
- gains_moment: float32 [2, 1536], P(None, ('dp', 'expert')), may hold values from -128 to 128
- gains_square: float32 [2, 1536], P(None, ('dp', 'expert')), may hold values from 819.2 to 13926.4
- expert_in: float32 [8, 1536, 1536], P('expert', 'dp'), may hold values from -0.15625 to 0.15625
- expert_in_moment: float32 [8, 1536, 1536], P('expert', 'dp'), may hold values from -32 to 32
- expert_in_square: float32 [8, 1536, 1536], P('expert', 'dp'), may hold values from 77.28302 to 1228.8
- expert_down: float32 [8, 768, 1536], P('expert', 'dp'), may hold values from -0.875 to 0.875
- expert_down_moment: float32 [8, 768, 1536], P('expert', 'dp'), may hold values from -6 to 6
- expert_down_square: float32 [8, 768, 1536], P('expert', 'dp'), may hold values from 2.4094117 to 38.64151
Outputs:
- outputs: float32 [8, 1024, 1536], P('dp', 'expert')
- input_grad: float32 [8, 1024, 1536], P('dp', 'expert')
- project_moment_new: float32 [1536, 2048], P(('dp', 'expert'))
- project_square_new: float32 [1536, 2048], P(('dp', 'expert'))
- project_weight_new: float32 [1536, 2048], P(('dp', 'expert'))
- output_moment_new: float32 [1536, 1536], P(('dp', 'expert'))
- output_square_new: float32 [1536, 1536], P(('dp', 'expert'))
- output_weight_new: float32 [1536, 1536], P(('dp', 'expert'))
- router_moment_new: float32 [1536, 8], P(('dp', 'expert'))
- router_square_new: float32 [1536, 8], P(('dp', 'expert'))
- router_weight_new: float32 [1536, 8], P(('dp', 'expert'))
- gains_moment_new: float32 [2, 1536], P(None, ('dp', 'expert'))
- gains_square_new: float32 [2, 1536], P(None, ('dp', 'expert'))
- norm_gains_new: float32 [2, 1536], P(None, ('dp', 'expert'))
- expert_in_moment_new: float32 [8, 1536, 1536], P('expert', 'dp')
- expert_in_square_new: float32 [8, 1536, 1536], P('expert', 'dp')
- expert_in_new: float32 [8, 1536, 1536], P('expert', 'dp')
- expert_down_moment_new: float32 [8, 768, 1536], P('expert', 'dp')
- expert_down_square_new: float32 [8, 768, 1536], P('expert', 'dp')
- expert_down_new: float32 [8, 768, 1536], P('expert', 'dp')
The draws below stay inside these ranges and needn't reach their ends.
Inputs may be any that keep to these rules, and one draw needn't show every extreme that they name: Each row names 4 different experts. Among the rows of one device (one block of routes) no expert is named more than 256 times, a bound that some block reaches.
All inputs are finite; a program needn't handle non-finite values.
Results may differ from the reference program's by a relative error of at most 0.022.
The reference program's roundings to bfloat16 on the way count: a program that leaves them out, or rounds other values in their place, can miss the bound.
Values may be sent and summed in bfloat16 or wider, within the bound.
No kernel may reach another device: no remote copies, remote signals or barrier semaphores. Data moves between devices by JAX's collectives and lax.ppermute only.
A program may use at most 256 MiB of HBM per device.

```python
import math
import jax
import jax.numpy as jnp
import numpy as np
from jax import lax

D = 1536
H = 12
KVH = 2
HD = 128
FF = 768
TOP = 4
SEQS = 2
STRETCH = 128
STEP = 10
EXPERTS = 8
SEQ = 1024
BATCH = 8
CAP = 256
QKV = 2048
N_DP = 4
N_EXPERT = 8


def shard_levels(own_key, extent, cuts, least, largest):
    factor_of, own = 1.0, jax.random.fold_in(own_key, 6)
    for position, parts in cuts:
        heights = jnp.exp(jax.random.uniform(jax.random.fold_in(own, position), (parts,), jnp.float32, least / len(cuts), largest / len(cuts)))
        factor_of = factor_of * jnp.repeat(heights, extent[position] // parts).reshape([-1 if axis == position else 1 for axis in range(len(extent))])
    return factor_of


def deal_out(rng, own, number, rows, amount, top, limit, lean):
    sequence = jax.random.permutation(rng, amount)
    crowded, common = shares(amount, rows * top, limit, lean, True), shares(amount, rows * top, limit, lean, False)
    places = jnp.arange(amount)

    def named(sizes, turn):
        used = int((sizes > 0).sum())
        fixed = max(1, used // 4)
        shifted = fixed + (places - fixed + turn * (used - fixed)) % max(1, amount - fixed)
        return jnp.zeros((amount,), jnp.int32).at[sequence[jnp.where(places < fixed, places, shifted)]].set(jnp.asarray(sizes, jnp.int32))

    sizes = jnp.where(number % 4 == 0, named(crowded, number // 4), named(common, number - number // 4 - 1))
    mixed = jax.random.permutation(jax.random.fold_in(own, 3), amount)
    source_of, taker = mixed[0:amount // 2 * 2:2], mixed[1:amount // 2 * 2:2]
    room = jnp.minimum(sizes[source_of] - 1, limit - sizes[taker]) // 2
    room = jnp.where((source_of == sequence[0]) | (taker == sequence[0]) | (sizes[taker] == 0), 0, jnp.maximum(room, 0))
    shifted = jax.random.randint(jax.random.fold_in(own, 4), (amount // 2,), 0, 1 << 20) % (room + 1)
    sizes = sizes.at[source_of].add(-shifted).at[taker].add(shifted)
    labels = jnp.searchsorted(jnp.cumsum(sizes), jnp.arange(rows * top), side="right").astype(jnp.int32)
    listing = labels.reshape(top, rows).T
    listing = listing[jax.random.permutation(jax.random.fold_in(own, 1), rows)]
    turn = jax.random.randint(jax.random.fold_in(own, 2), (rows, 1), 0, top)
    return jnp.take_along_axis(listing, (jnp.arange(top)[None, :] + turn) % top, axis=1)


def shares(count, total, limit, lean, full):
    portions = [(1 << 20) // math.isqrt(standing ** lean) + 1 for standing in range(1, count + 1)]
    largest = limit if full else min(limit, max(-(-total // count), total * portions[0] // sum(portions)))
    least = 1 if total - largest >= count - 1 else 0
    counts, spare = [largest] + [least] * (count - 1), total - largest - least * (count - 1)
    while spare > 0:
        candidates = [i for i in range(1, count) if counts[i] < largest] or [i for i in range(1, count) if counts[i] < limit]
        mass, budget = sum([portions[i] for i in candidates]), spare
        for i in candidates:
            more = min(limit - counts[i], max(1, budget * portions[i] // mass), spare)
            counts[i] = counts[i] + more
            spare = spare - more
    return np.array(counts)


def centred(key, shape, scale, reach, split=(), kind=jnp.bfloat16):
    entries = scale * jax.random.normal(key, shape, jnp.float32)
    if split:
        entries = entries * shard_levels(key, shape, split, -0.22, 0.18)
    return jnp.clip(entries, -reach, reach).astype(kind)


def setup_inputs(seed: int = 0) -> dict:
    key_of = jax.random.split(jax.random.key(seed), 22)
    inputs = centred(key_of[0], (BATCH, SEQ, D), 1.0, 6.0, ((0, 4), (1, 8)))
    cotangent = centred(key_of[1], (BATCH, SEQ, D), 1.0, 6.0, ((0, 4), (1, 8)))
    routes_keys = jax.random.split(jax.random.fold_in(key_of[2], 1), (N_DP * N_EXPERT) * (SEQS * STRETCH) // (SEQS * STRETCH))
    routes_turns = jax.random.permutation(jax.random.fold_in(key_of[2], 3), (N_DP * N_EXPERT) * (SEQS * STRETCH) // (SEQS * STRETCH))
    routes = jax.vmap(lambda own, number: deal_out(jax.random.fold_in(key_of[2], 2), own, number, SEQS * STRETCH, EXPERTS, TOP, CAP, 1))(routes_keys, routes_turns).reshape((N_DP * N_EXPERT, SEQS * STRETCH, TOP))
    project_weight = centred(key_of[3], (D, QKV), (D // 2) ** -0.5, 0.21875, ((0, 32),), jnp.float32)
    project_moment = centred(key_of[4], (D, QKV), ((N_DP * SEQS * SEQ) ** 0.5 / 9), 64.0, ((0, 32),), jnp.float32)
    project_square = jnp.clip(jnp.exp(math.log(3449.2632) - 2.7725887 * jax.random.uniform(key_of[5], (D, QKV), jnp.float32) ** shard_levels(key_of[5], (D, QKV), ((0, 32),), -0.2, 0.2)), 215.57895, 3449.2632)
    output_weight = centred(key_of[6], (H * HD, D), (H * HD * 32 // SEQ) ** -0.5, 0.875, ((0, 32),), jnp.float32)
    output_moment = centred(key_of[7], (H * HD, D), ((N_DP * SEQS * SEQ) ** 0.5 / 60), 8.0, ((0, 32),), jnp.float32)
    output_square = jnp.clip(jnp.exp(math.log(77.28302) - 2.7749445 * jax.random.uniform(key_of[8], (H * HD, D), jnp.float32) ** shard_levels(key_of[8], (H * HD, D), ((0, 32),), -0.2, 0.2)), 4.8188233, 77.28302)
    router_weight = centred(key_of[9], (D, EXPERTS), (4 * D) ** -0.5, 0.078125, ((0, 32),), jnp.float32)
    router_moment = centred(key_of[10], (D, EXPERTS), (2.6 * (N_DP * SEQS * SEQ * TOP / EXPERTS) ** 0.5), 1024.0, ((0, 32),), jnp.float32)
    router_square = jnp.clip(jnp.exp(math.log(913408.0) - 2.7681144 * jax.random.uniform(key_of[11], (D, EXPERTS), jnp.float32) ** shard_levels(key_of[11], (D, EXPERTS), ((0, 32),), -0.2, 0.2)), 57344.0, 913408.0)
    norm_gains = jnp.clip(1.0 + 0.1 * jax.random.normal(key_of[12], (2, D), jnp.float32), 0.5, 1.5)
    gains_moment = centred(key_of[13], (2, D), (0.22 * (N_DP * SEQS * SEQ) ** 0.5), 128.0, ((1, 32),), jnp.float32)
    gains_square = jnp.clip(jnp.exp(math.log(13926.4) - 2.8332134 * jax.random.uniform(key_of[14], (2, D), jnp.float32) ** shard_levels(key_of[14], (2, D), ((1, 32),), -0.2, 0.2)), 819.2, 13926.4)
    expert_in = centred(key_of[15], (EXPERTS, D, 2 * FF), D ** -0.5, 0.15625, ((0, 8), (1, 4)), jnp.float32)
    expert_in_moment = centred(key_of[16], (EXPERTS, D, 2 * FF), (0.094 * (N_DP * SEQS * SEQ * TOP / EXPERTS) ** 0.5), 32.0, ((0, 8), (1, 4)), jnp.float32)
    expert_in_square = jnp.clip(jnp.exp(math.log(1228.8) - 2.766319 * jax.random.uniform(key_of[17], (EXPERTS, D, 2 * FF), jnp.float32) ** shard_levels(key_of[17], (EXPERTS, D, 2 * FF), ((0, 8), (1, 4)), -0.2, 0.2)), 77.28302, 1228.8)
    expert_down = centred(key_of[18], (EXPERTS, FF, D), (FF // 16) ** -0.5, 0.875, ((0, 8), (1, 4)), jnp.float32)
    expert_down_moment = centred(key_of[19], (EXPERTS, FF, D), ((N_DP * SEQS * SEQ * TOP / EXPERTS) ** 0.5 / 60), 6.0, ((0, 8), (1, 4)), jnp.float32)
    expert_down_square = jnp.clip(jnp.exp(math.log(38.64151) - 2.7749445 * jax.random.uniform(key_of[20], (EXPERTS, FF, D), jnp.float32) ** shard_levels(key_of[20], (EXPERTS, FF, D), ((0, 8), (1, 4)), -0.2, 0.2)), 2.4094117, 38.64151)
    return dict(inputs=inputs, cotangent=cotangent, routes=routes, project_weight=project_weight, project_moment=project_moment, project_square=project_square, output_weight=output_weight, output_moment=output_moment, output_square=output_square, router_weight=router_weight, router_moment=router_moment, router_square=router_square, norm_gains=norm_gains, gains_moment=gains_moment, gains_square=gains_square, expert_in=expert_in, expert_in_moment=expert_in_moment, expert_in_square=expert_in_square, expert_down=expert_down, expert_down_moment=expert_down_moment, expert_down_square=expert_down_square)


@jax.custom_vjp
def low(v):
    return lax.optimization_barrier(v.astype(jnp.bfloat16)).astype(jnp.float32)

@jax.custom_vjp
def low_back(v):
    return v

def low_keep(v):
    return (low(v), None)

def low_pass(kept, grad):
    return (grad,)

def back_keep(v):
    return (v, None)

def back_low(kept, grad):
    return (low(grad),)
low.defvjp(low_keep, low_pass)
low_back.defvjp(back_keep, back_low)
norm_epsilon = 1e-06
adam_epsilon = 1e-08
beta_first = 0.9
beta_second = 0.95
weight_decay = 0.1
rope_base = 1000000.0
masked_score = -1e+30

def product(left_side, right_side):
    return jnp.dot(left_side, right_side, precision=lax.Precision.HIGHEST, preferred_element_type=jnp.float32)

def rms_norm(values, gain_row):
    factor = lax.rsqrt(lax.optimization_barrier(jnp.mean(values * values, axis=-1, keepdims=True)) + norm_epsilon)
    return values * factor * gain_row

def rotate(values, positions):
    half_width = values.shape[-1] // 2
    frequency = rope_base ** (-jnp.arange(half_width, dtype=jnp.float32) / half_width)
    angles = positions.astype(jnp.float32)[:, None] * frequency[None, :]
    cosine = jnp.cos(angles)[:, None, :]
    sine_part = jnp.sin(angles)[:, None, :]
    first_half = values[..., :half_width]
    second_half = values[..., half_width:]
    return jnp.concatenate([first_half * cosine - second_half * sine_part, second_half * cosine + first_half * sine_part], axis=-1)

def gated_unit(gate_up):
    return jax.nn.gelu(gate_up[..., :FF], approximate=True) * gate_up[..., FF:]

def slot_tables(route_block):
    flat_routes = route_block.reshape(-1)
    pick_count = flat_routes.shape[0]
    onehot = (flat_routes[:, None] == jnp.arange(EXPERTS, dtype=jnp.int32)[None, :]).astype(jnp.int32)
    earlier = jnp.cumsum(onehot, axis=0) - onehot
    rank_values = lax.optimization_barrier(jnp.sum(earlier * onehot, axis=1))
    slot_index = flat_routes * CAP + rank_values
    slot_table = jnp.full((EXPERTS * CAP,), pick_count, jnp.int32).at[slot_index].set(jnp.arange(pick_count, dtype=jnp.int32))
    return (slot_index, slot_table)

def attend_sequence(operands):
    queries, rotated_keys, values = operands
    group_size = H // KVH
    keys_wide = jnp.repeat(rotated_keys, group_size, axis=1)
    values_wide = jnp.repeat(values, group_size, axis=1)
    block_rows = min(512, SEQ)
    query_blocks = queries.reshape(SEQ // block_rows, block_rows, H, HD)
    block_starts = jnp.arange(SEQ // block_rows, dtype=jnp.int32) * block_rows
    key_positions = jnp.arange(SEQ, dtype=jnp.int32)

    def one_block(block_args):
        query_block, block_start = block_args
        scores = low_back(jnp.einsum('qhd,khd->hqk', query_block, keys_wide, precision=lax.Precision.HIGHEST) * HD ** (-0.5))
        query_positions = block_start + jnp.arange(block_rows, dtype=jnp.int32)
        allowed = key_positions[None, :] <= query_positions[:, None]
        scores = jnp.where(allowed[None], scores, masked_score)
        softmax_rows = low(jax.nn.softmax(scores, axis=-1))
        return jnp.einsum('hqk,khd->qhd', softmax_rows, values_wide, precision=lax.Precision.HIGHEST)
    mixed_rows = lax.map(jax.checkpoint(one_block), (query_blocks, block_starts))
    return mixed_rows.reshape(SEQ, H, HD)

def expert_rows(operands):
    rows_in, inner_weight, outer_weight = operands
    gate_up = low_back(product(rows_in, inner_weight))
    hidden = low(gated_unit(gate_up))
    return low(low_back(product(hidden, outer_weight)))

def layer_forward(group_inputs, weights, group_routes):
    project_copy = low(weights[0])
    output_copy = low(weights[1])
    router_copy = low(weights[2])
    gains_copy = low(weights[3])
    in_copy = low(weights[4])
    down_copy = low(weights[5])
    row_count = SEQS * STRETCH
    query_width = H * HD
    key_width = KVH * HD
    tokens = group_inputs.reshape(SEQS * SEQ, D)
    normed_one = low(rms_norm(tokens, gains_copy[0]))
    projected = low_back(product(normed_one, project_copy)).reshape(SEQS, SEQ, QKV)
    positions = jnp.arange(SEQ, dtype=jnp.int32)
    queries = low(rotate(projected[..., :query_width].reshape(SEQS, SEQ, H, HD), positions))
    rotated_keys = low(rotate(projected[..., query_width:query_width + key_width].reshape(SEQS, SEQ, KVH, HD), positions))
    values = low(projected[..., query_width + key_width:].reshape(SEQS, SEQ, KVH, HD))
    mixed_rows = lax.map(attend_sequence, (queries, rotated_keys, values))
    mixed_rows = low(low_back(mixed_rows.reshape(SEQS * SEQ, query_width)))
    hidden_one = tokens + low_back(product(mixed_rows, output_copy))
    normed_two = low(rms_norm(hidden_one, gains_copy[1]))
    logits = low_back(product(normed_two, router_copy))
    by_device = normed_two.reshape(SEQS, N_EXPERT, STRETCH, D).transpose(1, 0, 2, 3).reshape(N_EXPERT, row_count, D)
    device_logits = logits.reshape(SEQS, N_EXPERT, STRETCH, EXPERTS).transpose(1, 0, 2, 3).reshape(N_EXPERT, row_count, EXPERTS)
    chosen = jnp.take_along_axis(device_logits, group_routes, axis=2)
    gate_weights = jax.nn.softmax(chosen, axis=-1)
    slot_index, slot_table = jax.vmap(slot_tables)(group_routes)
    padded = jnp.concatenate([by_device, jnp.zeros((N_EXPERT, 1, D), jnp.float32)], axis=1)
    sent_rows = low_back(jax.vmap(lambda source_rows, row_index: source_rows[row_index])(padded, slot_table // TOP))
    arrived = sent_rows.reshape(N_EXPERT, EXPERTS, CAP, D).transpose(1, 0, 2, 3).reshape(EXPERTS, N_EXPERT * CAP, D)
    results = lax.map(jax.checkpoint(expert_rows), (arrived, in_copy, down_copy))
    returned = results.reshape(EXPERTS, N_EXPERT, CAP, D).transpose(1, 0, 2, 3).reshape(N_EXPERT, EXPERTS * CAP, D)
    picked = jax.vmap(lambda source_rows, row_index: source_rows[row_index])(returned, slot_index)
    picked = picked.reshape(N_EXPERT, row_count, TOP, D)
    mixture = lax.optimization_barrier(jnp.sum(gate_weights[..., None] * picked, axis=2))
    mixture = mixture.reshape(N_EXPERT, SEQS, STRETCH, D).transpose(1, 0, 2, 3).reshape(SEQS * SEQ, D)
    return (hidden_one + mixture).reshape(SEQS, SEQ, D)

def adam_update(weight, moment, square, gradient, step_rate, shrink):
    moment_new = beta_first * moment + (1.0 - beta_first) * gradient
    square_new = beta_second * square + (1.0 - beta_second) * gradient * gradient
    normalized = moment_new / (1.0 - beta_first ** STEP) / (jnp.sqrt(square_new / (1.0 - beta_second ** STEP)) + adam_epsilon)
    return (moment_new, square_new, weight - step_rate * (normalized + shrink * weight))

def reference(inputs, cotangent, routes, project_weight, project_moment, project_square, output_weight, output_moment, output_square, router_weight, router_moment, router_square, norm_gains, gains_moment, gains_square, expert_in, expert_in_moment, expert_in_square, expert_down, expert_down_moment, expert_down_square):
    weights = (project_weight, output_weight, router_weight, norm_gains, expert_in, expert_down)
    all_inputs = inputs.astype(jnp.float32).reshape(N_DP, SEQS, SEQ, D)
    all_cotangents = cotangent.astype(jnp.float32).reshape(N_DP, SEQS, SEQ, D)
    all_routes = routes.reshape(N_DP, N_EXPERT, SEQS * STRETCH, TOP)

    def one_group(totals, group_args):
        group_inputs, group_cotangent, group_routes = group_args
        group_outputs, pullback = jax.vjp(lambda values, params: layer_forward(values, params, group_routes), group_inputs, weights)
        input_grad, weight_grads = pullback(group_cotangent)
        return (jax.tree.map(jnp.add, totals, weight_grads), (group_outputs, input_grad))
    start_totals = jax.tree.map(jnp.zeros_like, weights)
    gradients, (outputs, input_grads) = lax.scan(one_group, start_totals, (all_inputs, all_cotangents, all_routes))
    rate_project = 3.0 * (2.0 / D) ** 0.5
    rate_output = 3.0 * (SEQ / (32.0 * H * HD)) ** 0.5
    rate_router = 1.5 / D ** 0.5
    rate_gains = 0.8
    rate_in = 3.0 / D ** 0.5
    rate_down = 12.0 / FF ** 0.5
    project_new = adam_update(project_weight, project_moment, project_square, gradients[0], rate_project, weight_decay)
    output_new = adam_update(output_weight, output_moment, output_square, gradients[1], rate_output, weight_decay)
    router_new = adam_update(router_weight, router_moment, router_square, gradients[2], rate_router, weight_decay)
    gains_new = adam_update(norm_gains, gains_moment, gains_square, gradients[3], rate_gains, 0.0)
    in_new = adam_update(expert_in, expert_in_moment, expert_in_square, gradients[4], rate_in, weight_decay)
    down_new = adam_update(expert_down, expert_down_moment, expert_down_square, gradients[5], rate_down, weight_decay)
    return (outputs.reshape(N_DP * SEQS, SEQ, D), input_grads.reshape(N_DP * SEQS, SEQ, D), project_new[0], project_new[1], project_new[2], output_new[0], output_new[1], output_new[2], router_new[0], router_new[1], router_new[2], gains_new[0], gains_new[1], gains_new[2], in_new[0], in_new[1], in_new[2], down_new[0], down_new[1], down_new[2])
```

```python
import jax
import jax.numpy as jnp
from jax import lax
from jax.experimental import pallas as pl
from jax.experimental.pallas import tpu as pltpu
from jax.sharding import PartitionSpec as P

D = 1536
H = 12
KVH = 2
HD = 128
FF = 768
TOP = 4
STEP = 10
GROUP = H // KVH
QW = H * HD
KW = KVH * HD
QKV = QW + 2 * KW
EXP_DEV = 1
EXTRA = 128

norm_epsilon = 1e-06
adam_epsilon = 1e-08
beta_first = 0.9
beta_second = 0.95
weight_decay = 0.1
rope_base = 1000000.0
masked_score = -1e30
score_scale = HD ** (-0.5)
BF = jnp.bfloat16
F32 = jnp.float32


def dot(a, b, da, db):
    return lax.dot_general(a, b, (((da,), (db,)), ((), ())), preferred_element_type=F32)


def after(value, *others):
    return lax.optimization_barrier((value, *others))[0]


def hop(value, mask):
    return lax.ppermute(value, "expert", [(i, i ^ mask) for i in range(8)])


def total(one, two):
    return (one.astype(F32) + two.astype(F32)).astype(one.dtype)


def gather_blocks(value):
    half = value.shape[0] // 2
    by_x, by_y = hop(value, 2), hop(value, 4)
    sibling = hop(value, 1)
    first, second = hop(by_x[:half], 4), hop(by_y[half:], 2)
    diagonal = jnp.concatenate([first, second], axis=0)
    return [value, sibling, by_x, hop(by_x, 1), by_y, hop(by_y, 1), diagonal, hop(diagonal, 1)]


def reduce_blocks(blocks, meanwhile=()):
    half = blocks[0].shape[0] // 2
    diagonal = total(blocks[6], hop(blocks[7], 1))
    over_x, over_y = hop(diagonal[:half], 2), hop(diagonal[half:], 4)
    by_x = total(blocks[2], hop(blocks[3], 1))
    by_y = total(blocks[4], hop(blocks[5], 1))
    by_y = jnp.concatenate([total(by_y[:half], over_x), by_y[half:]], axis=0)
    by_x = jnp.concatenate([by_x[:half], total(by_x[half:], over_y)], axis=0)
    last_x, last_y = hop(by_x, 2), hop(by_y, 4)
    own = total(blocks[0], hop(blocks[1], 1))
    if meanwhile:
        last_x = after(last_x, *meanwhile)
    return own.astype(F32) + last_x.astype(F32) + last_y.astype(F32)


def gather_plane(shard):
    mine = lax.axis_index("dp")
    plane = lax.dynamic_update_slice(
        jnp.zeros((4,) + shard.shape, shard.dtype), shard[None], (mine, 0, 0)
    )
    for shift in (1, 2, 3):
        block = lax.ppermute(shard, "dp", [(i, (i + shift) % 4) for i in range(4)])
        plane = lax.dynamic_update_slice(plane, block[None], ((mine - shift) % 4, 0, 0))
    return plane


def whole_rows(blocks):
    whole = jnp.zeros((4, 8) + blocks[0].shape[1:], blocks[0].dtype)
    for k, block in enumerate(blocks):
        whole = lax.dynamic_update_slice(
            whole, block[:, None], (0, lax.axis_index("expert") ^ k, 0, 0)
        )
    return whole.reshape(-1, whole.shape[-1])


def scatter_rows(gradient, meanwhile=()):
    width = gradient.shape[1]
    grid = gradient.astype(BF).reshape(4, 8, -1, width)
    rows = grid.shape[2]
    blocks = [
        lax.dynamic_slice(
            grid, (0, lax.axis_index("expert") ^ k, 0, 0), (4, 1, rows, width)
        ).reshape(4, rows, width)
        for k in range(8)
    ]
    plane = reduce_blocks(blocks, meanwhile)
    mine = lax.axis_index("dp")
    result = lax.dynamic_index_in_dim(plane, mine, 0, keepdims=False)
    sent = plane.astype(BF)
    for shift in (1, 2, 3):
        block = lax.dynamic_index_in_dim(sent, (mine + shift) % 4, 0, keepdims=False)
        arrived = lax.ppermute(block, "dp", [(i, (i + shift) % 4) for i in range(4)])
        result = result + arrived.astype(F32)
    return result


def key_block(kv_ref, row):
    return jnp.concatenate(
        [kv_ref[n, row : row + HD, :].astype(F32).T for n in range(kv_ref.shape[0])], axis=0
    ).astype(BF)


def forward_kernel(q_ref, kv_ref, bias_ref, mixed_ref, lse_ref):
    for g in range(KVH):
        keys = key_block(kv_ref, g * HD)
        values = jnp.concatenate(
            [kv_ref[n, KW + g * HD : KW + (g + 1) * HD, :] for n in range(kv_ref.shape[0])], axis=1
        )
        for h in range(g * GROUP, (g + 1) * GROUP):
            scores = dot(keys, q_ref[h], 1, 0) * score_scale + bias_ref[...]
            top = jnp.max(scores, axis=0, keepdims=True)
            weights = jnp.exp(scores - top)
            amount = jnp.sum(weights, axis=0, keepdims=True)
            mixed_ref[h] = dot(values, weights.astype(BF), 1, 0) / amount
            lse_ref[0, h : h + 1, :] = top + jnp.log(amount)


def backward_kernel(q_ref, kv_ref, bias_ref, mixed_ref, lse_ref, grad_ref, dq_ref, dkv_ref):
    blocks, stretch = kv_ref.shape[0], kv_ref.shape[2]
    for g in range(KVH):
        keys, values = key_block(kv_ref, g * HD), key_block(kv_ref, KW + g * HD)
        keys_flat = jnp.concatenate(
            [kv_ref[n, g * HD : (g + 1) * HD, :] for n in range(blocks)], axis=1
        )
        key_grad = jnp.zeros(keys.shape, F32)
        value_grad = jnp.zeros(keys.shape, F32)
        for h in range(g * GROUP, (g + 1) * GROUP):
            query, grad = q_ref[h], grad_ref[h]
            scores = dot(keys, query, 1, 0) * score_scale + bias_ref[...]
            probs = jnp.exp(scores - lse_ref[0, h : h + 1, :])
            delta = jnp.sum(mixed_ref[h] * grad.astype(F32), axis=0, keepdims=True)
            score_grad = (probs * (dot(values, grad, 1, 0) - delta)).astype(BF)
            dq_ref[h] = dot(keys_flat, score_grad, 1, 0) * score_scale
            key_grad += dot(score_grad, query, 1, 1)
            value_grad += dot(probs.astype(BF), grad, 1, 1)
        key_grad = (key_grad * score_scale).astype(BF)
        value_grad = value_grad.astype(BF)
        for n in range(blocks):
            part = slice(n * stretch, (n + 1) * stretch)
            dkv_ref[n, :, g * HD : (g + 1) * HD] = key_grad[part]
            dkv_ref[n, :, KW + g * HD : KW + (g + 1) * HD] = value_grad[part]


def attention_call(kernel, outs, out_specs, queries, pairs, bias, *more):
    blocks, _, tokens = pairs.shape
    stretch = bias.shape[1]
    head = pl.BlockSpec((H, HD, stretch), lambda s: (0, 0, s))
    row = pl.BlockSpec((1, H, stretch), lambda s: (s, 0, 0))
    specs = [
        head,
        pl.BlockSpec((blocks, 2 * KW, stretch), lambda s: (0, 0, s)),
        pl.BlockSpec(bias.shape, lambda s: (0, 0)),
        head,
        row,
        head,
    ]
    keys = blocks * stretch
    return pl.pallas_call(
        kernel,
        grid=(tokens // stretch,),
        in_specs=specs[: 3 + len(more)],
        out_specs=[head if s == "head" else row if s == "row" else s for s in out_specs],
        out_shape=outs,
        compiler_params=pltpu.CompilerParams(vmem_limit_bytes=56 * 1024 * 1024),
        cost_estimate=pl.CostEstimate(
            flops=(4 if not more else 10) * H * HD * tokens * keys,
            bytes_accessed=8 * 1024 * 1024,
            transcendentals=H * tokens * keys,
        ),
    )(queries, pairs, bias, *more)


def joined(refs):
    return jnp.concatenate([ref[...] for ref in refs], axis=0)


def inner(weight_ref):
    return jnp.concatenate([weight_ref[a, : D // 4] for a in range(4)], axis=0)


def outer(weight_ref):
    return jnp.concatenate([weight_ref[a, D // 4 :] for a in range(4)], axis=0)


def expert_kernel(
    me_ref,
    row0_ref,
    row1_ref,
    grad0_ref,
    grad1_ref,
    bias_ref,
    weight_ref,
    router_ref,
    out0_ref,
    out1_ref,
    gate_up_ref,
    hidden_ref,
    columns_ref,
    gates_ref,
):
    rows, grads = joined([row0_ref, row1_ref]), joined([grad0_ref, grad1_ref])
    half = row0_ref.shape[0]
    lanes = lax.broadcasted_iota(jnp.int32, (2 * half, EXTRA), 1)
    logits = dot(rows, router_ref[...], 1, 0) + bias_ref[...]
    parts = jnp.exp(logits - jnp.max(logits, axis=1, keepdims=True))
    gates = parts / jnp.sum(parts, axis=1, keepdims=True)
    gates_ref[...] = gates
    mine = jnp.sum(jnp.where(lanes == me_ref[0], gates, 0.0), axis=1, keepdims=True)
    gate_up = dot(rows, inner(weight_ref), 1, 0)
    hidden, slope_gate, slope_up = gated(gate_up[:, :FF], gate_up[:, FF:])
    hidden_low = hidden.astype(BF)
    weighted = (mine * dot(hidden_low, outer(weight_ref), 1, 0)).astype(BF)
    out0_ref[...] = weighted[:half]
    out1_ref[...] = weighted[half:]
    hidden_grad = dot(grads, outer(weight_ref), 1, 1)
    hidden = hidden_low.astype(F32)
    gate_grad = jnp.sum(hidden * hidden_grad, axis=1, keepdims=True)
    high = gate_grad.astype(BF).astype(F32)
    columns_ref[...] = (
        jnp.where(lanes == me_ref[0], high, 0.0)
        + jnp.where(lanes == me_ref[0] + 8, gate_grad - high, 0.0)
    ).astype(BF)
    hidden_grad = hidden_grad * mine
    gate_up_ref[:, :FF] = (hidden_grad * slope_gate).astype(BF)
    gate_up_ref[:, FF:] = (hidden_grad * slope_up).astype(BF)
    hidden = (mine * hidden).astype(BF)
    for a in range(4):
        hidden_ref[a] = hidden[:, a * (FF // 4) : (a + 1) * (FF // 4)]


def expert_call(me, rows, grads, bias, weight, router):
    count, width = rows[0].shape
    vmem = pl.BlockSpec(memory_space=pltpu.VMEM)
    shape = jax.ShapeDtypeStruct
    return pl.pallas_call(
        expert_kernel,
        in_specs=[pl.BlockSpec(memory_space=pltpu.SMEM)] + [vmem] * 7,
        out_specs=[vmem] * 6,
        out_shape=[
            shape((count, width), BF),
            shape((count, width), BF),
            shape((2 * count, 2 * FF), BF),
            shape((4, 2 * count, FF // 4), BF),
            shape((2 * count, EXTRA), BF),
            shape((2 * count, EXTRA), F32),
        ],
        compiler_params=pltpu.CompilerParams(vmem_limit_bytes=56 * 1024 * 1024),
        cost_estimate=pl.CostEstimate(
            flops=2 * 2 * count * 4 * FF * width,
            bytes_accessed=20 * 1024 * 1024,
            transcendentals=2 * count * FF,
        ),
    )(me, *rows, *grads, bias, weight, router)


def weight_kernel(*refs):
    rows, grads, gate_ups, hiddens, out_ref = refs[:8], refs[8:16], refs[16:20], refs[20:24], refs[24]
    out_ref[0, : D // 4] = dot(joined(rows), joined(gate_ups), 0, 0).astype(BF)
    hidden = jnp.concatenate([ref[0] for ref in hiddens], axis=0)
    out_ref[0, D // 4 :] = dot(hidden, joined(grads), 0, 0).astype(BF)


def weight_call(rows, grads, gate_ups, hiddens):
    count, width = rows[0].shape
    share = D // 4 + FF // 4
    fixed = lambda a: (0, 0)
    return pl.pallas_call(
        weight_kernel,
        grid=(4,),
        in_specs=[pl.BlockSpec((count, D // 4), lambda a: (0, a))] * 8
        + [pl.BlockSpec((count, width), fixed)] * 8
        + [pl.BlockSpec((2 * count, 2 * FF), fixed)] * 4
        + [pl.BlockSpec((1, 2 * count, FF // 4), lambda a: (a, 0, 0))] * 4,
        out_specs=pl.BlockSpec((1, share, width), lambda a: (a, 0, 0)),
        out_shape=jax.ShapeDtypeStruct((4, share, width), BF),
        compiler_params=pltpu.CompilerParams(vmem_limit_bytes=60 * 1024 * 1024),
        cost_estimate=pl.CostEstimate(
            flops=2 * 8 * count * 3 * FF * width,
            bytes_accessed=32 * 1024 * 1024,
            transcendentals=0,
        ),
    )(*rows, *grads, *gate_ups, *hiddens)


def copy_kernel(gate_up_ref, columns_ref, weight_ref, out0_ref, out1_ref):
    half = out0_ref.shape[0]
    copies = dot(gate_up_ref[...], inner(weight_ref), 1, 1).astype(BF)
    for n, ref in enumerate((out0_ref, out1_ref)):
        ref[:, :D] = copies[n * half : (n + 1) * half]
        ref[:, D:] = columns_ref[n * half : (n + 1) * half]


def copy_call(gate_up, columns, weight):
    count, width = gate_up.shape[0] // 2, D + EXTRA
    vmem = pl.BlockSpec(memory_space=pltpu.VMEM)
    return pl.pallas_call(
        copy_kernel,
        in_specs=[vmem] * 3,
        out_specs=[vmem] * 2,
        out_shape=[jax.ShapeDtypeStruct((count, width), BF)] * 2,
        compiler_params=pltpu.CompilerParams(vmem_limit_bytes=56 * 1024 * 1024),
        cost_estimate=pl.CostEstimate(
            flops=2 * 2 * count * 2 * FF * D, bytes_accessed=10 * 1024 * 1024, transcendentals=0
        ),
    )(gate_up, columns, weight)


def rms_factor(values):
    return lax.rsqrt(jnp.mean(values * values, axis=-1, keepdims=True) + norm_epsilon)


def rms_back(gradient, values, factor, gain):
    scaled = gradient * gain
    inner = jnp.mean(scaled * values, axis=-1, keepdims=True)
    return (
        factor * scaled - values * (factor * factor * factor * inner),
        jnp.sum(gradient * values * factor, axis=0),
    )


def turn(heads, cosine, sine):
    half = HD // 2
    first, second = heads[:, :half], heads[:, half:]
    return jnp.concatenate(
        [first * cosine - second * sine, second * cosine + first * sine], axis=1
    )


def adam_update(weight, moment, square, gradient, step_rate, shrink):
    moment_new = beta_first * moment + (1.0 - beta_first) * gradient
    square_new = beta_second * square + (1.0 - beta_second) * gradient * gradient
    normalized = (
        moment_new
        / (1.0 - beta_first**STEP)
        / (jnp.sqrt(square_new / (1.0 - beta_second**STEP)) + adam_epsilon)
    )
    return (moment_new, square_new, weight - step_rate * (normalized + shrink * weight))


def gated(gate, up):
    rate = (2.0 / jnp.pi) ** 0.5
    inner = jnp.tanh(rate * (gate + 0.044715 * gate * gate * gate))
    gelu = 0.5 * gate * (1.0 + inner)
    slope = 0.5 * (1.0 + inner) + 0.5 * gate * (1.0 - inner * inner) * rate * (
        1.0 + 3.0 * 0.044715 * gate * gate
    )
    return gelu * up, slope * up, gelu


def local(
    inputs,
    cotangent,
    routes,
    project_weight,
    project_moment,
    project_square,
    output_weight,
    output_moment,
    output_square,
    router_weight,
    router_moment,
    router_square,
    norm_gains,
    gains_moment,
    gains_square,
    expert_in,
    expert_in_moment,
    expert_in_square,
    expert_down,
    expert_down_moment,
    expert_down_square,
):
    seq_count, stretch, width = inputs.shape
    device_count = lax.axis_size("expert")
    expert_count = device_count
    rows = seq_count * stretch
    me = lax.axis_index("expert")
    others = me ^ jnp.arange(device_count, dtype=jnp.int32)
    shard = project_weight.shape[0]

    expert_weights = lax.all_gather(
        jnp.concatenate([expert_in[0].astype(BF), expert_down[0].astype(BF)], axis=0), "dp"
    )
    own_grad = cotangent.reshape(rows, width)
    grad_blocks = gather_blocks(own_grad)
    first_payload = jnp.concatenate(
        [
            project_weight.astype(BF),
            router_weight.astype(BF),
            norm_gains.T.astype(BF),
            jnp.zeros((shard, EXTRA - expert_count - 2), BF),
        ],
        axis=1,
    )
    first_blocks = gather_blocks(gather_plane(first_payload))
    full_first = whole_rows(first_blocks)
    full_output = whole_rows(
        gather_blocks(
            gather_plane(after(output_weight.astype(BF), first_blocks[2], first_blocks[4]))
        )
    )
    gains = full_first[:, QKV + expert_count : QKV + expert_count + 2].astype(F32).T
    lanes = jnp.arange(EXTRA, dtype=jnp.int32)[None, :]
    router = jnp.where(lanes < expert_count, full_first[:, QKV:], 0).astype(BF)

    tokens = inputs.astype(F32).reshape(rows, width)
    factor_one = rms_factor(tokens)
    normed_one = (tokens * factor_one * gains[0:1]).astype(BF)
    projected = dot(full_first, normed_one, 0, 1)
    positions = me * stretch + jnp.arange(stretch, dtype=jnp.int32)
    frequency = rope_base ** (-jnp.arange(HD // 2, dtype=F32) / (HD // 2))
    angles = frequency[:, None] * positions.astype(F32)[None, :]
    cosine = jnp.tile(jnp.cos(angles), (1, seq_count))
    sine = jnp.tile(jnp.sin(angles), (1, seq_count))
    turned = turn(projected[: QW + KW].reshape(H + KVH, HD, rows), cosine, sine).astype(BF)
    queries = turned[:H]
    route_rows = routes.reshape(rows, TOP).T.astype(BF)
    pair_payload = jnp.concatenate(
        [
            turned[H:].reshape(KW, rows),
            projected[QW + KW : QKV].astype(BF),
            route_rows,
            jnp.zeros((32 - TOP, rows), BF),
        ],
        axis=0,
    )
    pair_blocks = gather_blocks(pair_payload)
    pairs = jnp.stack(pair_blocks)
    key_positions = (others[:, None] * stretch + jnp.arange(stretch)[None, :]).reshape(-1)
    bias = jnp.where(key_positions[:, None] <= positions[None, :], 0.0, masked_score).astype(F32)
    mixed, lse = attention_call(
        forward_kernel,
        [
            jax.ShapeDtypeStruct((H, HD, rows), F32),
            jax.ShapeDtypeStruct((seq_count, H, stretch), F32),
        ],
        ["head", "row"],
        queries,
        pairs,
        bias,
    )
    mixed_rows = mixed.reshape(QW, rows).astype(BF)
    hidden_one = tokens + dot(mixed_rows, full_output, 0, 0)
    factor_two = rms_factor(hidden_one)
    normed_two = (hidden_one * factor_two * gains[1:2]).astype(BF)

    row_blocks = gather_blocks(normed_two)
    all_routes = jnp.concatenate(
        [block[2 * KW : 2 * KW + TOP].T for block in pair_blocks], axis=0
    ).astype(jnp.int32)
    named = jnp.any(all_routes[:, :, None] == lanes[None], axis=1)
    route_bias = jnp.where(named, 0.0, masked_score).astype(F32)
    chunk = 2 * rows
    parts = [
        expert_call(
            me[None],
            row_blocks[2 * c : 2 * c + 2],
            grad_blocks[2 * c : 2 * c + 2],
            route_bias[c * chunk : (c + 1) * chunk],
            expert_weights,
            router,
        )
        for c in range(4)
    ]
    expert_grads = lax.psum_scatter(
        weight_call(row_blocks, grad_blocks, [p[2] for p in parts], [p[3] for p in parts]), "dp"
    ).astype(F32)
    copies = [copy_call(p[2], p[4], expert_weights) for p in parts]
    gates_own = parts[0][5][:rows, :expert_count]
    outputs = hidden_one + reduce_blocks([b for p in parts for b in p[:2]])
    copies = reduce_blocks([b for pair in copies for b in pair])

    grad_rows = own_grad.astype(F32)
    gate_grad = copies[:, width : width + expert_count] + copies[
        :, width + expert_count : width + 2 * expert_count
    ]
    logit_grad = (
        gates_own * (gate_grad - jnp.sum(gates_own * gate_grad, axis=1, keepdims=True))
    ).astype(BF)
    normed_two_grad = copies[:, :width] + dot(logit_grad, router[:, :expert_count], 1, 1)
    router_grad = dot(logit_grad, normed_two, 0, 0)
    part_two, gain_two = rms_back(normed_two_grad, hidden_one, factor_two, gains[1:2])
    hidden_grad_one = grad_rows + part_two
    branch_grad = hidden_grad_one.astype(BF)
    mixed_grad = dot(full_output, branch_grad, 1, 1).astype(BF).reshape(H, HD, rows)
    output_grad = scatter_rows(dot(mixed_rows, branch_grad, 1, 0))

    query_grad, pair_grad = attention_call(
        backward_kernel,
        [
            jax.ShapeDtypeStruct((H, HD, rows), F32),
            jax.ShapeDtypeStruct((device_count, rows, 2 * KW), BF),
        ],
        ["head", pl.BlockSpec((device_count, stretch, 2 * KW), lambda s: (0, s, 0))],
        queries,
        pairs,
        bias,
        mixed,
        lse,
        mixed_grad,
    )
    pair_sum = reduce_blocks([pair_grad[k] for k in range(device_count)]).T
    key_sum = turn(pair_sum[:KW].reshape(KVH, HD, rows), cosine, -sine).reshape(KW, rows)
    query_part = turn(query_grad, cosine, -sine).reshape(QW, rows).astype(BF)
    late_part = jnp.concatenate([key_sum, pair_sum[KW:]], axis=0).astype(BF)
    query_weight_grad = scatter_rows(dot(normed_one, query_part, 0, 1))
    projected_grad = jnp.concatenate(
        [query_part, late_part, jnp.zeros((EXTRA, rows), BF)], axis=0
    )
    normed_one_grad = dot(projected_grad, full_first, 0, 1)
    part_one, gain_one = rms_back(normed_one_grad, tokens, factor_one, gains[0:1])
    input_grad = hidden_grad_one + part_one
    extras = jnp.concatenate(
        [router_grad, gain_one[None], gain_two[None], jnp.zeros((EXTRA - expert_count - 2, D), F32)]
    ).T
    late = scatter_rows(jnp.concatenate([dot(normed_one, late_part, 0, 1), extras], axis=1))
    project_grad = jnp.concatenate([query_weight_grad, late[:, : 2 * KW]], axis=1)
    router_sum = late[:, 2 * KW : 2 * KW + expert_count]
    gains_sum = late[:, 2 * KW + expert_count : 2 * KW + expert_count + 2].T

    sequence = stretch * device_count
    project_new = adam_update(
        project_weight,
        project_moment,
        project_square,
        project_grad,
        3.0 * (2.0 / D) ** 0.5,
        weight_decay,
    )
    output_new = adam_update(
        output_weight,
        output_moment,
        output_square,
        output_grad,
        3.0 * (sequence / (32.0 * H * HD)) ** 0.5,
        weight_decay,
    )
    router_new = adam_update(
        router_weight, router_moment, router_square, router_sum, 1.5 / D**0.5, weight_decay
    )
    gains_new = adam_update(norm_gains, gains_moment, gains_square, gains_sum, 0.8, 0.0)
    in_new = adam_update(
        expert_in,
        expert_in_moment,
        expert_in_square,
        expert_grads[None, : D // 4],
        3.0 / D**0.5,
        weight_decay,
    )
    down_new = adam_update(
        expert_down,
        expert_down_moment,
        expert_down_square,
        expert_grads[None, D // 4 :],
        12.0 / FF**0.5,
        weight_decay,
    )
    return (
        outputs.reshape(inputs.shape),
        input_grad.reshape(inputs.shape),
        *project_new,
        *output_new,
        *router_new,
        *gains_new,
        *in_new,
        *down_new,
    )


def rms_norm(values, gain_row):
    factor = lax.rsqrt(jnp.mean(values * values, axis=-1, keepdims=True) + norm_epsilon)
    return values * factor * gain_row


def rotate(values, positions):
    half_width = values.shape[-1] // 2
    frequency = rope_base ** (-jnp.arange(half_width, dtype=jnp.float32) / half_width)
    angles = positions.astype(jnp.float32)[:, None] * frequency[None, :]
    cosine = jnp.cos(angles)[:, None, :]
    sine_part = jnp.sin(angles)[:, None, :]
    first_half = values[..., :half_width]
    second_half = values[..., half_width:]
    return jnp.concatenate(
        [
            first_half * cosine - second_half * sine_part,
            second_half * cosine + first_half * sine_part,
        ],
        axis=-1,
    )


def gated_unit(gate_up):
    return jax.nn.gelu(gate_up[..., :FF], approximate=True) * gate_up[..., FF:]


def slot_tables(route_block, expert_count, capacity):
    flat_routes = route_block.reshape(-1)
    pick_count = flat_routes.shape[0]
    onehot = (flat_routes[:, None] == jnp.arange(expert_count, dtype=jnp.int32)[None, :]).astype(
        jnp.int32
    )
    earlier = jnp.cumsum(onehot, axis=0) - onehot
    rank_values = jnp.sum(earlier * onehot, axis=1)
    slot_index = flat_routes * capacity + rank_values
    slot_table = (
        jnp.full((expert_count * capacity,), pick_count, jnp.int32)
        .at[slot_index]
        .set(jnp.arange(pick_count, dtype=jnp.int32))
    )
    return (slot_index, slot_table)


def attention_blocks(step_fn, carried, key_values, last_query):
    key_count = key_values.shape[1]
    block_keys = 512

    def one_turn(turn_index, state_now):
        offset = turn_index * block_keys
        key_block = lax.dynamic_slice_in_dim(key_values, offset, block_keys, 1)
        return lax.cond(
            offset > last_query,
            lambda held_state: held_state,
            lambda held_state: step_fn(held_state, key_block, offset),
            state_now,
        )

    return lax.fori_loop(0, key_count // block_keys, one_turn, carried)


def general(
    inputs,
    cotangent,
    routes,
    project_weight,
    project_moment,
    project_square,
    output_weight,
    output_moment,
    output_square,
    router_weight,
    router_moment,
    router_square,
    norm_gains,
    gains_moment,
    gains_square,
    expert_in,
    expert_in_moment,
    expert_in_square,
    expert_down,
    expert_down_moment,
    expert_down_square,
):
    seq_count, stretch_len, model_width = inputs.shape
    expert_devices = lax.axis_size("expert")
    seq_length = stretch_len * expert_devices
    expert_count = EXP_DEV * expert_devices
    row_count = seq_count * stretch_len
    capacity = 2 * row_count * TOP // expert_count
    group_size = H // KVH
    query_width = H * HD
    key_width = KVH * HD
    group_rows = group_size * stretch_len
    score_scale = HD ** (-0.5)
    first_query = lax.axis_index("expert") * stretch_len
    last_query = first_query + stretch_len - 1
    full_project, full_output, full_router, full_gains = (
        lax.all_gather(project_weight.astype(jnp.bfloat16), ("dp", "expert"), axis=0, tiled=True),
        lax.all_gather(output_weight.astype(jnp.bfloat16), ("dp", "expert"), axis=0, tiled=True),
        lax.all_gather(router_weight.astype(jnp.bfloat16), ("dp", "expert"), axis=0, tiled=True),
        lax.all_gather(norm_gains.astype(jnp.bfloat16), ("dp", "expert"), axis=1, tiled=True),
    )
    full_in, full_down = (
        lax.all_gather(expert_in.astype(jnp.bfloat16), "dp", axis=1, tiled=True),
        lax.all_gather(expert_down.astype(jnp.bfloat16), "dp", axis=1, tiled=True),
    )
    gain_values = full_gains.astype(jnp.float32)
    tokens = inputs.astype(jnp.float32).reshape(row_count, model_width)
    normed_one = rms_norm(tokens, gain_values[0]).astype(jnp.bfloat16)
    projected = jnp.dot(normed_one, full_project, preferred_element_type=jnp.float32).reshape(
        seq_count, stretch_len, -1
    )
    positions = first_query + jnp.arange(stretch_len, dtype=jnp.int32)

    def rope_back(gradient):
        unused, pullback = jax.vjp(
            lambda values: rotate(values, positions), jnp.zeros_like(gradient)
        )
        return pullback(gradient)[0]

    queries = rotate(
        projected[..., :query_width].reshape(seq_count, stretch_len, H, HD), positions
    ).astype(jnp.bfloat16)
    rotated_keys = rotate(
        projected[..., query_width : query_width + key_width].reshape(
            seq_count, stretch_len, KVH, HD
        ),
        positions,
    ).astype(jnp.bfloat16)
    values = projected[..., query_width + key_width :].astype(jnp.bfloat16)
    local_pairs = jnp.concatenate(
        [rotated_keys.reshape(seq_count, stretch_len, key_width), values], axis=-1
    )
    all_pairs = lax.all_gather(local_pairs, "expert", axis=1, tiled=True)

    def to_grid(token_rows):
        return (
            token_rows.reshape(seq_count, stretch_len, KVH, group_size, HD)
            .transpose(0, 2, 3, 1, 4)
            .reshape(seq_count, KVH, group_rows, HD)
        )

    def from_grid(grid_rows):
        return (
            grid_rows.reshape(seq_count, KVH, group_size, stretch_len, HD)
            .transpose(0, 3, 1, 2, 4)
            .reshape(row_count, query_width)
        )

    query_grid = to_grid(queries)
    row_positions = first_query + jnp.arange(group_rows, dtype=jnp.int32) % stretch_len

    def scores_for(sequence, key_block, offset):
        key_part = key_block[sequence, :, :key_width].reshape(-1, KVH, HD)
        raw_scores = (
            jnp.einsum(
                "krd,nkd->krn", query_grid[sequence], key_part, preferred_element_type=jnp.float32
            )
            * score_scale
        )
        key_positions = offset + jnp.arange(key_block.shape[1], dtype=jnp.int32)
        allowed = (key_positions[None, :] <= row_positions[:, None])[None]
        return (raw_scores, allowed)

    def stats_step(carried, key_block, offset):
        top_now, total_now = carried
        new_tops = []
        new_totals = []
        for sequence in range(seq_count):
            raw_scores, allowed = scores_for(sequence, key_block, offset)
            masked = jnp.where(allowed, raw_scores, masked_score)
            top_new = jnp.maximum(top_now[sequence], jnp.max(masked, axis=-1))
            weights = jnp.where(allowed, jnp.exp(masked - top_new[..., None]), 0.0)
            new_totals.append(
                total_now[sequence] * jnp.exp(top_now[sequence] - top_new)
                + jnp.sum(weights, axis=-1)
            )
            new_tops.append(top_new)
        return (jnp.stack(new_tops), jnp.stack(new_totals))

    stats_shape = (seq_count, KVH, group_rows)
    top_all, total_all = attention_blocks(
        stats_step,
        (jnp.full(stats_shape, masked_score, jnp.float32), jnp.zeros(stats_shape, jnp.float32)),
        all_pairs,
        last_query,
    )
    log_total = top_all + jnp.log(total_all)

    def softmax_for(sequence, key_block, offset):
        raw_scores, allowed = scores_for(sequence, key_block, offset)
        return jnp.where(
            allowed,
            jnp.exp(jnp.where(allowed, raw_scores, masked_score) - log_total[sequence][..., None]),
            0.0,
        )

    def mix_step(carried, key_block, offset):
        new_rows = []
        for sequence in range(seq_count):
            softmax_rows = softmax_for(sequence, key_block, offset).astype(jnp.bfloat16)
            value_part = key_block[sequence, :, key_width:].reshape(-1, KVH, HD)
            new_rows.append(
                carried[sequence]
                + jnp.einsum(
                    "krn,nkd->krd", softmax_rows, value_part, preferred_element_type=jnp.float32
                )
            )
        return jnp.stack(new_rows)

    mixed_grid = attention_blocks(
        mix_step, jnp.zeros((seq_count, KVH, group_rows, HD), jnp.float32), all_pairs, last_query
    )
    mixed_rows = from_grid(mixed_grid).astype(jnp.bfloat16)
    hidden_one = tokens + jnp.dot(mixed_rows, full_output, preferred_element_type=jnp.float32)
    normed_two = rms_norm(hidden_one, gain_values[1]).astype(jnp.bfloat16)
    logits = jnp.dot(normed_two, full_router, preferred_element_type=jnp.float32)
    route_rows = routes.reshape(row_count, TOP)
    onehot = (
        route_rows[:, :, None] == jnp.arange(expert_count, dtype=jnp.int32)[None, None, :]
    ).astype(jnp.float32)
    gate_weights = jax.nn.softmax(
        jnp.einsum("rte,re->rt", onehot, logits, precision=lax.Precision.HIGHEST), axis=-1
    )
    slot_index, slot_table = slot_tables(route_rows, expert_count, capacity)
    padded = jnp.concatenate([normed_two, jnp.zeros((1, model_width), jnp.bfloat16)], axis=0)
    sent_rows = padded[slot_table // TOP].reshape(expert_count, capacity, model_width)
    arrived_rows = lax.all_to_all(sent_rows, "expert", split_axis=0, concat_axis=0, tiled=True)
    batched = arrived_rows.reshape(expert_devices, EXP_DEV, -1, model_width)
    gate_up = jnp.einsum("neid,edf->neif", batched, full_in, preferred_element_type=jnp.float32)
    hidden = gated_unit(gate_up).astype(jnp.bfloat16)
    result = jnp.einsum(
        "neif,efd->neid", hidden, full_down, preferred_element_type=jnp.float32
    ).astype(jnp.bfloat16)
    results = result.reshape(arrived_rows.shape)
    kept_gate_up = gate_up.reshape(arrived_rows.shape[0], arrived_rows.shape[1], 2 * FF)
    returned = lax.all_to_all(results, "expert", split_axis=0, concat_axis=0, tiled=True)
    picked = returned.reshape(expert_count * capacity, model_width)[slot_index].reshape(
        row_count, TOP, model_width
    )
    picked_wide = picked.astype(jnp.float32)
    mixture = jnp.sum(gate_weights[:, :, None] * picked_wide, axis=1)
    outputs = hidden_one + mixture
    grad_rows = cotangent.astype(jnp.float32).reshape(row_count, model_width)
    gate_grad = jnp.sum(grad_rows[:, None, :] * picked_wide, axis=-1)
    chosen_grad = gate_weights * (
        gate_grad - jnp.sum(gate_weights * gate_grad, axis=-1, keepdims=True)
    )
    logit_grad = jnp.einsum(
        "rte,rt->re", onehot, chosen_grad, precision=lax.Precision.HIGHEST
    ).astype(jnp.bfloat16)
    copy_out_grad = (
        (gate_weights[:, :, None] * grad_rows[:, None, :])
        .astype(jnp.bfloat16)
        .reshape(row_count * TOP, model_width)
    )
    grad_sent = jnp.concatenate([copy_out_grad, jnp.zeros((1, model_width), jnp.bfloat16)], axis=0)[
        slot_table
    ].reshape(expert_count, capacity, model_width)
    grad_arrived = lax.all_to_all(grad_sent, "expert", split_axis=0, concat_axis=0, tiled=True)
    batched_grad = grad_arrived.reshape(expert_devices, EXP_DEV, -1, model_width)
    batched_in = arrived_rows.reshape(expert_devices, EXP_DEV, -1, model_width)
    gate_up = kept_gate_up.reshape(expert_devices, EXP_DEV, -1, 2 * FF)
    hidden, unit_pull = jax.vjp(gated_unit, gate_up)
    grad_down = jnp.einsum(
        "neif,neid->efd",
        hidden.astype(jnp.bfloat16),
        batched_grad,
        preferred_element_type=jnp.float32,
    )
    hidden_grad = jnp.einsum(
        "neid,efd->neif", batched_grad, full_down, preferred_element_type=jnp.float32
    )
    gate_up_grad = unit_pull(hidden_grad)[0].astype(jnp.bfloat16)
    grad_in = jnp.einsum(
        "neid,neif->edf", batched_in, gate_up_grad, preferred_element_type=jnp.float32
    )
    copy_in_grad = (
        jnp.einsum("neif,edf->neid", gate_up_grad, full_in, preferred_element_type=jnp.float32)
        .astype(jnp.bfloat16)
        .reshape(arrived_rows.shape)
    )
    expert_in_grad, expert_down_grad = (
        lax.psum_scatter(
            grad_in.astype(jnp.bfloat16), "dp", scatter_dimension=1, tiled=True
        ).astype(jnp.float32),
        lax.psum_scatter(
            grad_down.astype(jnp.bfloat16), "dp", scatter_dimension=1, tiled=True
        ).astype(jnp.float32),
    )
    returned_grad = lax.all_to_all(copy_in_grad, "expert", split_axis=0, concat_axis=0, tiled=True)
    copies_grad = returned_grad.reshape(expert_count * capacity, model_width)[slot_index].reshape(
        row_count, TOP, model_width
    )
    normed_two_grad = jnp.sum(copies_grad.astype(jnp.float32), axis=1) + jnp.dot(
        logit_grad, full_router.T, preferred_element_type=jnp.float32
    )
    router_grad_full = jnp.einsum(
        "rd,re->de", normed_two, logit_grad, preferred_element_type=jnp.float32
    )
    unused_two, norm_two_pull = jax.vjp(rms_norm, hidden_one, gain_values[1])
    hidden_part, gain_two_grad = norm_two_pull(normed_two_grad)
    hidden_grad_one = grad_rows + hidden_part
    branch_grad = hidden_grad_one.astype(jnp.bfloat16)
    output_grad_full = jnp.einsum(
        "rh,rd->hd", mixed_rows, branch_grad, preferred_element_type=jnp.float32
    )
    mixed_grad = jnp.dot(branch_grad, full_output.T, preferred_element_type=jnp.float32).astype(
        jnp.bfloat16
    )
    mixed_grad_grid = to_grid(mixed_grad.reshape(seq_count, stretch_len, H, HD))
    row_delta = jnp.sum(mixed_grad_grid.astype(jnp.float32) * mixed_grid, axis=-1)

    def back_step(carried, key_block, offset):
        query_grad, pair_grad = carried
        new_query = []
        block_len = key_block.shape[1]
        for sequence in range(seq_count):
            softmax_rows = softmax_for(sequence, key_block, offset)
            key_part = key_block[sequence, :, :key_width].reshape(-1, KVH, HD)
            value_part = key_block[sequence, :, key_width:].reshape(-1, KVH, HD)
            softmax_grad = jnp.einsum(
                "krd,nkd->krn",
                mixed_grad_grid[sequence],
                value_part,
                preferred_element_type=jnp.float32,
            )
            score_grad = (softmax_rows * (softmax_grad - row_delta[sequence][..., None])).astype(
                jnp.bfloat16
            )
            new_query.append(
                query_grad[sequence]
                + jnp.einsum(
                    "krn,nkd->krd", score_grad, key_part, preferred_element_type=jnp.float32
                )
                * score_scale
            )
            key_grad = (
                jnp.einsum(
                    "krn,krd->nkd",
                    score_grad,
                    query_grid[sequence],
                    preferred_element_type=jnp.float32,
                )
                * score_scale
            )
            value_grad = jnp.einsum(
                "krn,krd->nkd",
                softmax_rows.astype(jnp.bfloat16),
                mixed_grad_grid[sequence],
                preferred_element_type=jnp.float32,
            )
            block_grad = jnp.concatenate(
                [key_grad.reshape(block_len, key_width), value_grad.reshape(block_len, key_width)],
                axis=-1,
            )
            current = lax.dynamic_slice(
                pair_grad,
                (jnp.int32(sequence), offset, jnp.int32(0)),
                (1, block_len, 2 * key_width),
            )
            pair_grad = lax.dynamic_update_slice(
                pair_grad, current + block_grad[None], (jnp.int32(sequence), offset, jnp.int32(0))
            )
        return (jnp.stack(new_query), pair_grad)

    query_start = jnp.zeros((seq_count, KVH, group_rows, HD), jnp.float32)
    pair_start = jnp.zeros((seq_count, seq_length, 2 * key_width), jnp.float32)
    query_grad_grid, pair_grad_all = attention_blocks(
        back_step, (query_start, pair_start), all_pairs, last_query
    )
    pair_grad_local = lax.psum_scatter(
        pair_grad_all.astype(jnp.bfloat16), "expert", scatter_dimension=1, tiled=True
    ).astype(jnp.float32)
    query_grad_rows = rope_back(from_grid(query_grad_grid).reshape(seq_count, stretch_len, H, HD))
    key_grad_rows = rope_back(
        pair_grad_local[..., :key_width].reshape(seq_count, stretch_len, KVH, HD)
    )
    projected_grad = jnp.concatenate(
        [
            query_grad_rows.reshape(row_count, query_width),
            key_grad_rows.reshape(row_count, key_width),
            pair_grad_local[..., key_width:].reshape(row_count, key_width),
        ],
        axis=-1,
    ).astype(jnp.bfloat16)
    project_grad_full = jnp.einsum(
        "rd,rf->df", normed_one, projected_grad, preferred_element_type=jnp.float32
    )
    normed_one_grad = jnp.dot(projected_grad, full_project.T, preferred_element_type=jnp.float32)
    unused_one, norm_one_pull = jax.vjp(rms_norm, tokens, gain_values[0])
    token_part, gain_one_grad = norm_one_pull(normed_one_grad)
    input_grad = hidden_grad_one + token_part
    gains_grad_full = jnp.stack([gain_one_grad, gain_two_grad])
    project_grad, output_grad, router_grad, gains_grad = (
        lax.psum_scatter(project_grad_full, ("dp", "expert"), scatter_dimension=0, tiled=True),
        lax.psum_scatter(output_grad_full, ("dp", "expert"), scatter_dimension=0, tiled=True),
        lax.psum_scatter(router_grad_full, ("dp", "expert"), scatter_dimension=0, tiled=True),
        lax.psum_scatter(gains_grad_full, ("dp", "expert"), scatter_dimension=1, tiled=True),
    )
    rate_project = 3.0 * (2.0 / D) ** 0.5
    rate_output = 3.0 * (seq_length / (32.0 * H * HD)) ** 0.5
    rate_router = 1.5 / D**0.5
    rate_gains = 0.8
    rate_in = 3.0 / D**0.5
    rate_down = 12.0 / FF**0.5
    project_new = adam_update(
        project_weight, project_moment, project_square, project_grad, rate_project, weight_decay
    )
    output_new = adam_update(
        output_weight, output_moment, output_square, output_grad, rate_output, weight_decay
    )
    router_new = adam_update(
        router_weight, router_moment, router_square, router_grad, rate_router, weight_decay
    )
    gains_new = adam_update(norm_gains, gains_moment, gains_square, gains_grad, rate_gains, 0.0)
    in_new = adam_update(
        expert_in, expert_in_moment, expert_in_square, expert_in_grad, rate_in, weight_decay
    )
    down_new = adam_update(
        expert_down,
        expert_down_moment,
        expert_down_square,
        expert_down_grad,
        rate_down,
        weight_decay,
    )
    return (
        outputs.reshape(seq_count, stretch_len, model_width),
        input_grad.reshape(seq_count, stretch_len, model_width),
        project_new[0],
        project_new[1],
        project_new[2],
        output_new[0],
        output_new[1],
        output_new[2],
        router_new[0],
        router_new[1],
        router_new[2],
        gains_new[0],
        gains_new[1],
        gains_new[2],
        in_new[0],
        in_new[1],
        in_new[2],
        down_new[0],
        down_new[1],
        down_new[2],
    )


def solution(mesh):
    token_spec = P("dp", "expert", None)
    row_spec = P(("dp", "expert"), None)
    gain_spec = P(None, ("dp", "expert"))
    expert_spec = P("expert", "dp", None)
    states = (row_spec,) * 9 + (gain_spec,) * 3 + (expert_spec,) * 6
    small = mesh.shape["dp"] == 4 and mesh.shape["expert"] == 8
    return jax.shard_map(
        local if small else general,
        mesh=mesh,
        in_specs=(token_spec, token_spec, P(("dp", "expert"), None, None)) + states,
        out_specs=(token_spec, token_spec) + states,
        check_vma=False,
    )
```

```python
import jax
import jax.numpy as jnp
from jax import lax
from jax.experimental import pallas as pl
from jax.experimental.pallas import tpu as pltpu
from jax.sharding import PartitionSpec as P

D = 1536
H = 12
KVH = 2
HD = 128
FF = 768
TOP = 4
STEP = 10
GROUP = H // KVH
QW = H * HD
KW = KVH * HD
QKV = QW + 2 * KW
EXP_DEV = 1
EXTRA = 128

norm_epsilon = 1e-06
adam_epsilon = 1e-08
beta_first = 0.9
beta_second = 0.95
weight_decay = 0.1
rope_base = 1000000.0
masked_score = -1e30
score_scale = HD ** (-0.5)
BF = jnp.bfloat16
F32 = jnp.float32
VMEM_BYTES = 50 * 1024 * 1024
HINT = pl.CostEstimate(flops=0, bytes_accessed=0, transcendentals=0)


def dot(a, b, da, db):
    return lax.dot_general(a, b, (((da,), (db,)), ((), ())), preferred_element_type=F32)


def after(value, *others):
    return lax.optimization_barrier((value, *others))[0]


def bring(pairs, sems):
    copies = [pltpu.make_async_copy(a, b, sems.at[n]) for n, (a, b) in enumerate(pairs)]
    for copy in copies:
        copy.start()
    return copies


def glue_call(kernel, out_shape, *operands, scalars=1, **options):
    vmem = pl.BlockSpec(memory_space=pltpu.VMEM)
    options.setdefault(
        "in_specs",
        [pl.BlockSpec(memory_space=pltpu.SMEM)] * scalars + [vmem] * (len(operands) - scalars),
    )
    options.setdefault("out_specs", [vmem] * len(out_shape))
    return pl.pallas_call(
        kernel,
        out_shape=out_shape,
        compiler_params=pltpu.CompilerParams(vmem_limit_bytes=VMEM_BYTES),
        cost_estimate=HINT,
        **options,
    )(*operands)


def plane_kernel(place_ref, *refs):
    blocks, out_ref, sems = refs[:4], refs[4], refs[5]
    moves = [
        (block, out_ref.at[lax.rem(place_ref[0] + step, 4)]) for step, block in enumerate(blocks)
    ]
    for copy in bring(moves, sems):
        copy.wait()


def plane_end(blocks):
    anywhere = pl.BlockSpec(memory_space=pl.ANY)
    return glue_call(
        plane_kernel,
        [jax.ShapeDtypeStruct((4,) + blocks[0].shape, BF)],
        lax.axis_index("dp")[None],
        *blocks,
        in_specs=[pl.BlockSpec(memory_space=pltpu.SMEM)] + [anywhere] * 4,
        out_specs=[anywhere],
        scratch_shapes=[pltpu.SemaphoreType.DMA((4,))],
    )[0]


def halves_kernel(by_x_ref, by_y_ref, low_ref, high_ref, sems):
    half = low_ref.shape[0]
    moves = [(by_x_ref.at[pl.ds(0, half)], low_ref), (by_y_ref.at[pl.ds(half, half)], high_ref)]
    for copy in bring(moves, sems):
        copy.wait()


def halves_call(near):
    anywhere = pl.BlockSpec(memory_space=pl.ANY)
    half = jax.ShapeDtypeStruct((near[0].shape[0] // 2, *near[0].shape[1:]), BF)
    return glue_call(
        halves_kernel,
        [half, half],
        *near,
        in_specs=[anywhere] * 2,
        out_specs=[anywhere] * 2,
        scratch_shapes=[pltpu.SemaphoreType.DMA((2,))],
    )


def hop(value, mask):
    return lax.ppermute(value, "expert", [(i, i ^ mask) for i in range(8)])


def total(one, two):
    return (one.astype(F32) + two.astype(F32)).astype(one.dtype)


def gather_near(value):
    return hop(value, 2), hop(value, 4)


def gather_over(near):
    low, high = halves_call(near)
    return hop(low, 4), hop(high, 2)


def gather_cores(near):
    return hop(near[0], 1), hop(near[1], 1)


def gathered(value, sibling, near, cores, diagonal, diagonal_core):
    return [value, sibling, near[0], cores[0], near[1], cores[1], diagonal, diagonal_core]


def core_sums(blocks, arrived):
    return [total(blocks[n], arrived[n]) for n in range(4)]


def reduce_over(diagonal):
    half = diagonal.shape[0] // 2
    return hop(diagonal[:half], 2), hop(diagonal[half:], 4)


def reduce_last(by_x, by_y, over):
    half = by_x.shape[0] // 2
    start = (0,) * by_x.ndim
    by_y = lax.dynamic_update_slice(by_y, total(by_y[:half], over[0]), start)
    by_x = lax.dynamic_update_slice(by_x, total(by_x[half:], over[1]), (half,) + start[1:])
    return by_x, by_y


def last_hops(by_x, by_y):
    return hop(by_x, 2), hop(by_y, 4)


def reduced(own, last):
    return own.astype(F32) + last[0].astype(F32) + last[1].astype(F32)


def phase(*values):
    return lax.optimization_barrier(values)


def plane_hop(shard, step):
    return lax.ppermute(shard, "dp", [((i + step) % 4, i) for i in range(4)])


def key_block(kv_ref, row):
    return jnp.concatenate(
        [kv_ref[n, row : row + HD, :].astype(F32).T for n in range(kv_ref.shape[0])], axis=0
    ).astype(BF)


def two(ref, h):
    return jnp.concatenate([ref[h], ref[h + 1]], axis=1)


def forward_kernel(q_ref, kv_ref, bias_ref, mixed_ref, lse_ref):
    stretch = bias_ref.shape[1]
    bias = jnp.concatenate([bias_ref[...]] * 2, axis=1)
    for g in range(KVH):
        keys = key_block(kv_ref, g * HD)
        values = jnp.concatenate(
            [kv_ref[n, KW + g * HD : KW + (g + 1) * HD, :] for n in range(kv_ref.shape[0])], axis=1
        )
        for h in range(g * GROUP, (g + 1) * GROUP, 2):
            scores = dot(keys, two(q_ref, h), 1, 0) * score_scale + bias
            top = jnp.max(scores, axis=0, keepdims=True)
            weights = jnp.exp(scores - top)
            amount = jnp.sum(weights, axis=0, keepdims=True)
            mixed = dot(values, weights.astype(BF), 1, 0) / amount
            lse = top + jnp.log(amount)
            for n in range(2):
                part = slice(n * stretch, (n + 1) * stretch)
                mixed_ref[h + n] = mixed[:, part]
                lse_ref[0, h + n : h + n + 1, :] = lse[:, part]


def backward_kernel(q_ref, kv_ref, bias_ref, mixed_ref, lse_ref, grad_ref, dq_ref, same_ref, other_ref):
    blocks, stretch = kv_ref.shape[0], kv_ref.shape[2]
    bias = jnp.concatenate([bias_ref[...]] * 2, axis=1)
    for g in range(KVH):
        keys, values = key_block(kv_ref, g * HD), key_block(kv_ref, KW + g * HD)
        keys_flat = jnp.concatenate(
            [kv_ref[n, g * HD : (g + 1) * HD, :] for n in range(blocks)], axis=1
        )
        key_grad = jnp.zeros(keys.shape, F32)
        value_grad = jnp.zeros(keys.shape, F32)
        for h in range(g * GROUP, (g + 1) * GROUP, 2):
            query, grad = two(q_ref, h), two(grad_ref, h)
            lse = jnp.concatenate([lse_ref[0, h : h + 1, :], lse_ref[0, h + 1 : h + 2, :]], axis=1)
            scores = dot(keys, query, 1, 0) * score_scale + bias
            probs = jnp.exp(scores - lse)
            delta = jnp.sum(two(mixed_ref, h) * grad.astype(F32), axis=0, keepdims=True)
            score_grad = (probs * (dot(values, grad, 1, 0) - delta)).astype(BF)
            query_grad = dot(keys_flat, score_grad, 1, 0) * score_scale
            for n in range(2):
                dq_ref[h + n] = query_grad[:, n * stretch : (n + 1) * stretch]
            key_grad += dot(score_grad, query, 1, 1)
            value_grad += dot(probs.astype(BF), grad, 1, 1)
        key_grad = (key_grad * score_scale).astype(BF)
        value_grad = value_grad.astype(BF)
        for n in range(blocks):
            part, ref = slice(n * stretch, (n + 1) * stretch), (same_ref, other_ref)[n % 2]
            ref[n // 2, :, g * HD : (g + 1) * HD] = key_grad[part]
            ref[n // 2, :, KW + g * HD : KW + (g + 1) * HD] = value_grad[part]


def attention_call(kernel, outs, out_specs, queries, pairs, bias, *more):
    blocks, _, tokens = pairs.shape
    stretch = bias.shape[1]
    head = pl.BlockSpec((H, HD, stretch), lambda s: (0, 0, s))
    row = pl.BlockSpec((1, H, stretch), lambda s: (s, 0, 0))
    specs = [
        head,
        pl.BlockSpec((blocks, 2 * KW, stretch), lambda s: (0, 0, s)),
        pl.BlockSpec(bias.shape, lambda s: (0, 0)),
        head,
        row,
        head,
    ]
    keys = blocks * stretch
    return pl.pallas_call(
        kernel,
        grid=(tokens // stretch,),
        in_specs=specs[: 3 + len(more)],
        out_specs=[head if s == "head" else row if s == "row" else s for s in out_specs],
        out_shape=outs,
        compiler_params=pltpu.CompilerParams(vmem_limit_bytes=56 * 1024 * 1024),
        cost_estimate=HINT,
    )(queries, pairs, bias, *more)


HALF = FF // 2
ROWS = D // 4
DOWN = FF // 4


def joined(refs):
    return jnp.concatenate([ref[...] for ref in refs], axis=0)


def inner(weight_ref):
    return jnp.concatenate([weight_ref[a, :ROWS] for a in range(4)], axis=0)


def outer(first_ref, half=None):
    owners = range(4) if half is None else (2 * half, 2 * half + 1)
    return jnp.concatenate(
        [
            jnp.concatenate(
                [first_ref[a, ROWS : ROWS + DOWN], first_ref[a, ROWS + DOWN :]], axis=1
            )
            for a in owners
        ],
        axis=0,
    )


def gates_for(me_ref, gates):
    lanes = lax.broadcasted_iota(jnp.int32, gates.shape, 1)
    return jnp.sum(jnp.where(lanes == me_ref[0], gates, 0.0), axis=1, keepdims=True)


def first_kernel(me_ref, *refs):
    rows_in, grads_in = refs[:8], refs[8:16]
    bias_ref, first_ref, router_ref = refs[16:19]
    gates_out, gate_grad_out, gate_up_out, hidden_out, weight_out = refs[19:24]
    rows_v, grads_v, gate_up_v, hidden_v, weight_v, in_sems, out_sems = refs[24:]
    count = rows_in[0].shape[0]
    moves = []
    for k in range(8):
        t, part = k // 2, pl.ds((k % 2) * count, count)
        moves += [(rows_in[k], rows_v.at[t, part]), (grads_in[k], grads_v.at[t, part])]
    arriving = bring(moves, in_sems)
    weight, back = inner(first_ref), outer(first_ref, 0)
    leaving = []
    for t in range(4):
        part = slice(t * 2 * count, (t + 1) * 2 * count)
        for copy in arriving[4 * t : 4 * t + 4]:
            copy.wait()
        rows, grads = rows_v[t], grads_v[t]
        logits = dot(rows, router_ref[...], 1, 0) + bias_ref[part]
        exps = jnp.exp(logits - jnp.max(logits, axis=1, keepdims=True))
        gates = exps / jnp.sum(exps, axis=1, keepdims=True)
        gates_out[part] = gates
        mine = gates_for(me_ref, gates)
        gate_up = dot(rows, weight, 1, 0)
        hidden, slope_gate, slope_up = gated(gate_up[:, :HALF], gate_up[:, HALF:])
        hidden_grad = dot(grads, back, 1, 1)
        hidden = hidden.astype(BF).astype(F32)
        gate_grad = jnp.sum(hidden * hidden_grad, axis=1, keepdims=True)
        gate_grad_out[part] = jnp.broadcast_to(gate_grad, (2 * count, EXTRA))
        hidden_grad = hidden_grad * mine
        gate_up_v[t, :, :HALF] = (hidden_grad * slope_gate).astype(BF)
        gate_up_v[t, :, HALF:] = (hidden_grad * slope_up).astype(BF)
        hidden_v[t] = (mine * hidden).astype(BF)
        pairs = [(gate_up_v.at[t], gate_up_out.at[t]), (hidden_v.at[t], hidden_out.at[t])]
        leaving += bring(pairs, out_sems.at[pl.ds(2 * t, 2)])
    gate_up = gate_up_v[...].reshape(8 * count, 2 * HALF)
    for a in range(4):
        rows = rows_v[:, :, a * ROWS : (a + 1) * ROWS].reshape(8 * count, ROWS)
        weight_v[a] = dot(rows, gate_up, 0, 0).astype(BF)
        leaving += bring([(weight_v.at[a], weight_out.at[a])], out_sems.at[pl.ds(8 + a, 1)])
    for copy in leaving:
        copy.wait()


def first_call(me, rows, grads, bias, first, router):
    count, width = rows[0].shape
    shape = jax.ShapeDtypeStruct
    vmem, anywhere = pl.BlockSpec(memory_space=pltpu.VMEM), pl.BlockSpec(memory_space=pl.ANY)
    return pl.pallas_call(
        first_kernel,
        in_specs=[pl.BlockSpec(memory_space=pltpu.SMEM)] + [anywhere] * 16 + [vmem] * 3,
        out_specs=[vmem] * 2 + [anywhere] * 3,
        out_shape=[shape((8 * count, EXTRA), F32)] * 2
        + [
            shape((4, 2 * count, 2 * HALF), BF),
            shape((4, 2 * count, HALF), BF),
            shape((4, ROWS, 2 * HALF), BF),
        ],
        scratch_shapes=[
            pltpu.VMEM((4, 2 * count, width), BF),
            pltpu.VMEM((4, 2 * count, width), BF),
            pltpu.VMEM((4, 2 * count, 2 * HALF), BF),
            pltpu.VMEM((4, 2 * count, HALF), BF),
            pltpu.VMEM((4, ROWS, 2 * HALF), BF),
            pltpu.SemaphoreType.DMA((16,)),
            pltpu.SemaphoreType.DMA((12,)),
        ],
        compiler_params=pltpu.CompilerParams(vmem_limit_bytes=VMEM_BYTES),
        cost_estimate=HINT,
    )(me, *rows, *grads, bias, first, router)


def second_kernel(t, me_ref, *refs):
    row0, row1, grad0, grad1, gates_in, gate_grad_in, up_in, hidden_in, first, second = refs[:10]
    out0, out1, result0, result1, up_out, hidden_out = refs[10:16]
    rows_v, grads_v, gates_v, gate_grad_v, up_v, hidden_v, inner0_v, inner1_v, outer_v, sems = refs[16:]
    count = row0.shape[0]
    low, high, part = pl.ds(0, count), pl.ds(count, count), pl.ds(t * 2 * count, 2 * count)
    moves = [
        (row0, rows_v.at[low]),
        (row1, rows_v.at[high]),
        (second, inner1_v),
        (grad0, grads_v.at[low]),
        (grad1, grads_v.at[high]),
        (first.at[:, pl.ds(ROWS, 2 * DOWN)], outer_v),
        (gates_in.at[part], gates_v),
        (gate_grad_in.at[part], gate_grad_v),
        (up_in.at[t], up_v),
        (first.at[:, pl.ds(0, ROWS)], inner0_v),
        (hidden_in.at[t], hidden_v),
    ]
    arriving = bring(moves, sems)
    for copy in arriving[:3]:
        copy.wait()
    inner1 = inner1_v[...].reshape(D, 2 * HALF)
    gate_up = dot(rows_v[...], inner1, 1, 0)
    for copy in arriving[3:6]:
        copy.wait()
    outer0, outer1 = [
        jnp.concatenate(
            [jnp.concatenate([outer_v[a, :DOWN], outer_v[a, DOWN:]], axis=1) for a in owners], axis=0
        )
        for owners in ((0, 1), (2, 3))
    ]
    hidden_grad = dot(grads_v[...], outer1, 1, 1)
    for copy in arriving[6:]:
        copy.wait()
    copies = dot(up_v[...], inner0_v[...].reshape(D, 2 * HALF), 1, 1)
    result = dot(hidden_v[...], outer0, 1, 0)
    hidden, slope_gate, slope_up = gated(gate_up[:, :HALF], gate_up[:, HALF:])
    mine = gates_for(me_ref, gates_v[...])
    hidden = hidden.astype(BF).astype(F32)
    gate_grad = gate_grad_v[...] + jnp.sum(hidden * hidden_grad, axis=1, keepdims=True)
    hidden_grad = hidden_grad * mine
    up_out[:, :HALF] = (hidden_grad * slope_gate).astype(BF)
    up_out[:, HALF:] = (hidden_grad * slope_up).astype(BF)
    hidden_out[...] = (mine * hidden).astype(BF)
    copies = (copies + dot(up_out[...], inner1, 1, 1)).astype(BF)
    result = (result + dot(hidden_out[...], outer1, 1, 0)).astype(BF)
    result0[...] = result[:count]
    result1[...] = result[count:]
    lanes = lax.broadcasted_iota(jnp.int32, (2 * count, EXTRA), 1)
    rounded = gate_grad.astype(BF).astype(F32)
    columns = (
        jnp.where(lanes == me_ref[0], rounded, 0.0)
        + jnp.where(lanes == me_ref[0] + 8, gate_grad - rounded, 0.0)
    ).astype(BF)
    for n, ref in enumerate((out0, out1)):
        ref[:, :D] = copies[n * count : (n + 1) * count]
        ref[:, D:] = columns[n * count : (n + 1) * count]


def second_call(t, me, rows, grads, gates, gate_grad, up_first, hidden_first, first, second):
    count, width = rows[0].shape
    shape = jax.ShapeDtypeStruct
    vmem, anywhere = pl.BlockSpec(memory_space=pltpu.VMEM), pl.BlockSpec(memory_space=pl.ANY)
    return pl.pallas_call(
        lambda *refs: second_kernel(t, *refs),
        in_specs=[pl.BlockSpec(memory_space=pltpu.SMEM)] + [anywhere] * 10,
        out_specs=[vmem] * 6,
        out_shape=[shape((count, D + EXTRA), BF)] * 2
        + [shape((count, D), BF)] * 2
        + [shape((2 * count, 2 * HALF), BF), shape((2 * count, HALF), BF)],
        scratch_shapes=[
            pltpu.VMEM((2 * count, width), BF),
            pltpu.VMEM((2 * count, width), BF),
            pltpu.VMEM((2 * count, EXTRA), F32),
            pltpu.VMEM((2 * count, EXTRA), F32),
            pltpu.VMEM((2 * count, 2 * HALF), BF),
            pltpu.VMEM((2 * count, HALF), BF),
            pltpu.VMEM((4, ROWS, 2 * HALF), BF),
            pltpu.VMEM((4, ROWS, 2 * HALF), BF),
            pltpu.VMEM((4, 2 * DOWN, 2 * HALF), BF),
            pltpu.SemaphoreType.DMA((11,)),
        ],
        compiler_params=pltpu.CompilerParams(vmem_limit_bytes=VMEM_BYTES),
        cost_estimate=HINT,
    )(
        me,
        *rows[2 * t : 2 * t + 2],
        *grads[2 * t : 2 * t + 2],
        gates,
        gate_grad,
        up_first,
        hidden_first,
        first,
        second,
    )


def last_kernel(*refs):
    rows_in, grads_in, ups, hiddens = refs[:8], refs[8:16], refs[16:20], refs[20:24]
    hidden0_ref, out_ref, rows_v, grads_v, out_v, in_sems, out_sems = refs[24:]
    count = rows_in[0].shape[0]
    arriving = bring(
        [(ref, grads_v.at[pl.ds(k * count, count)]) for k, ref in enumerate(grads_in)]
        + [(ref, rows_v.at[pl.ds(k * count, count)]) for k, ref in enumerate(rows_in)],
        in_sems,
    )
    for copy in arriving[:8]:
        copy.wait()
    grads = grads_v[...]
    for half, hidden in enumerate((hidden0_ref[...].reshape(8 * count, HALF), joined(hiddens))):
        sums = dot(hidden, grads, 0, 0).astype(BF)
        for n in range(2):
            for side in range(2):
                out_v[2 * half + n, ROWS + side * DOWN : ROWS + (side + 1) * DOWN] = sums[
                    n * DOWN : (n + 1) * DOWN, side * 2 * HALF : (side + 1) * 2 * HALF
                ]
    for copy in arriving[8:]:
        copy.wait()
    leaving = []
    gate_up = joined(ups)
    for a in range(4):
        out_v[a, :ROWS] = dot(rows_v[:, a * ROWS : (a + 1) * ROWS], gate_up, 0, 0).astype(BF)
        leaving += bring([(out_v.at[a], out_ref.at[a])], out_sems.at[pl.ds(a, 1)])
    for copy in leaving:
        copy.wait()


def last_call(rows, grads, ups, hiddens, hidden0):
    count, width = rows[0].shape
    vmem, anywhere = pl.BlockSpec(memory_space=pltpu.VMEM), pl.BlockSpec(memory_space=pl.ANY)
    whole = (4, ROWS + 2 * DOWN, 2 * HALF)
    return pl.pallas_call(
        last_kernel,
        in_specs=[anywhere] * 16 + [vmem] * 9,
        out_specs=anywhere,
        out_shape=jax.ShapeDtypeStruct(whole, BF),
        scratch_shapes=[
            pltpu.VMEM((8 * count, width), BF),
            pltpu.VMEM((8 * count, width), BF),
            pltpu.VMEM(whole, BF),
            pltpu.SemaphoreType.DMA((16,)),
            pltpu.SemaphoreType.DMA((4,)),
        ],
        compiler_params=pltpu.CompilerParams(vmem_limit_bytes=VMEM_BYTES),
        cost_estimate=HINT,
    )(*rows, *grads, *ups, *hiddens, hidden0)


def rms_factor(values):
    return lax.rsqrt(jnp.mean(values * values, axis=-1, keepdims=True) + norm_epsilon)


def rms_back(gradient, values, factor, gain):
    scaled = gradient * gain
    inner = jnp.mean(scaled * values, axis=-1, keepdims=True)
    return (
        factor * scaled - values * (factor * factor * factor * inner),
        jnp.sum(gradient * values * factor, axis=0),
    )


def turn(heads, cosine, sine):
    half = HD // 2
    first, second = heads[:, :half], heads[:, half:]
    return jnp.concatenate(
        [first * cosine - second * sine, second * cosine + first * sine], axis=1
    )


def adam_update(weight, moment, square, gradient, step_rate, shrink):
    moment_new = beta_first * moment + (1.0 - beta_first) * gradient
    square_new = beta_second * square + (1.0 - beta_second) * gradient * gradient
    normalized = (
        moment_new
        / (1.0 - beta_first**STEP)
        / (jnp.sqrt(square_new / (1.0 - beta_second**STEP)) + adam_epsilon)
    )
    return (moment_new, square_new, weight - step_rate * (normalized + shrink * weight))


def assemble(me_ref, refs, weight_v, whole_ref, sems, out_sem):
    rows = refs[0].shape[1]
    moves = []
    for k in range(8):
        for a in range(4):
            if k < 6:
                source = refs[k].at[a]
            else:
                source = refs[2 * k - 6 + a // 2].at[a % 2]
            start = pl.multiple_of((a * 8 + (me_ref[0] ^ k)) * rows, 16)
            moves.append((source, weight_v.at[pl.ds(start, rows)]))
    for copy in bring(moves, sems):
        copy.wait()
    return bring([(weight_v, whole_ref)], out_sem)[0]


def project_kernel(me_ref, *refs):
    blocks, (inputs_ref, cosine_ref, sine_ref, routes_ref) = refs[:10], refs[10:14]
    query_ref, pair_ref, normed_ref, factor_ref, gains_ref, router_ref, whole_ref = refs[14:21]
    weight_v, sems, out_sem = refs[21:]
    leaving = assemble(me_ref, blocks, weight_v, whole_ref, sems, out_sem)
    extras = weight_v[:, QKV:]
    lanes = lax.broadcasted_iota(jnp.int32, extras.shape, 1)
    router_ref[...] = jnp.where(lanes < 8, extras.astype(F32), 0.0).astype(BF)
    gains = extras.astype(F32).T[8:16]
    gains_ref[...] = gains
    tokens = inputs_ref[...].astype(F32)
    factor = rms_factor(tokens)
    factor_ref[...] = factor
    normed = (tokens * factor * gains[:1]).astype(BF)
    normed_ref[...] = normed
    projected = dot(normed, weight_v[:, :QKV], 1, 0)
    half = HD // 2
    cosine, sine = cosine_ref[...], sine_ref[...]
    for h in range(H + KVH):
        head = projected[:, h * HD : (h + 1) * HD].T
        first, second = head[:half], head[half:]
        head = jnp.concatenate(
            [first * cosine - second * sine, second * cosine + first * sine], axis=0
        ).astype(BF)
        if h < H:
            query_ref[h] = head
        else:
            pair_ref[(h - H) * HD : (h - H + 1) * HD] = head
    for h in range(KVH):
        start = QW + KW + h * HD
        pair_ref[KW + h * HD : KW + (h + 1) * HD] = projected[:, start : start + HD].T.astype(BF)
    pair_ref[2 * KW :] = routes_ref[...]
    leaving.wait()


def attended_kernel(me_ref, *refs):
    blocks, (mixed_ref, inputs_ref, gains_ref) = refs[:10], refs[10:13]
    hidden_ref, normed_ref, factor_ref, rows_ref, whole_ref, weight_v, sems, out_sem = refs[13:]
    leaving = assemble(me_ref, blocks, weight_v, whole_ref, sems, out_sem)
    rows_ref[...] = mixed_ref[...].reshape(rows_ref.shape).astype(BF)
    hidden = inputs_ref[...].astype(F32) + dot(rows_ref[...], weight_v[...], 0, 0)
    factor = rms_factor(hidden)
    hidden_ref[...] = hidden
    factor_ref[...] = factor
    normed_ref[...] = (hidden * factor * gains_ref[1:2]).astype(BF)
    leaving.wait()


def assembled_call(kernel, out_shape, whole_shape, me, blocks, *operands):
    vmem, anywhere = pl.BlockSpec(memory_space=pltpu.VMEM), pl.BlockSpec(memory_space=pl.ANY)
    return glue_call(
        kernel,
        [*out_shape, jax.ShapeDtypeStruct(whole_shape, BF)],
        me,
        *blocks,
        *operands,
        in_specs=[pl.BlockSpec(memory_space=pltpu.SMEM)]
        + [anywhere] * len(blocks)
        + [vmem] * len(operands),
        out_specs=[vmem] * len(out_shape) + [anywhere],
        scratch_shapes=[
            pltpu.VMEM(whole_shape, BF),
            pltpu.SemaphoreType.DMA((32,)),
            pltpu.SemaphoreType.DMA((1,)),
        ],
    )


def token_kernel(
    own_ref,
    core_ref,
    last_x_ref,
    last_y_ref,
    gates_ref,
    router_ref,
    hidden_ref,
    factor_ref,
    gain_ref,
    grad_ref,
    normed_ref,
    weight_ref,
    hidden_grad_ref,
    branch_ref,
    mixed_grad_ref,
    extras_ref,
):
    copies = sum(ref[...].astype(F32) for ref in (own_ref, core_ref, last_x_ref, last_y_ref))
    columns, gates = copies[:, D:], gates_ref[...]
    gate_grad = columns + pltpu.roll(columns, EXTRA - 8, 1)
    inner_sum = jnp.sum(gates * gate_grad, axis=1, keepdims=True)
    logit_grad = (gates * (gate_grad - inner_sum)).astype(BF)
    gradient = copies[:, :D] + dot(logit_grad, router_ref[...], 1, 1)
    hidden, factor = hidden_ref[...], factor_ref[...]
    scaled = gradient * gain_ref[...]
    inner_mean = jnp.mean(scaled * hidden, axis=-1, keepdims=True)
    part = factor * scaled - hidden * (factor * factor * factor * inner_mean)
    hidden_grad = grad_ref[...].astype(F32) + part
    hidden_grad_ref[...] = hidden_grad
    branch = hidden_grad.astype(BF)
    branch_ref[...] = branch
    mixed_grad_ref[...] = dot(weight_ref[...], branch, 1, 1).astype(BF)
    gain_grad = jnp.sum(gradient * hidden * factor, axis=0, keepdims=True)
    router_grad = dot(logit_grad, normed_ref[...], 0, 0)
    row = lax.broadcasted_iota(jnp.int32, router_grad.shape, 0)
    extras_ref[...] = jnp.where(row == 8, gain_grad, router_grad)


def put_cut(me_ref, scratch, same_ref, other_ref):
    core, chip = lax.rem(me_ref[0], 2), lax.div(me_ref[0], 2)
    rows = same_ref.shape[2]
    for n in range(4):
        for side, ref in enumerate((same_ref, other_ref)):
            device = 2 * (chip ^ n) + (core ^ side)
            for a in range(4):
                start = pl.multiple_of((a * 8 + device) * rows, 16)
                ref[n, a] = scratch[pl.ds(start, rows), :]


def cut_shapes(rows, width):
    return [jax.ShapeDtypeStruct((4, 4, rows, width), BF)] * 2


def output_kernel(me_ref, mixed_ref, branch_ref, extras_ref, same_ref, other_ref, scratch):
    scratch[:, :D] = dot(mixed_ref[...], branch_ref[...], 1, 0).astype(BF)
    scratch[:, D:] = extras_ref[...].T.astype(BF)
    put_cut(me_ref, scratch, same_ref, other_ref)


def turned_back(value, cosine, sine):
    half = HD // 2
    first, second = value[:half], value[half:]
    return jnp.concatenate(
        [first * cosine + second * sine, second * cosine - first * sine], axis=0
    )


def query_kernel(
    me_ref, query_ref, cosine_ref, sine_ref, normed_ref, part_ref, same_ref, other_ref, scratch
):
    for h in range(H):
        part = turned_back(query_ref[h], cosine_ref[...], sine_ref[...])
        part_ref[h * HD : (h + 1) * HD] = part.astype(BF)
    scratch[...] = dot(normed_ref[...], part_ref[...], 0, 1).astype(BF)
    put_cut(me_ref, scratch, same_ref, other_ref)


def late_kernel(
    me_ref,
    own_ref,
    last_x_ref,
    last_y_ref,
    cosine_ref,
    sine_ref,
    normed_ref,
    part_ref,
    same_ref,
    other_ref,
    scratch,
):
    value = sum(ref[...].astype(F32) for ref in (own_ref, last_x_ref, last_y_ref)).T
    for h in range(KVH):
        part = turned_back(value[h * HD : (h + 1) * HD], cosine_ref[...], sine_ref[...])
        part_ref[h * HD : (h + 1) * HD] = part.astype(BF)
    part_ref[KW:] = value[KW:].astype(BF)
    scratch[...] = dot(normed_ref[...], part_ref[...], 0, 1).astype(BF)
    put_cut(me_ref, scratch, same_ref, other_ref)


def sums_kernel(same_ref, arrived_ref, own_ref, by_x_ref, by_y_ref, low_ref, high_ref):
    for n, ref in enumerate((own_ref, by_x_ref, by_y_ref)):
        ref[...] = total(same_ref[n], arrived_ref[n])
    for half, ref in enumerate((low_ref, high_ref)):

        @pl.when(pl.program_id(0) == half)
        def _():
            ref[...] = total(same_ref[3], arrived_ref[3])


def sums_call(same, arrived):
    _, parts, rows, width = same.shape
    half = parts // 2
    both = pl.BlockSpec((4, half, rows, width), lambda i: (0, i, 0, 0))
    one = pl.BlockSpec((half, rows, width), lambda i: (i, 0, 0))
    fixed = pl.BlockSpec((half, rows, width), lambda i: (0, 0, 0))
    shape = jax.ShapeDtypeStruct
    return glue_call(
        sums_kernel,
        [shape((parts, rows, width), BF)] * 3 + [shape((half, rows, width), BF)] * 2,
        same,
        arrived,
        grid=(2,),
        in_specs=[both] * 2,
        out_specs=[one] * 3 + [fixed] * 2,
    )


def over_hops(sums):
    return hop(sums[3], 2), hop(sums[4], 4)


def join_kernel(by_x_ref, by_y_ref, over_x_ref, over_y_ref, new_x_ref, new_y_ref):
    new_y_ref[...] = total(by_y_ref[...], over_x_ref[...])
    new_x_ref[...] = total(by_x_ref[...], over_y_ref[...])


def join_call(sums, over):
    by_x, by_y = sums[1:3]
    half = (by_x.shape[0] // 2, *by_x.shape[1:])
    low = pl.BlockSpec(half, lambda i: (0, 0, 0))
    high = pl.BlockSpec(half, lambda i: (1, 0, 0))
    return glue_call(
        join_kernel,
        [jax.ShapeDtypeStruct(by_x.shape, BF)] * 2,
        by_x,
        by_y,
        *over,
        grid=(1,),
        in_specs=[high, low, low, low],
        out_specs=[high, low],
        input_output_aliases={0: 0, 1: 1},
    )


def send_kernel(place_ref, *refs):
    groups, outs = (len(refs) - 4) // 3, refs[-4:]
    start = 0
    for g in range(groups):
        own_ref, last_x_ref, last_y_ref = refs[3 * g : 3 * g + 3]
        size = own_ref.shape[2]
        for step, out in enumerate(outs):
            at = lax.rem(place_ref[0] + step, 4)
            value = sum(ref[at].astype(F32) for ref in (own_ref, last_x_ref, last_y_ref))
            out[:, start : start + size] = value.astype(out.dtype)
        start += size


def send_call(*groups):
    rows, width = groups[0][0].shape[1], sum(group[0].shape[2] for group in groups)
    shape = jax.ShapeDtypeStruct
    own, *sent = glue_call(
        send_kernel,
        [shape((rows, width), F32)] + [shape((rows, width), BF)] * 3,
        lax.axis_index("dp")[None],
        *[part for group in groups for part in group],
    )
    return own, [
        lax.ppermute(value, "dp", [(i, (i + step) % 4) for i in range(4)])
        for step, value in enumerate(sent, 1)
    ]


def adam_kernel(pieces, step_rate, shrink, weight_ref, moment_ref, square_ref, *refs):
    grads, outs = refs[: len(pieces)], refs[len(pieces) :]
    for ref, (_, _, parts) in zip(grads, pieces):
        for source, target, size in parts:
            columns = slice(target, target + size)
            news = adam_update(
                weight_ref[:, columns],
                moment_ref[:, columns],
                square_ref[:, columns],
                ref[:, source : source + size].astype(F32),
                step_rate,
                shrink,
            )
            for out, new in zip(outs, news):
                out[:, columns] = new


def adam_call(weight, moment, square, pieces, step_rate, shrink, rows):
    width = weight.shape[2]
    state = pl.BlockSpec((None, rows, width), lambda i: (0, i, 0))
    return pl.pallas_call(
        lambda *refs: adam_kernel(pieces, step_rate, shrink, *refs),
        grid=(weight.shape[1] // rows,),
        in_specs=[state] * 3
        + [
            pl.BlockSpec((rows, piece.shape[1]), lambda i, first=first: (first + i, 0))
            for piece, first, _ in pieces
        ],
        out_specs=[state] * 3,
        out_shape=[jax.ShapeDtypeStruct(weight.shape, F32)] * 3,
        compiler_params=pltpu.CompilerParams(vmem_limit_bytes=VMEM_BYTES),
        cost_estimate=HINT,
    )(weight, moment, square, *[piece for piece, _, _ in pieces])


def owned_kernel(step_rate, weight_ref, moment_ref, square_ref, own_ref, *refs):
    arrived, outs, rest = refs[:3], refs[3:6], refs[6]
    total_grad = own_ref[...] + sum(ref[...].astype(F32) for ref in arrived)
    size = weight_ref.shape[1]
    weight, gradient = weight_ref[...], total_grad[:, :size]
    news = adam_update(
        weight, moment_ref[...], square_ref[...], gradient, step_rate, weight_decay
    )
    for out, new in zip(outs, news):
        out[...] = new
    if total_grad.shape[1] > size:
        rest[...] = total_grad[:, size:]
    else:
        products = jnp.sum(weight.astype(BF).astype(F32) * gradient, axis=1, keepdims=True)
        rest[...] = jnp.broadcast_to(products, rest.shape)


def owned_call(weight, moment, square, sums, step_rate):
    vmem = pl.BlockSpec(memory_space=pltpu.VMEM)
    state = jax.ShapeDtypeStruct(weight.shape, F32)
    return pl.pallas_call(
        lambda *refs: owned_kernel(step_rate, *refs),
        in_specs=[vmem] * 7,
        out_specs=[vmem] * 4,
        out_shape=[state] * 3 + [jax.ShapeDtypeStruct((weight.shape[0], EXTRA), F32)],
        compiler_params=pltpu.CompilerParams(vmem_limit_bytes=VMEM_BYTES),
        cost_estimate=HINT,
    )(weight, moment, square, *sums)


def input_kernel(query_ref, late_ref, weight_ref, tokens_ref, factor_ref, gain_ref, grad_ref, out_ref):
    gradient = dot(query_ref[...], weight_ref[:, :QW], 0, 1)
    gradient = gradient + dot(late_ref[...], weight_ref[:, QW:QKV], 0, 1)
    tokens, factor = tokens_ref[...].astype(F32), factor_ref[...]
    scaled = gradient * gain_ref[...]
    inner_mean = jnp.mean(scaled * tokens, axis=-1, keepdims=True)
    part = factor * scaled - tokens * (factor * factor * factor * inner_mean)
    out_ref[...] = grad_ref[...] + part


def input_call(*operands):
    vmem = pl.BlockSpec(memory_space=pltpu.VMEM)
    return pl.pallas_call(
        input_kernel,
        in_specs=[vmem] * 7,
        out_specs=vmem,
        out_shape=jax.ShapeDtypeStruct(operands[-1].shape, F32),
        compiler_params=pltpu.CompilerParams(vmem_limit_bytes=VMEM_BYTES),
        cost_estimate=HINT,
    )(*operands)


def gated(gate, up):
    rate = (2.0 / jnp.pi) ** 0.5
    bend = 0.044715 * rate
    square = gate * gate
    part = 0.5 + 0.5 * jnp.tanh(gate * (rate + bend * square))
    gelu = gate * part
    slope = part + gelu * (1.0 - part) * (2.0 * rate + 6.0 * bend * square)
    return gelu * up, slope * up, gelu


def local(
    inputs,
    cotangent,
    routes,
    project_weight,
    project_moment,
    project_square,
    output_weight,
    output_moment,
    output_square,
    router_weight,
    router_moment,
    router_square,
    norm_gains,
    gains_moment,
    gains_square,
    expert_in,
    expert_in_moment,
    expert_in_square,
    expert_down,
    expert_down_moment,
    expert_down_square,
):
    seq_count, stretch, width = inputs.shape
    device_count = lax.axis_size("expert")
    expert_count = device_count
    rows = seq_count * stretch
    me = lax.axis_index("expert")
    others = me ^ jnp.arange(device_count, dtype=jnp.int32)
    shard = project_weight.shape[0]

    first_payload = jnp.concatenate(
        [
            project_weight.astype(BF),
            router_weight.astype(BF),
            norm_gains.T.astype(BF),
            jnp.zeros((shard, EXTRA - expert_count - 2), BF),
        ],
        axis=1,
    )
    first_hops = [first_payload] + [plane_hop(first_payload, step) for step in (1, 2, 3)]
    own_grad = cotangent.reshape(rows, width)
    grad_near = gather_near(own_grad)
    in_low, down_low = expert_in[0].astype(BF), expert_down[0].astype(BF)
    share_first, share_second = [
        jnp.concatenate([in_low[:, p * HALF : (p + 1) * HALF] for p in (h, h + 2)], axis=1)
        for h in range(2)
    ]
    share_first = jnp.concatenate(
        [share_first, down_low[:, : 2 * HALF], down_low[:, 2 * HALF :]], axis=0
    )
    first_hops, grad_near, inputs, routes, output_low, place = phase(
        first_hops, grad_near, inputs, routes, output_weight, me
    )

    first_plane = plane_end(first_hops)
    first_near = gather_near(first_plane)
    output_low = output_low.astype(BF)
    output_hops = [output_low] + [plane_hop(output_low, step) for step in (1, 2, 3)]
    positions = place * stretch + jnp.arange(stretch, dtype=jnp.int32)
    frequency = rope_base ** (-jnp.arange(HD // 2, dtype=F32) / (HD // 2))
    angles = frequency[:, None] * positions.astype(F32)[None, :]
    cosine = jnp.tile(jnp.cos(angles), (1, seq_count))
    sine = jnp.tile(jnp.sin(angles), (1, seq_count))
    route_rows = jnp.concatenate(
        [routes.reshape(rows, TOP).T.astype(BF), jnp.zeros((32 - TOP, rows), BF)], axis=0
    )
    first_near, output_hops, share_first, share_second, cosine, sine, route_rows = phase(
        first_near, output_hops, share_first, share_second, cosine, sine, route_rows
    )

    weights_first = lax.all_gather(share_first, "dp")
    weights_second = lax.all_gather(share_second, "dp")
    first_over, first_cores = gather_over(first_near), gather_cores(first_near)
    first_sibling = hop(first_plane, 1)
    output_plane = plane_end(output_hops)
    first_over, first_cores, first_sibling, output_plane = phase(
        first_over, first_cores, first_sibling, output_plane
    )

    first_far = hop(first_over[0], 1), hop(first_over[1], 1)
    output_near, output_sibling = gather_near(output_plane), hop(output_plane, 1)
    first_far = phase(first_far)[0]

    inputs = inputs.reshape(rows, width)
    shape = jax.ShapeDtypeStruct
    queries, pair_payload, normed_one, factor_one, gains, router, full_first = assembled_call(
        project_kernel,
        [
            shape((H, HD, rows), BF),
            shape((2 * KW + 32, rows), BF),
            shape((rows, width), BF),
            shape((rows, 1), F32),
            shape((8, D), F32),
            shape((D, EXTRA), BF),
        ],
        (D, QKV + EXTRA),
        me[None],
        [
            first_plane,
            first_sibling,
            first_near[0],
            first_cores[0],
            first_near[1],
            first_cores[1],
            *first_over,
            *first_far,
        ],
        inputs,
        cosine,
        sine,
        route_rows,
    )
    pair_payload, output_near, output_sibling, queries = phase(
        pair_payload, output_near, output_sibling, queries
    )

    key_positions = (others[:, None] * stretch + jnp.arange(stretch)[None, :]).reshape(-1)
    bias = jnp.where(key_positions[:, None] <= positions[None, :], 0.0, masked_score).astype(F32)
    pair_near, pair_sibling = gather_near(pair_payload), hop(pair_payload, 1)
    output_over = gather_over(output_near)
    pair_near, pair_sibling, output_over, bias = phase(pair_near, pair_sibling, output_over, bias)

    pair_over, pair_cores = gather_over(pair_near), gather_cores(pair_near)
    output_core_x = hop(output_near[0], 1)
    pair_over, pair_cores, output_core_x = phase(pair_over, pair_cores, output_core_x)

    pair_diagonal = jnp.concatenate(pair_over, axis=0)
    pair_core, output_core_y = hop(pair_diagonal, 1), hop(output_near[1], 1)
    output_far = hop(output_over[0], 1), hop(output_over[1], 1)
    pair_core, output_core_y, output_far = phase(pair_core, output_core_y, output_far)

    pair_blocks = gathered(
        pair_payload, pair_sibling, pair_near, pair_cores, pair_diagonal, pair_core
    )
    pairs = jnp.stack(pair_blocks)
    lanes = jnp.arange(EXTRA, dtype=jnp.int32)[None, :]
    grad_over, grad_cores = gather_over(grad_near), gather_cores(grad_near)
    grad_sibling = hop(own_grad, 1)
    mixed, lse = attention_call(
        forward_kernel,
        [shape((H, HD, rows), F32), shape((seq_count, H, stretch), F32)],
        ["head", "row"],
        queries,
        pairs,
        bias,
    )
    mixed, lse, grad_over, grad_cores, grad_sibling = phase(
        mixed, lse, grad_over, grad_cores, grad_sibling
    )

    hidden_one, normed_two, factor_two, mixed_rows, full_output = assembled_call(
        attended_kernel,
        [
            shape((rows, width), F32),
            shape((rows, width), BF),
            shape((rows, 1), F32),
            shape((QW, rows), BF),
        ],
        (QW, D),
        me[None],
        [
            output_plane,
            output_sibling,
            output_near[0],
            output_core_x,
            output_near[1],
            output_core_y,
            *output_over,
            *output_far,
        ],
        mixed,
        inputs,
        gains,
    )

    row_near, row_sibling = gather_near(normed_two), hop(normed_two, 1)
    grad_diagonal = jnp.concatenate(grad_over, axis=0)
    grad_core = hop(grad_diagonal, 1)
    row_near, row_sibling, grad_core = phase(row_near, row_sibling, grad_core)
    grad_blocks = gathered(
        own_grad, grad_sibling, grad_near, grad_cores, grad_diagonal, grad_core
    )
    row_over, row_cores = gather_over(row_near), gather_cores(row_near)
    all_routes = jnp.concatenate(
        [block[2 * KW : 2 * KW + TOP].T for block in pair_blocks], axis=0
    ).astype(jnp.int32)
    named = jnp.any(all_routes[:, :, None] == lanes[None], axis=1)
    route_bias = jnp.where(named, 0.0, masked_score).astype(F32)
    row_over, row_cores, route_bias = phase(row_over, row_cores, route_bias)
    row_diagonal = jnp.concatenate(row_over, axis=0)
    row_core = phase(hop(row_diagonal, 1))[0]
    row_blocks = gathered(normed_two, row_sibling, row_near, row_cores, row_diagonal, row_core)
    gates, gate_grad_first, up_first, hidden_first, in_grad_first = first_call(
        me[None], row_blocks, grad_blocks, route_bias, weights_first, router
    )
    grads_first = lax.psum_scatter(in_grad_first, "dp")

    def second_part(t, *others):
        return second_call(
            t,
            me[None],
            row_blocks,
            grad_blocks,
            gates,
            gate_grad_first,
            after(up_first, *others),
            hidden_first,
            weights_first,
            weights_second,
        )

    far = second_part(3)
    far_cores = hop(far[1], 1), hop(far[3], 1)
    by_y = second_part(2, far[0])
    far_cores, by_y = phase(far_cores, by_y)
    diagonal = total(far[0], far_cores[0])
    copy_over = reduce_over(diagonal)
    by_y_cores = hop(by_y[1], 1), hop(by_y[3], 1)
    result_diagonal = total(far[2], far_cores[1])
    by_x = second_part(1, diagonal, result_diagonal)
    copy_over, by_y_cores, by_x, result_diagonal = phase(
        copy_over, by_y_cores, by_x, result_diagonal
    )
    result_over, by_x_cores = reduce_over(result_diagonal), (hop(by_x[1], 1), hop(by_x[3], 1))
    copy_y, result_y = total(by_y[0], by_y_cores[0]), total(by_y[2], by_y_cores[1])
    own = second_part(0, by_x[0], copy_y, result_y)
    result_over, by_x_cores, own, copy_y, result_y = phase(
        result_over, by_x_cores, own, copy_y, result_y
    )
    copy_last = reduce_last(total(by_x[0], by_x_cores[0]), copy_y, copy_over)
    last = last_hops(*copy_last)
    own_cores = hop(own[1], 1), hop(own[3], 1)
    result_last = reduce_last(
        total(by_x[2], after(by_x_cores[1], *copy_last)), result_y, result_over
    )
    parts = (own, by_x, by_y, far)
    weight_grads = last_call(
        row_blocks,
        grad_blocks,
        [part[4] for part in parts],
        [part[5] for part in parts],
        after(hidden_first, *result_last, grads_first),
    )
    grads_second = lax.psum_scatter(weight_grads, "dp")
    last, own_cores, weight_grads, result_last = phase(last, own_cores, weight_grads, result_last)

    hidden_grad_one, branch_grad, mixed_grad, extras = glue_call(
        token_kernel,
        [
            jax.ShapeDtypeStruct((rows, width), F32),
            jax.ShapeDtypeStruct((rows, width), BF),
            jax.ShapeDtypeStruct((QW, rows), BF),
            jax.ShapeDtypeStruct((EXTRA, D), F32),
        ],
        own[0],
        own_cores[0],
        *last,
        gates[:rows],
        router,
        hidden_one,
        factor_two,
        gains[1:2],
        own_grad,
        normed_two,
        full_output,
        scalars=0,
    )
    mixed_grad = mixed_grad.reshape(H, HD, rows)
    mixed_grad, branch_grad, extras, hidden_grad_one, result_last = phase(
        mixed_grad, branch_grad, extras, hidden_grad_one, result_last
    )

    result_hops = last_hops(*result_last)
    query_grad, pairs_same, pairs_other = attention_call(
        backward_kernel,
        [
            jax.ShapeDtypeStruct((H, HD, rows), F32),
            jax.ShapeDtypeStruct((4, rows, 2 * KW), BF),
            jax.ShapeDtypeStruct((4, rows, 2 * KW), BF),
        ],
        ["head"] + [pl.BlockSpec((4, stretch, 2 * KW), lambda s: (0, s, 0))] * 2,
        queries,
        pairs,
        bias,
        mixed,
        lse,
        mixed_grad,
    )
    query_grad, pairs_same, pairs_other, cosine, sine = phase(
        query_grad, pairs_same, pairs_other, cosine, sine
    )

    pair_cores = hop(pairs_other, 1)
    output_same, output_other = glue_call(
        output_kernel,
        cut_shapes(shard, D + EXTRA),
        me[None],
        mixed_rows,
        branch_grad,
        extras,
        scratch_shapes=[pltpu.VMEM((QW, D + EXTRA), BF)],
    )
    pair_cores, output_same, output_other, result_hops = phase(
        pair_cores, output_same, output_other, result_hops
    )

    quarters = (4, 4, rows // 4, 2 * KW)
    pair_sums = sums_call(pairs_same.reshape(quarters), pair_cores.reshape(quarters))
    pair_over, output_cores = over_hops(pair_sums), hop(output_other, 1)
    query_part, query_same, query_other = glue_call(
        query_kernel,
        [jax.ShapeDtypeStruct((QW, rows), BF)] + cut_shapes(shard, QW),
        me[None],
        after(query_grad, *pair_sums),
        cosine,
        sine,
        normed_one,
        scratch_shapes=[pltpu.VMEM((D, QW), BF)],
    )
    pair_over, pair_sums, query_same, query_other, query_part, output_cores = phase(
        pair_over, pair_sums, query_same, query_other, query_part, output_cores
    )

    pair_last = join_call(pair_sums, pair_over)
    pair_hops, query_cores = last_hops(*pair_last), hop(query_other, 1)
    output_sums = sums_call(output_same, after(output_cores, *pair_last))
    output_over = over_hops(output_sums)
    pair_hops, query_cores, output_sums, output_over = phase(
        pair_hops, query_cores, output_sums, output_over
    )

    late_part, late_same, late_other = glue_call(
        late_kernel,
        [jax.ShapeDtypeStruct((2 * KW, rows), BF)] + cut_shapes(shard, 2 * KW),
        me[None],
        *[value.reshape(rows, 2 * KW) for value in (pair_sums[0], *pair_hops)],
        cosine,
        sine,
        normed_one,
        scratch_shapes=[pltpu.VMEM((D, 2 * KW), BF)],
    )
    late_cores = hop(late_other, 1)
    output_last = join_call(output_sums, after(output_over, late_other))
    output_hops = last_hops(*output_last)
    query_sums = sums_call(query_same, after(query_cores, *output_last))
    query_over = over_hops(query_sums)
    output_hops, late_cores, late_same, late_part, query_sums, query_over = phase(
        output_hops, late_cores, late_same, late_part, query_sums, query_over
    )

    late_sums = sums_call(late_same, late_cores)
    late_over = over_hops(late_sums)
    query_last = join_call(query_sums, after(query_over, *late_sums))
    query_hops = last_hops(*query_last)
    input_grad = input_call(
        query_part,
        after(late_part, *query_last),
        full_first,
        inputs,
        factor_one,
        gains[0:1],
        hidden_grad_one,
    )
    late_over, query_hops, late_sums, input_grad, grads_first, grads_second = phase(
        late_over, query_hops, late_sums, input_grad, grads_first, grads_second
    )

    late_last = join_call(late_sums, late_over)
    late_hops = last_hops(*late_last)
    output_own, output_arrived = send_call(
        (output_sums[0], *after(output_hops, *late_last))
    )
    grads_first, grads_second = phase(grads_first, grads_second, late_last, output_own)[:2]
    in_new = adam_call(
        expert_in,
        expert_in_moment,
        expert_in_square,
        [
            (grads_first, 0, [(0, 0, HALF), (HALF, FF, HALF)]),
            (grads_second, 0, [(0, HALF, HALF), (HALF, FF + HALF, HALF)]),
        ],
        3.0 / D**0.5,
        weight_decay,
        ROWS // 4,
    )
    down_new = adam_call(
        expert_down,
        expert_down_moment,
        expert_down_square,
        [
            (grads_second, 4, [(0, 0, 2 * HALF)]),
            (grads_second, 6, [(0, 2 * HALF, 2 * HALF)]),
        ],
        12.0 / FF**0.5,
        weight_decay,
        ROWS // 4,
    )
    late_hops, output_arrived, output_own, in_new, down_new = phase(
        late_hops, output_arrived, output_own, in_new, down_new
    )

    project_own, project_arrived = send_call(
        (query_sums[0], *query_hops), (late_sums[0], *late_hops)
    )
    output_own = after(output_own, project_own)
    sequence = stretch * device_count
    *output_new, output_rest = owned_call(
        output_weight,
        output_moment,
        output_square,
        [output_own, *output_arrived],
        3.0 * (sequence / (32.0 * H * HD)) ** 0.5,
    )
    outputs = hidden_one + reduced(
        total(own[2], after(own_cores[1], output_rest)), result_hops
    )
    project_arrived, output_new, output_rest, outputs = phase(
        project_arrived, output_new, output_rest, outputs
    )
    *project_new, products = owned_call(
        project_weight,
        project_moment,
        project_square,
        [project_own, *project_arrived],
        3.0 * (2.0 / D) ** 0.5,
    )
    router_new = adam_update(
        router_weight,
        router_moment,
        router_square,
        output_rest[:, :expert_count],
        1.5 / D**0.5,
        weight_decay,
    )
    own_gains = norm_gains.astype(BF).astype(F32)
    gains_sum = jnp.stack([products[:, 0] / own_gains[0], output_rest[:, expert_count]])
    gains_new = adam_update(norm_gains, gains_moment, gains_square, gains_sum, 0.8, 0.0)
    return (
        outputs.reshape(seq_count, stretch, width),
        input_grad.reshape(seq_count, stretch, width),
        *project_new,
        *output_new,
        *router_new,
        *gains_new,
        *in_new,
        *down_new,
    )


def rms_norm(values, gain_row):
    factor = lax.rsqrt(jnp.mean(values * values, axis=-1, keepdims=True) + norm_epsilon)
    return values * factor * gain_row


def rotate(values, positions):
    half_width = values.shape[-1] // 2
    frequency = rope_base ** (-jnp.arange(half_width, dtype=jnp.float32) / half_width)
    angles = positions.astype(jnp.float32)[:, None] * frequency[None, :]
    cosine = jnp.cos(angles)[:, None, :]
    sine_part = jnp.sin(angles)[:, None, :]
    first_half = values[..., :half_width]
    second_half = values[..., half_width:]
    return jnp.concatenate(
        [
            first_half * cosine - second_half * sine_part,
            second_half * cosine + first_half * sine_part,
        ],
        axis=-1,
    )


def gated_unit(gate_up):
    return jax.nn.gelu(gate_up[..., :FF], approximate=True) * gate_up[..., FF:]


def slot_tables(route_block, expert_count, capacity):
    flat_routes = route_block.reshape(-1)
    pick_count = flat_routes.shape[0]
    onehot = (flat_routes[:, None] == jnp.arange(expert_count, dtype=jnp.int32)[None, :]).astype(
        jnp.int32
    )
    earlier = jnp.cumsum(onehot, axis=0) - onehot
    rank_values = jnp.sum(earlier * onehot, axis=1)
    slot_index = flat_routes * capacity + rank_values
    slot_table = (
        jnp.full((expert_count * capacity,), pick_count, jnp.int32)
        .at[slot_index]
        .set(jnp.arange(pick_count, dtype=jnp.int32))
    )
    return (slot_index, slot_table)


def attention_blocks(step_fn, carried, key_values, last_query):
    key_count = key_values.shape[1]
    block_keys = 512

    def one_turn(turn_index, state_now):
        offset = turn_index * block_keys
        key_block = lax.dynamic_slice_in_dim(key_values, offset, block_keys, 1)
        return lax.cond(
            offset > last_query,
            lambda held_state: held_state,
            lambda held_state: step_fn(held_state, key_block, offset),
            state_now,
        )

    return lax.fori_loop(0, key_count // block_keys, one_turn, carried)


def general(
    inputs,
    cotangent,
    routes,
    project_weight,
    project_moment,
    project_square,
    output_weight,
    output_moment,
    output_square,
    router_weight,
    router_moment,
    router_square,
    norm_gains,
    gains_moment,
    gains_square,
    expert_in,
    expert_in_moment,
    expert_in_square,
    expert_down,
    expert_down_moment,
    expert_down_square,
):
    seq_count, stretch_len, model_width = inputs.shape
    expert_devices = lax.axis_size("expert")
    seq_length = stretch_len * expert_devices
    expert_count = EXP_DEV * expert_devices
    row_count = seq_count * stretch_len
    capacity = 2 * row_count * TOP // expert_count
    group_size = H // KVH
    query_width = H * HD
    key_width = KVH * HD
    group_rows = group_size * stretch_len
    score_scale = HD ** (-0.5)
    first_query = lax.axis_index("expert") * stretch_len
    last_query = first_query + stretch_len - 1
    full_project, full_output, full_router, full_gains = (
        lax.all_gather(project_weight.astype(jnp.bfloat16), ("dp", "expert"), axis=0, tiled=True),
        lax.all_gather(output_weight.astype(jnp.bfloat16), ("dp", "expert"), axis=0, tiled=True),
        lax.all_gather(router_weight.astype(jnp.bfloat16), ("dp", "expert"), axis=0, tiled=True),
        lax.all_gather(norm_gains.astype(jnp.bfloat16), ("dp", "expert"), axis=1, tiled=True),
    )
    full_in, full_down = (
        lax.all_gather(expert_in.astype(jnp.bfloat16), "dp", axis=1, tiled=True),
        lax.all_gather(expert_down.astype(jnp.bfloat16), "dp", axis=1, tiled=True),
    )
    gain_values = full_gains.astype(jnp.float32)
    tokens = inputs.astype(jnp.float32).reshape(row_count, model_width)
    normed_one = rms_norm(tokens, gain_values[0]).astype(jnp.bfloat16)
    projected = jnp.dot(normed_one, full_project, preferred_element_type=jnp.float32).reshape(
        seq_count, stretch_len, -1
    )
    positions = first_query + jnp.arange(stretch_len, dtype=jnp.int32)

    def rope_back(gradient):
        unused, pullback = jax.vjp(
            lambda values: rotate(values, positions), jnp.zeros_like(gradient)
        )
        return pullback(gradient)[0]

    queries = rotate(
        projected[..., :query_width].reshape(seq_count, stretch_len, H, HD), positions
    ).astype(jnp.bfloat16)
    rotated_keys = rotate(
        projected[..., query_width : query_width + key_width].reshape(
            seq_count, stretch_len, KVH, HD
        ),
        positions,
    ).astype(jnp.bfloat16)
    values = projected[..., query_width + key_width :].astype(jnp.bfloat16)
    local_pairs = jnp.concatenate(
        [rotated_keys.reshape(seq_count, stretch_len, key_width), values], axis=-1
    )
    all_pairs = lax.all_gather(local_pairs, "expert", axis=1, tiled=True)

    def to_grid(token_rows):
        return (
            token_rows.reshape(seq_count, stretch_len, KVH, group_size, HD)
            .transpose(0, 2, 3, 1, 4)
            .reshape(seq_count, KVH, group_rows, HD)
        )

    def from_grid(grid_rows):
        return (
            grid_rows.reshape(seq_count, KVH, group_size, stretch_len, HD)
            .transpose(0, 3, 1, 2, 4)
            .reshape(row_count, query_width)
        )

    query_grid = to_grid(queries)
    row_positions = first_query + jnp.arange(group_rows, dtype=jnp.int32) % stretch_len

    def scores_for(sequence, key_block, offset):
        key_part = key_block[sequence, :, :key_width].reshape(-1, KVH, HD)
        raw_scores = (
            jnp.einsum(
                "krd,nkd->krn", query_grid[sequence], key_part, preferred_element_type=jnp.float32
            )
            * score_scale
        )
        key_positions = offset + jnp.arange(key_block.shape[1], dtype=jnp.int32)
        allowed = (key_positions[None, :] <= row_positions[:, None])[None]
        return (raw_scores, allowed)

    def stats_step(carried, key_block, offset):
        top_now, total_now = carried
        new_tops = []
        new_totals = []
        for sequence in range(seq_count):
            raw_scores, allowed = scores_for(sequence, key_block, offset)
            masked = jnp.where(allowed, raw_scores, masked_score)
            top_new = jnp.maximum(top_now[sequence], jnp.max(masked, axis=-1))
            weights = jnp.where(allowed, jnp.exp(masked - top_new[..., None]), 0.0)
            new_totals.append(
                total_now[sequence] * jnp.exp(top_now[sequence] - top_new)
                + jnp.sum(weights, axis=-1)
            )
            new_tops.append(top_new)
        return (jnp.stack(new_tops), jnp.stack(new_totals))

    stats_shape = (seq_count, KVH, group_rows)
    top_all, total_all = attention_blocks(
        stats_step,
        (jnp.full(stats_shape, masked_score, jnp.float32), jnp.zeros(stats_shape, jnp.float32)),
        all_pairs,
        last_query,
    )
    log_total = top_all + jnp.log(total_all)

    def softmax_for(sequence, key_block, offset):
        raw_scores, allowed = scores_for(sequence, key_block, offset)
        return jnp.where(
            allowed,
            jnp.exp(jnp.where(allowed, raw_scores, masked_score) - log_total[sequence][..., None]),
            0.0,
        )

    def mix_step(carried, key_block, offset):
        new_rows = []
        for sequence in range(seq_count):
            softmax_rows = softmax_for(sequence, key_block, offset).astype(jnp.bfloat16)
            value_part = key_block[sequence, :, key_width:].reshape(-1, KVH, HD)
            new_rows.append(
                carried[sequence]
                + jnp.einsum(
                    "krn,nkd->krd", softmax_rows, value_part, preferred_element_type=jnp.float32
                )
            )
        return jnp.stack(new_rows)

    mixed_grid = attention_blocks(
        mix_step, jnp.zeros((seq_count, KVH, group_rows, HD), jnp.float32), all_pairs, last_query
    )
    mixed_rows = from_grid(mixed_grid).astype(jnp.bfloat16)
    hidden_one = tokens + jnp.dot(mixed_rows, full_output, preferred_element_type=jnp.float32)
    normed_two = rms_norm(hidden_one, gain_values[1]).astype(jnp.bfloat16)
    logits = jnp.dot(normed_two, full_router, preferred_element_type=jnp.float32)
    route_rows = routes.reshape(row_count, TOP)
    onehot = (
        route_rows[:, :, None] == jnp.arange(expert_count, dtype=jnp.int32)[None, None, :]
    ).astype(jnp.float32)
    gate_weights = jax.nn.softmax(
        jnp.einsum("rte,re->rt", onehot, logits, precision=lax.Precision.HIGHEST), axis=-1
    )
    slot_index, slot_table = slot_tables(route_rows, expert_count, capacity)
    padded = jnp.concatenate([normed_two, jnp.zeros((1, model_width), jnp.bfloat16)], axis=0)
    sent_rows = padded[slot_table // TOP].reshape(expert_count, capacity, model_width)
    arrived_rows = lax.all_to_all(sent_rows, "expert", split_axis=0, concat_axis=0, tiled=True)
    batched = arrived_rows.reshape(expert_devices, EXP_DEV, -1, model_width)
    gate_up = jnp.einsum("neid,edf->neif", batched, full_in, preferred_element_type=jnp.float32)
    hidden = gated_unit(gate_up).astype(jnp.bfloat16)
    result = jnp.einsum(
        "neif,efd->neid", hidden, full_down, preferred_element_type=jnp.float32
    ).astype(jnp.bfloat16)
    results = result.reshape(arrived_rows.shape)
    kept_gate_up = gate_up.reshape(arrived_rows.shape[0], arrived_rows.shape[1], 2 * FF)
    returned = lax.all_to_all(results, "expert", split_axis=0, concat_axis=0, tiled=True)
    picked = returned.reshape(expert_count * capacity, model_width)[slot_index].reshape(
        row_count, TOP, model_width
    )
    picked_wide = picked.astype(jnp.float32)
    mixture = jnp.sum(gate_weights[:, :, None] * picked_wide, axis=1)
    outputs = hidden_one + mixture
    grad_rows = cotangent.astype(jnp.float32).reshape(row_count, model_width)
    gate_grad = jnp.sum(grad_rows[:, None, :] * picked_wide, axis=-1)
    chosen_grad = gate_weights * (
        gate_grad - jnp.sum(gate_weights * gate_grad, axis=-1, keepdims=True)
    )
    logit_grad = jnp.einsum(
        "rte,rt->re", onehot, chosen_grad, precision=lax.Precision.HIGHEST
    ).astype(jnp.bfloat16)
    copy_out_grad = (
        (gate_weights[:, :, None] * grad_rows[:, None, :])
        .astype(jnp.bfloat16)
        .reshape(row_count * TOP, model_width)
    )
    grad_sent = jnp.concatenate([copy_out_grad, jnp.zeros((1, model_width), jnp.bfloat16)], axis=0)[
        slot_table
    ].reshape(expert_count, capacity, model_width)
    grad_arrived = lax.all_to_all(grad_sent, "expert", split_axis=0, concat_axis=0, tiled=True)
    batched_grad = grad_arrived.reshape(expert_devices, EXP_DEV, -1, model_width)
    batched_in = arrived_rows.reshape(expert_devices, EXP_DEV, -1, model_width)
    gate_up = kept_gate_up.reshape(expert_devices, EXP_DEV, -1, 2 * FF)
    hidden, unit_pull = jax.vjp(gated_unit, gate_up)
    grad_down = jnp.einsum(
        "neif,neid->efd",
        hidden.astype(jnp.bfloat16),
        batched_grad,
        preferred_element_type=jnp.float32,
    )
    hidden_grad = jnp.einsum(
        "neid,efd->neif", batched_grad, full_down, preferred_element_type=jnp.float32
    )
    gate_up_grad = unit_pull(hidden_grad)[0].astype(jnp.bfloat16)
    grad_in = jnp.einsum(
        "neid,neif->edf", batched_in, gate_up_grad, preferred_element_type=jnp.float32
    )
    copy_in_grad = (
        jnp.einsum("neif,edf->neid", gate_up_grad, full_in, preferred_element_type=jnp.float32)
        .astype(jnp.bfloat16)
        .reshape(arrived_rows.shape)
    )
    expert_in_grad, expert_down_grad = (
        lax.psum_scatter(
            grad_in.astype(jnp.bfloat16), "dp", scatter_dimension=1, tiled=True
        ).astype(jnp.float32),
        lax.psum_scatter(
            grad_down.astype(jnp.bfloat16), "dp", scatter_dimension=1, tiled=True
        ).astype(jnp.float32),
    )
    returned_grad = lax.all_to_all(copy_in_grad, "expert", split_axis=0, concat_axis=0, tiled=True)
    copies_grad = returned_grad.reshape(expert_count * capacity, model_width)[slot_index].reshape(
        row_count, TOP, model_width
    )
    normed_two_grad = jnp.sum(copies_grad.astype(jnp.float32), axis=1) + jnp.dot(
        logit_grad, full_router.T, preferred_element_type=jnp.float32
    )
    router_grad_full = jnp.einsum(
        "rd,re->de", normed_two, logit_grad, preferred_element_type=jnp.float32
    )
    unused_two, norm_two_pull = jax.vjp(rms_norm, hidden_one, gain_values[1])
    hidden_part, gain_two_grad = norm_two_pull(normed_two_grad)
    hidden_grad_one = grad_rows + hidden_part
    branch_grad = hidden_grad_one.astype(jnp.bfloat16)
    output_grad_full = jnp.einsum(
        "rh,rd->hd", mixed_rows, branch_grad, preferred_element_type=jnp.float32
    )
    mixed_grad = jnp.dot(branch_grad, full_output.T, preferred_element_type=jnp.float32).astype(
        jnp.bfloat16
    )
    mixed_grad_grid = to_grid(mixed_grad.reshape(seq_count, stretch_len, H, HD))
    row_delta = jnp.sum(mixed_grad_grid.astype(jnp.float32) * mixed_grid, axis=-1)

    def back_step(carried, key_block, offset):
        query_grad, pair_grad = carried
        new_query = []
        block_len = key_block.shape[1]
        for sequence in range(seq_count):
            softmax_rows = softmax_for(sequence, key_block, offset)
            key_part = key_block[sequence, :, :key_width].reshape(-1, KVH, HD)
            value_part = key_block[sequence, :, key_width:].reshape(-1, KVH, HD)
            softmax_grad = jnp.einsum(
                "krd,nkd->krn",
                mixed_grad_grid[sequence],
                value_part,
                preferred_element_type=jnp.float32,
            )
            score_grad = (softmax_rows * (softmax_grad - row_delta[sequence][..., None])).astype(
                jnp.bfloat16
            )
            new_query.append(
                query_grad[sequence]
                + jnp.einsum(
                    "krn,nkd->krd", score_grad, key_part, preferred_element_type=jnp.float32
                )
                * score_scale
            )
            key_grad = (
                jnp.einsum(
                    "krn,krd->nkd",
                    score_grad,
                    query_grid[sequence],
                    preferred_element_type=jnp.float32,
                )
                * score_scale
            )
            value_grad = jnp.einsum(
                "krn,krd->nkd",
                softmax_rows.astype(jnp.bfloat16),
                mixed_grad_grid[sequence],
                preferred_element_type=jnp.float32,
            )
            block_grad = jnp.concatenate(
                [key_grad.reshape(block_len, key_width), value_grad.reshape(block_len, key_width)],
                axis=-1,
            )
            current = lax.dynamic_slice(
                pair_grad,
                (jnp.int32(sequence), offset, jnp.int32(0)),
                (1, block_len, 2 * key_width),
            )
            pair_grad = lax.dynamic_update_slice(
                pair_grad, current + block_grad[None], (jnp.int32(sequence), offset, jnp.int32(0))
            )
        return (jnp.stack(new_query), pair_grad)

    query_start = jnp.zeros((seq_count, KVH, group_rows, HD), jnp.float32)
    pair_start = jnp.zeros((seq_count, seq_length, 2 * key_width), jnp.float32)
    query_grad_grid, pair_grad_all = attention_blocks(
        back_step, (query_start, pair_start), all_pairs, last_query
    )
    pair_grad_local = lax.psum_scatter(
        pair_grad_all.astype(jnp.bfloat16), "expert", scatter_dimension=1, tiled=True
    ).astype(jnp.float32)
    query_grad_rows = rope_back(from_grid(query_grad_grid).reshape(seq_count, stretch_len, H, HD))
    key_grad_rows = rope_back(
        pair_grad_local[..., :key_width].reshape(seq_count, stretch_len, KVH, HD)
    )
    projected_grad = jnp.concatenate(
        [
            query_grad_rows.reshape(row_count, query_width),
            key_grad_rows.reshape(row_count, key_width),
            pair_grad_local[..., key_width:].reshape(row_count, key_width),
        ],
        axis=-1,
    ).astype(jnp.bfloat16)
    project_grad_full = jnp.einsum(
        "rd,rf->df", normed_one, projected_grad, preferred_element_type=jnp.float32
    )
    normed_one_grad = jnp.dot(projected_grad, full_project.T, preferred_element_type=jnp.float32)
    unused_one, norm_one_pull = jax.vjp(rms_norm, tokens, gain_values[0])
    token_part, gain_one_grad = norm_one_pull(normed_one_grad)
    input_grad = hidden_grad_one + token_part
    gains_grad_full = jnp.stack([gain_one_grad, gain_two_grad])
    project_grad, output_grad, router_grad, gains_grad = (
        lax.psum_scatter(project_grad_full, ("dp", "expert"), scatter_dimension=0, tiled=True),
        lax.psum_scatter(output_grad_full, ("dp", "expert"), scatter_dimension=0, tiled=True),
        lax.psum_scatter(router_grad_full, ("dp", "expert"), scatter_dimension=0, tiled=True),
        lax.psum_scatter(gains_grad_full, ("dp", "expert"), scatter_dimension=1, tiled=True),
    )
    rate_project = 3.0 * (2.0 / D) ** 0.5
    rate_output = 3.0 * (seq_length / (32.0 * H * HD)) ** 0.5
    rate_router = 1.5 / D**0.5
    rate_gains = 0.8
    rate_in = 3.0 / D**0.5
    rate_down = 12.0 / FF**0.5
    project_new = adam_update(
        project_weight, project_moment, project_square, project_grad, rate_project, weight_decay
    )
    output_new = adam_update(
        output_weight, output_moment, output_square, output_grad, rate_output, weight_decay
    )
    router_new = adam_update(
        router_weight, router_moment, router_square, router_grad, rate_router, weight_decay
    )
    gains_new = adam_update(norm_gains, gains_moment, gains_square, gains_grad, rate_gains, 0.0)
    in_new = adam_update(
        expert_in, expert_in_moment, expert_in_square, expert_in_grad, rate_in, weight_decay
    )
    down_new = adam_update(
        expert_down,
        expert_down_moment,
        expert_down_square,
        expert_down_grad,
        rate_down,
        weight_decay,
    )
    return (
        outputs.reshape(seq_count, stretch_len, model_width),
        input_grad.reshape(seq_count, stretch_len, model_width),
        project_new[0],
        project_new[1],
        project_new[2],
        output_new[0],
        output_new[1],
        output_new[2],
        router_new[0],
        router_new[1],
        router_new[2],
        gains_new[0],
        gains_new[1],
        gains_new[2],
        in_new[0],
        in_new[1],
        in_new[2],
        down_new[0],
        down_new[1],
        down_new[2],
    )


def solution(mesh):
    token_spec = P("dp", "expert", None)
    row_spec = P(("dp", "expert"), None)
    gain_spec = P(None, ("dp", "expert"))
    expert_spec = P("expert", "dp", None)
    states = (row_spec,) * 9 + (gain_spec,) * 3 + (expert_spec,) * 6
    small = mesh.shape["dp"] == 4 and mesh.shape["expert"] == 8
    return jax.shard_map(
        local if small else general,
        mesh=mesh,
        in_specs=(token_spec, token_spec, P(("dp", "expert"), None, None)) + states,
        out_specs=(token_spec, token_spec) + states,
        check_vma=False,
    )
```

```python
import jax
import jax.numpy as jnp
from jax import lax
from jax.experimental import pallas as pl
from jax.experimental.pallas import tpu as pltpu
from jax.sharding import PartitionSpec as P

D = 1536
H = 12
KVH = 2
HD = 128
FF = 768
TOP = 4
STEP = 10
GROUP = H // KVH
QW = H * HD
KW = KVH * HD
QKV = QW + 2 * KW
EXP_DEV = 1
EXTRA = 128

norm_epsilon = 1e-06
adam_epsilon = 1e-08
beta_first = 0.9
beta_second = 0.95
weight_decay = 0.1
rope_base = 1000000.0
masked_score = -1e30
score_scale = HD ** (-0.5)
BF = jnp.bfloat16
F32 = jnp.float32
VMEM_BYTES = 50 * 1024 * 1024
HINT = pl.CostEstimate(flops=0, bytes_accessed=0, transcendentals=0)


def dot(a, b, da, db):
    return lax.dot_general(a, b, (((da,), (db,)), ((), ())), preferred_element_type=F32)


def after(value, *others):
    return lax.optimization_barrier((value, *others))[0]


def bring(pairs, sems):
    copies = [pltpu.make_async_copy(a, b, sems.at[n]) for n, (a, b) in enumerate(pairs)]
    for copy in copies:
        copy.start()
    return copies


def glue_call(kernel, out_shape, *operands, scalars=1, **options):
    vmem = pl.BlockSpec(memory_space=pltpu.VMEM)
    options.setdefault(
        "in_specs",
        [pl.BlockSpec(memory_space=pltpu.SMEM)] * scalars + [vmem] * (len(operands) - scalars),
    )
    options.setdefault("out_specs", [vmem] * len(out_shape))
    return pl.pallas_call(
        kernel,
        out_shape=out_shape,
        compiler_params=pltpu.CompilerParams(vmem_limit_bytes=VMEM_BYTES),
        cost_estimate=HINT,
        **options,
    )(*operands)


def plane_kernel(place_ref, *refs):
    blocks, out_ref, sems = refs[:4], refs[4], refs[5]
    moves = [
        (block, out_ref.at[lax.rem(place_ref[0] + step, 4)]) for step, block in enumerate(blocks)
    ]
    for copy in bring(moves, sems):
        copy.wait()


def plane_end(blocks):
    anywhere = pl.BlockSpec(memory_space=pl.ANY)
    return glue_call(
        plane_kernel,
        [jax.ShapeDtypeStruct((4,) + blocks[0].shape, BF)],
        lax.axis_index("dp")[None],
        *blocks,
        in_specs=[pl.BlockSpec(memory_space=pltpu.SMEM)] + [anywhere] * 4,
        out_specs=[anywhere],
        scratch_shapes=[pltpu.SemaphoreType.DMA((4,))],
    )[0]


def halves_kernel(by_x_ref, by_y_ref, low_ref, high_ref, sems):
    half = low_ref.shape[0]
    moves = [(by_x_ref.at[pl.ds(0, half)], low_ref), (by_y_ref.at[pl.ds(half, half)], high_ref)]
    for copy in bring(moves, sems):
        copy.wait()


def halves_call(near):
    anywhere = pl.BlockSpec(memory_space=pl.ANY)
    half = jax.ShapeDtypeStruct((near[0].shape[0] // 2, *near[0].shape[1:]), BF)
    return glue_call(
        halves_kernel,
        [half, half],
        *near,
        in_specs=[anywhere] * 2,
        out_specs=[anywhere] * 2,
        scratch_shapes=[pltpu.SemaphoreType.DMA((2,))],
    )


def hop(value, mask):
    return lax.ppermute(value, "expert", [(i, i ^ mask) for i in range(8)])


def total(one, two):
    return (one.astype(F32) + two.astype(F32)).astype(one.dtype)


def gather_near(value):
    return hop(value, 2), hop(value, 4)


def gather_over(near):
    low, high = halves_call(near)
    return hop(low, 4), hop(high, 2)


def gather_cores(near):
    return hop(near[0], 1), hop(near[1], 1)


def gathered(value, sibling, near, cores, diagonal, diagonal_core):
    return [value, sibling, near[0], cores[0], near[1], cores[1], diagonal, diagonal_core]


def reduce_over(diagonal):
    half = diagonal.shape[0] // 2
    return hop(diagonal[:half], 2), hop(diagonal[half:], 4)


def last_hops(by_x, by_y):
    return hop(by_x, 2), hop(by_y, 4)


def reduced(own, last):
    return own.astype(F32) + last[0].astype(F32) + last[1].astype(F32)


def phase(*values):
    return lax.optimization_barrier(values)


def plane_hop(shard, step):
    return lax.ppermute(shard, "dp", [((i + step) % 4, i) for i in range(4)])


def key_block(kv_ref, row):
    return jnp.concatenate(
        [kv_ref[n, row : row + HD, :].astype(F32).T for n in range(kv_ref.shape[0])], axis=0
    ).astype(BF)


def two(ref, h):
    return jnp.concatenate([ref[h], ref[h + 1]], axis=1)


def forward_kernel(q_ref, kv_ref, bias_ref, mixed_ref, lse_ref):
    stretch = bias_ref.shape[1]
    bias = jnp.concatenate([bias_ref[...]] * 2, axis=1)
    for g in range(KVH):
        keys = key_block(kv_ref, g * HD)
        values = jnp.concatenate(
            [kv_ref[n, KW + g * HD : KW + (g + 1) * HD, :] for n in range(kv_ref.shape[0])], axis=1
        )
        for h in range(g * GROUP, (g + 1) * GROUP, 2):
            scores = dot(keys, two(q_ref, h), 1, 0) * score_scale + bias
            top = jnp.max(scores, axis=0, keepdims=True)
            weights = jnp.exp(scores - top)
            amount = jnp.sum(weights, axis=0, keepdims=True)
            mixed = dot(values, weights.astype(BF), 1, 0) / amount
            lse = top + jnp.log(amount)
            for n in range(2):
                part = slice(n * stretch, (n + 1) * stretch)
                mixed_ref[h + n] = mixed[:, part]
                lse_ref[0, h + n : h + n + 1, :] = lse[:, part]


def backward_kernel(q_ref, kv_ref, bias_ref, mixed_ref, lse_ref, grad_ref, dq_ref, same_ref, other_ref):
    blocks, stretch = kv_ref.shape[0], kv_ref.shape[2]
    bias = jnp.concatenate([bias_ref[...]] * 2, axis=1)
    for g in range(KVH):
        keys, values = key_block(kv_ref, g * HD), key_block(kv_ref, KW + g * HD)
        keys_flat = jnp.concatenate(
            [kv_ref[n, g * HD : (g + 1) * HD, :] for n in range(blocks)], axis=1
        )
        key_grad = jnp.zeros(keys.shape, F32)
        value_grad = jnp.zeros(keys.shape, F32)
        for h in range(g * GROUP, (g + 1) * GROUP, 2):
            query, grad = two(q_ref, h), two(grad_ref, h)
            lse = jnp.concatenate([lse_ref[0, h : h + 1, :], lse_ref[0, h + 1 : h + 2, :]], axis=1)
            scores = dot(keys, query, 1, 0) * score_scale + bias
            probs = jnp.exp(scores - lse)
            delta = jnp.sum(two(mixed_ref, h) * grad.astype(F32), axis=0, keepdims=True)
            score_grad = (probs * (dot(values, grad, 1, 0) - delta)).astype(BF)
            query_grad = dot(keys_flat, score_grad, 1, 0) * score_scale
            for n in range(2):
                dq_ref[h + n] = query_grad[:, n * stretch : (n + 1) * stretch]
            key_grad += dot(score_grad, query, 1, 1)
            value_grad += dot(probs.astype(BF), grad, 1, 1)
        key_grad = (key_grad * score_scale).astype(BF)
        value_grad = value_grad.astype(BF)
        for n in range(blocks):
            part, ref = slice(n * stretch, (n + 1) * stretch), (same_ref, other_ref)[n % 2]
            ref[n // 2, :, g * HD : (g + 1) * HD] = key_grad[part]
            ref[n // 2, :, KW + g * HD : KW + (g + 1) * HD] = value_grad[part]


def attention_call(kernel, outs, out_specs, queries, pairs, bias, *more):
    blocks, _, tokens = pairs.shape
    stretch = bias.shape[1]
    head = pl.BlockSpec((H, HD, stretch), lambda s: (0, 0, s))
    row = pl.BlockSpec((1, H, stretch), lambda s: (s, 0, 0))
    specs = [
        head,
        pl.BlockSpec((blocks, 2 * KW, stretch), lambda s: (0, 0, s)),
        pl.BlockSpec(bias.shape, lambda s: (0, 0)),
        head,
        row,
        head,
    ]
    keys = blocks * stretch
    return pl.pallas_call(
        kernel,
        grid=(tokens // stretch,),
        in_specs=specs[: 3 + len(more)],
        out_specs=[head if s == "head" else row if s == "row" else s for s in out_specs],
        out_shape=outs,
        compiler_params=pltpu.CompilerParams(vmem_limit_bytes=56 * 1024 * 1024),
        cost_estimate=HINT,
    )(queries, pairs, bias, *more)


HALF = FF // 2
ROWS = D // 4
DOWN = FF // 4


def inner(weight_ref):
    return jnp.concatenate([weight_ref[a, :ROWS] for a in range(4)], axis=0)


def outer(first_ref, half=None):
    owners = range(4) if half is None else (2 * half, 2 * half + 1)
    return jnp.concatenate(
        [
            jnp.concatenate(
                [first_ref[a, ROWS : ROWS + DOWN], first_ref[a, ROWS + DOWN :]], axis=1
            )
            for a in owners
        ],
        axis=0,
    )


def gates_for(me_ref, gates):
    lanes = lax.broadcasted_iota(jnp.int32, gates.shape, 1)
    return jnp.sum(jnp.where(lanes == me_ref[0], gates, 0.0), axis=1, keepdims=True)


def first_kernel(me_ref, *refs):
    rows_in, grads_in = refs[:8], refs[8:16]
    bias_ref, first_ref, router_ref = refs[16:19]
    gates_out, gate_grad_out, gate_up_out, hidden_out, weight_out = refs[19:24]
    rows_v, grads_v, gate_up_v, hidden_v, weight_v, in_sems, out_sems = refs[24:]
    count = rows_in[0].shape[0]
    moves = []
    for k in range(8):
        t, part = k // 2, pl.ds((k % 2) * count, count)
        moves += [(rows_in[k], rows_v.at[t, part]), (grads_in[k], grads_v.at[t, part])]
    arriving = bring(moves, in_sems)
    weight, back = inner(first_ref), outer(first_ref, 0)
    leaving = []
    for t in range(4):
        part = slice(t * 2 * count, (t + 1) * 2 * count)
        for copy in arriving[4 * t : 4 * t + 4]:
            copy.wait()
        rows, grads = rows_v[t], grads_v[t]
        logits = dot(rows, router_ref[...], 1, 0) + bias_ref[part]
        exps = jnp.exp(logits - jnp.max(logits, axis=1, keepdims=True))
        gates = exps / jnp.sum(exps, axis=1, keepdims=True)
        gates_out[part] = gates
        mine = gates_for(me_ref, gates)
        gate_up = dot(rows, weight, 1, 0)
        hidden, slope_gate, slope_up = gated(gate_up[:, :HALF], gate_up[:, HALF:])
        hidden_grad = dot(grads, back, 1, 1)
        hidden = hidden.astype(BF).astype(F32)
        gate_grad = jnp.sum(hidden * hidden_grad, axis=1, keepdims=True)
        gate_grad_out[part] = jnp.broadcast_to(gate_grad, (2 * count, EXTRA))
        hidden_grad = hidden_grad * mine
        gate_up_v[t, :, :HALF] = (hidden_grad * slope_gate).astype(BF)
        gate_up_v[t, :, HALF:] = (hidden_grad * slope_up).astype(BF)
        hidden_v[t] = (mine * hidden).astype(BF)
        pairs = [(gate_up_v.at[t], gate_up_out.at[t]), (hidden_v.at[t], hidden_out.at[t])]
        leaving += bring(pairs, out_sems.at[pl.ds(2 * t, 2)])
    gate_up = gate_up_v[...].reshape(8 * count, 2 * HALF)
    for a in range(4):
        rows = rows_v[:, :, a * ROWS : (a + 1) * ROWS].reshape(8 * count, ROWS)
        weight_v[a] = dot(rows, gate_up, 0, 0).astype(BF)
        leaving += bring([(weight_v.at[a], weight_out.at[a])], out_sems.at[pl.ds(8 + a, 1)])
    for copy in leaving:
        copy.wait()


def first_call(me, rows, grads, bias, first, router):
    count, width = rows[0].shape
    shape = jax.ShapeDtypeStruct
    vmem, anywhere = pl.BlockSpec(memory_space=pltpu.VMEM), pl.BlockSpec(memory_space=pl.ANY)
    return pl.pallas_call(
        first_kernel,
        in_specs=[pl.BlockSpec(memory_space=pltpu.SMEM)] + [anywhere] * 16 + [vmem] * 3,
        out_specs=[vmem] * 2 + [anywhere] * 3,
        out_shape=[shape((8 * count, EXTRA), F32)] * 2
        + [
            shape((4, 2 * count, 2 * HALF), BF),
            shape((4, 2 * count, HALF), BF),
            shape((4, ROWS, 2 * HALF), BF),
        ],
        scratch_shapes=[
            pltpu.VMEM((4, 2 * count, width), BF),
            pltpu.VMEM((4, 2 * count, width), BF),
            pltpu.VMEM((4, 2 * count, 2 * HALF), BF),
            pltpu.VMEM((4, 2 * count, HALF), BF),
            pltpu.VMEM((4, ROWS, 2 * HALF), BF),
            pltpu.SemaphoreType.DMA((16,)),
            pltpu.SemaphoreType.DMA((12,)),
        ],
        compiler_params=pltpu.CompilerParams(vmem_limit_bytes=VMEM_BYTES),
        cost_estimate=HINT,
    )(me, *rows, *grads, bias, first, router)


def second_kernel(t, me_ref, *refs):
    row0, row1, grad0, grad1, gates_in, gate_grad_in, up_in, hidden_in, first, second = refs[:10]
    outs = refs[10:16]
    rows_v, grads_v, gates_v, gate_grad_v, up_v, hidden_v, inner0_v, inner1_v, outer_v = refs[16:25]
    out_v, result_v, up_out, hidden_out, sems, out_sems = refs[25:]
    count = row0.shape[0]
    low, high, part = pl.ds(0, count), pl.ds(count, count), pl.ds(t * 2 * count, 2 * count)
    moves = [
        (row0, rows_v.at[low]),
        (row1, rows_v.at[high]),
        (second, inner1_v),
        (grad0, grads_v.at[low]),
        (grad1, grads_v.at[high]),
        (first.at[:, pl.ds(ROWS, 2 * DOWN)], outer_v),
        (gates_in.at[part], gates_v),
        (gate_grad_in.at[part], gate_grad_v),
        (up_in.at[t], up_v),
        (first.at[:, pl.ds(0, ROWS)], inner0_v),
        (hidden_in.at[t], hidden_v),
    ]
    arriving = bring(moves, sems)
    for copy in arriving[:3]:
        copy.wait()
    inner1 = inner1_v[...].reshape(D, 2 * HALF)
    gate_up = dot(rows_v[...], inner1, 1, 0)
    for copy in arriving[3:6]:
        copy.wait()
    outer0, outer1 = [
        jnp.concatenate(
            [jnp.concatenate([outer_v[a, :DOWN], outer_v[a, DOWN:]], axis=1) for a in owners], axis=0
        )
        for owners in ((0, 1), (2, 3))
    ]
    hidden_grad = dot(grads_v[...], outer1, 1, 1)
    for copy in arriving[6:]:
        copy.wait()
    copies = dot(up_v[...], inner0_v[...].reshape(D, 2 * HALF), 1, 1)
    result = dot(hidden_v[...], outer0, 1, 0)
    hidden, slope_gate, slope_up = gated(gate_up[:, :HALF], gate_up[:, HALF:])
    mine = gates_for(me_ref, gates_v[...])
    hidden = hidden.astype(BF).astype(F32)
    gate_grad = gate_grad_v[...] + jnp.sum(hidden * hidden_grad, axis=1, keepdims=True)
    hidden_grad = hidden_grad * mine
    up_out[:, :HALF] = (hidden_grad * slope_gate).astype(BF)
    up_out[:, HALF:] = (hidden_grad * slope_up).astype(BF)
    hidden_out[...] = (mine * hidden).astype(BF)
    leaving = bring([(up_out, outs[4]), (hidden_out, outs[5])], out_sems.at[pl.ds(0, 2)])
    copies = (copies + dot(up_out[...], inner1, 1, 1)).astype(BF)
    lanes = lax.broadcasted_iota(jnp.int32, (2 * count, EXTRA), 1)
    rounded = gate_grad.astype(BF).astype(F32)
    columns = (
        jnp.where(lanes == me_ref[0], rounded, 0.0)
        + jnp.where(lanes == me_ref[0] + 8, gate_grad - rounded, 0.0)
    ).astype(BF)
    for n in range(2):
        out_v[n, :, :D] = copies[n * count : (n + 1) * count]
        out_v[n, :, D:] = columns[n * count : (n + 1) * count]
    leaving += bring(
        [(out_v.at[1], outs[1]), (out_v.at[0], outs[0])], out_sems.at[pl.ds(2, 2)]
    )
    result = (result + dot(hidden_out[...], outer1, 1, 0)).astype(BF)
    for n in range(2):
        result_v[n] = result[n * count : (n + 1) * count]
    leaving += bring(
        [(result_v.at[1], outs[3]), (result_v.at[0], outs[2])], out_sems.at[pl.ds(4, 2)]
    )
    for copy in leaving:
        copy.wait()


def second_call(t, me, rows, grads, gates, gate_grad, up_first, hidden_first, first, second):
    count, width = rows[0].shape
    shape = jax.ShapeDtypeStruct
    anywhere = pl.BlockSpec(memory_space=pl.ANY)
    return pl.pallas_call(
        lambda *refs: second_kernel(t, *refs),
        in_specs=[pl.BlockSpec(memory_space=pltpu.SMEM)] + [anywhere] * 10,
        out_specs=[pl.BlockSpec(memory_space=pltpu.HBM)] * 6,
        out_shape=[shape((count, D + EXTRA), BF)] * 2
        + [shape((count, D), BF)] * 2
        + [shape((2 * count, 2 * HALF), BF), shape((2 * count, HALF), BF)],
        scratch_shapes=[
            pltpu.VMEM((2 * count, width), BF),
            pltpu.VMEM((2 * count, width), BF),
            pltpu.VMEM((2 * count, EXTRA), F32),
            pltpu.VMEM((2 * count, EXTRA), F32),
            pltpu.VMEM((2 * count, 2 * HALF), BF),
            pltpu.VMEM((2 * count, HALF), BF),
            pltpu.VMEM((4, ROWS, 2 * HALF), BF),
            pltpu.VMEM((4, ROWS, 2 * HALF), BF),
            pltpu.VMEM((4, 2 * DOWN, 2 * HALF), BF),
            pltpu.VMEM((2, count, D + EXTRA), BF),
            pltpu.VMEM((2, count, D), BF),
            pltpu.VMEM((2 * count, 2 * HALF), BF),
            pltpu.VMEM((2 * count, HALF), BF),
            pltpu.SemaphoreType.DMA((11,)),
            pltpu.SemaphoreType.DMA((6,)),
        ],
        compiler_params=pltpu.CompilerParams(vmem_limit_bytes=VMEM_BYTES),
        cost_estimate=HINT,
    )(
        me,
        *rows[2 * t : 2 * t + 2],
        *grads[2 * t : 2 * t + 2],
        gates,
        gate_grad,
        up_first,
        hidden_first,
        first,
        second,
    )


def last_kernel(*refs):
    rows_in, grads_in, ups, hiddens = refs[:8], refs[8:16], refs[16:20], refs[20:24]
    hidden0, out_ref, rows_v, grads_v, up_v, hidden0_v, hidden1_v, out_v, in_sems, out_sems = refs[24:]
    count = rows_in[0].shape[0]
    arriving = bring(
        [(ref, grads_v.at[pl.ds(k * count, count)]) for k, ref in enumerate(grads_in)]
        + [(hidden0, hidden0_v)]
        + [(ref, hidden1_v.at[t]) for t, ref in enumerate(hiddens)]
        + [(ref, rows_v.at[pl.ds(k * count, count)]) for k, ref in enumerate(rows_in)]
        + [(ref, up_v.at[t]) for t, ref in enumerate(ups)],
        in_sems,
    )
    for copy in arriving[:9]:
        copy.wait()
    grads = grads_v[...]
    for half, ref in enumerate((hidden0_v, hidden1_v)):
        if half:
            for copy in arriving[9:13]:
                copy.wait()
        sums = dot(ref[...].reshape(8 * count, HALF), grads, 0, 0).astype(BF)
        for n in range(2):
            for side in range(2):
                out_v[2 * half + n, ROWS + side * DOWN : ROWS + (side + 1) * DOWN] = sums[
                    n * DOWN : (n + 1) * DOWN, side * 2 * HALF : (side + 1) * 2 * HALF
                ]
    for copy in arriving[13:]:
        copy.wait()
    leaving = []
    gate_up = up_v[...].reshape(8 * count, 2 * HALF)
    for a in range(4):
        out_v[a, :ROWS] = dot(rows_v[:, a * ROWS : (a + 1) * ROWS], gate_up, 0, 0).astype(BF)
        leaving += bring([(out_v.at[a], out_ref.at[a])], out_sems.at[pl.ds(a, 1)])
    for copy in leaving:
        copy.wait()


def last_call(rows, grads, ups, hiddens, hidden0):
    count, width = rows[0].shape
    anywhere = pl.BlockSpec(memory_space=pl.ANY)
    whole = (4, ROWS + 2 * DOWN, 2 * HALF)
    return pl.pallas_call(
        last_kernel,
        in_specs=[anywhere] * 25,
        out_specs=anywhere,
        out_shape=jax.ShapeDtypeStruct(whole, BF),
        scratch_shapes=[
            pltpu.VMEM((8 * count, width), BF),
            pltpu.VMEM((8 * count, width), BF),
            pltpu.VMEM((4, 2 * count, 2 * HALF), BF),
            pltpu.VMEM((4, 2 * count, HALF), BF),
            pltpu.VMEM((4, 2 * count, HALF), BF),
            pltpu.VMEM(whole, BF),
            pltpu.SemaphoreType.DMA((25,)),
            pltpu.SemaphoreType.DMA((4,)),
        ],
        compiler_params=pltpu.CompilerParams(vmem_limit_bytes=VMEM_BYTES),
        cost_estimate=HINT,
    )(*rows, *grads, *ups, *hiddens, hidden0)


def rms_factor(values):
    return lax.rsqrt(jnp.mean(values * values, axis=-1, keepdims=True) + norm_epsilon)


def rms_back(gradient, values, factor, gain):
    scaled = gradient * gain
    inner = jnp.mean(scaled * values, axis=-1, keepdims=True)
    return (
        factor * scaled - values * (factor * factor * factor * inner),
        jnp.sum(gradient * values * factor, axis=0),
    )


def turn(heads, cosine, sine):
    half = HD // 2
    first, second = heads[:, :half], heads[:, half:]
    return jnp.concatenate(
        [first * cosine - second * sine, second * cosine + first * sine], axis=1
    )


def adam_update(weight, moment, square, gradient, step_rate, shrink):
    moment_new = beta_first * moment + (1.0 - beta_first) * gradient
    square_new = beta_second * square + (1.0 - beta_second) * gradient * gradient
    normalized = (
        moment_new
        / (1.0 - beta_first**STEP)
        / (jnp.sqrt(square_new / (1.0 - beta_second**STEP)) + adam_epsilon)
    )
    return (moment_new, square_new, weight - step_rate * (normalized + shrink * weight))


def assemble(me_ref, refs, weight_v, whole_ref, sems, out_sem):
    rows = refs[0].shape[1]
    moves = []
    for k in range(8):
        for a in range(4):
            if k < 6:
                source = refs[k].at[a]
            else:
                source = refs[2 * k - 6 + a // 2].at[a % 2]
            start = pl.multiple_of((a * 8 + (me_ref[0] ^ k)) * rows, 16)
            moves.append((source, weight_v.at[pl.ds(start, rows)]))
    for copy in bring(moves, sems):
        copy.wait()
    return bring([(weight_v, whole_ref)], out_sem)[0]


def project_kernel(me_ref, *refs):
    blocks, (inputs_ref, cosine_ref, sine_ref, routes_ref) = refs[:10], refs[10:14]
    query_ref, pair_ref, normed_ref, factor_ref, gains_ref, router_ref, whole_ref = refs[14:21]
    weight_v, sems, out_sem = refs[21:]
    leaving = assemble(me_ref, blocks, weight_v, whole_ref, sems, out_sem)
    extras = weight_v[:, QKV:]
    lanes = lax.broadcasted_iota(jnp.int32, extras.shape, 1)
    router_ref[...] = jnp.where(lanes < 8, extras.astype(F32), 0.0).astype(BF)
    gains = extras.astype(F32).T[8:16]
    gains_ref[...] = gains
    tokens = inputs_ref[...].astype(F32)
    factor = rms_factor(tokens)
    factor_ref[...] = factor
    normed = (tokens * factor * gains[:1]).astype(BF)
    normed_ref[...] = normed
    projected = dot(normed, weight_v[:, :QKV], 1, 0)
    half = HD // 2
    cosine, sine = cosine_ref[...], sine_ref[...]
    for h in range(H + KVH):
        head = projected[:, h * HD : (h + 1) * HD].T
        first, second = head[:half], head[half:]
        head = jnp.concatenate(
            [first * cosine - second * sine, second * cosine + first * sine], axis=0
        ).astype(BF)
        if h < H:
            query_ref[h] = head
        else:
            pair_ref[(h - H) * HD : (h - H + 1) * HD] = head
    for h in range(KVH):
        start = QW + KW + h * HD
        pair_ref[KW + h * HD : KW + (h + 1) * HD] = projected[:, start : start + HD].T.astype(BF)
    pair_ref[2 * KW :] = routes_ref[...]
    leaving.wait()


def attended_kernel(me_ref, *refs):
    blocks, (mixed_ref, inputs_ref, gains_ref) = refs[:10], refs[10:13]
    hidden_ref, normed_ref, factor_ref, rows_ref, whole_ref, weight_v, sems, out_sem = refs[13:]
    leaving = assemble(me_ref, blocks, weight_v, whole_ref, sems, out_sem)
    rows_ref[...] = mixed_ref[...].reshape(rows_ref.shape).astype(BF)
    hidden = inputs_ref[...].astype(F32) + dot(rows_ref[...], weight_v[...], 0, 0)
    factor = rms_factor(hidden)
    hidden_ref[...] = hidden
    factor_ref[...] = factor
    normed_ref[...] = (hidden * factor * gains_ref[1:2]).astype(BF)
    leaving.wait()


def assembled_call(kernel, out_shape, whole_shape, me, blocks, *operands):
    vmem, anywhere = pl.BlockSpec(memory_space=pltpu.VMEM), pl.BlockSpec(memory_space=pl.ANY)
    return glue_call(
        kernel,
        [*out_shape, jax.ShapeDtypeStruct(whole_shape, BF)],
        me,
        *blocks,
        *operands,
        in_specs=[pl.BlockSpec(memory_space=pltpu.SMEM)]
        + [anywhere] * len(blocks)
        + [vmem] * len(operands),
        out_specs=[vmem] * len(out_shape) + [anywhere],
        scratch_shapes=[
            pltpu.VMEM(whole_shape, BF),
            pltpu.SemaphoreType.DMA((32,)),
            pltpu.SemaphoreType.DMA((1,)),
        ],
    )


def token_kernel(
    own_ref,
    core_ref,
    last_x_ref,
    last_y_ref,
    gates_ref,
    router_ref,
    hidden_ref,
    factor_ref,
    gain_ref,
    grad_ref,
    normed_ref,
    weight_ref,
    hidden_grad_ref,
    branch_ref,
    mixed_grad_ref,
    extras_ref,
):
    copies = sum(ref[...].astype(F32) for ref in (own_ref, core_ref, last_x_ref, last_y_ref))
    columns, gates = copies[:, D:], gates_ref[: copies.shape[0]]
    gate_grad = columns + pltpu.roll(columns, EXTRA - 8, 1)
    inner_sum = jnp.sum(gates * gate_grad, axis=1, keepdims=True)
    logit_grad = (gates * (gate_grad - inner_sum)).astype(BF)
    gradient = copies[:, :D] + dot(logit_grad, router_ref[...], 1, 1)
    hidden, factor = hidden_ref[...], factor_ref[...]
    scaled = gradient * gain_ref[1:2]
    inner_mean = jnp.mean(scaled * hidden, axis=-1, keepdims=True)
    part = factor * scaled - hidden * (factor * factor * factor * inner_mean)
    hidden_grad = grad_ref[...].astype(F32) + part
    hidden_grad_ref[...] = hidden_grad
    branch = hidden_grad.astype(BF)
    branch_ref[...] = branch
    mixed_grad_ref[...] = dot(weight_ref[...], branch, 1, 1).astype(BF)
    gain_grad = jnp.sum(gradient * hidden * factor, axis=0, keepdims=True)
    router_grad = dot(logit_grad, normed_ref[...], 0, 0)
    row = lax.broadcasted_iota(jnp.int32, router_grad.shape, 0)
    extras_ref[...] = jnp.where(row == 8, gain_grad, router_grad)


def put_cut(me_ref, scratch, same_ref, other_ref):
    core, chip = lax.rem(me_ref[0], 2), lax.div(me_ref[0], 2)
    rows = same_ref.shape[2]
    for n in range(4):
        for side, ref in enumerate((same_ref, other_ref)):
            device = 2 * (chip ^ n) + (core ^ side)
            for a in range(4):
                start = pl.multiple_of((a * 8 + device) * rows, 16)
                ref[n, a] = scratch[pl.ds(start, rows), :]


def cut_shapes(rows, width):
    return [jax.ShapeDtypeStruct((4, 4, rows, width), BF)] * 2


def output_kernel(me_ref, mixed_ref, branch_ref, extras_ref, same_ref, other_ref, scratch):
    scratch[:, :D] = dot(mixed_ref[...], branch_ref[...], 1, 0).astype(BF)
    scratch[:, D:] = extras_ref[...].T.astype(BF)
    put_cut(me_ref, scratch, same_ref, other_ref)


def turned_back(value, cosine, sine):
    half = HD // 2
    first, second = value[:half], value[half:]
    return jnp.concatenate(
        [first * cosine + second * sine, second * cosine - first * sine], axis=0
    )


def query_kernel(
    me_ref, query_ref, cosine_ref, sine_ref, normed_ref, part_ref, same_ref, other_ref, scratch
):
    for h in range(H):
        part = turned_back(query_ref[h], cosine_ref[...], sine_ref[...])
        part_ref[h * HD : (h + 1) * HD] = part.astype(BF)
    scratch[...] = dot(normed_ref[...], part_ref[...], 0, 1).astype(BF)
    put_cut(me_ref, scratch, same_ref, other_ref)


def late_kernel(
    me_ref,
    own_ref,
    last_x_ref,
    last_y_ref,
    cosine_ref,
    sine_ref,
    normed_ref,
    part_ref,
    same_ref,
    other_ref,
    scratch,
):
    value = sum(ref[...].astype(F32) for ref in (own_ref, last_x_ref, last_y_ref)).T
    for h in range(KVH):
        part = turned_back(value[h * HD : (h + 1) * HD], cosine_ref[...], sine_ref[...])
        part_ref[h * HD : (h + 1) * HD] = part.astype(BF)
    part_ref[KW:] = value[KW:].astype(BF)
    scratch[...] = dot(normed_ref[...], part_ref[...], 0, 1).astype(BF)
    put_cut(me_ref, scratch, same_ref, other_ref)


def sums_kernel(same_ref, arrived_ref, own_ref, by_x_ref, by_y_ref, low_ref, high_ref):
    for n, ref in enumerate((own_ref, by_x_ref, by_y_ref)):
        ref[...] = total(same_ref[n], arrived_ref[n])
    for half, ref in enumerate((low_ref, high_ref)):

        @pl.when(pl.program_id(0) == half)
        def _():
            ref[...] = total(same_ref[3], arrived_ref[3])


def sums_call(same, arrived):
    _, parts, rows, width = same.shape
    half = parts // 2
    both = pl.BlockSpec((4, half, rows, width), lambda i: (0, i, 0, 0))
    one = pl.BlockSpec((half, rows, width), lambda i: (i, 0, 0))
    fixed = pl.BlockSpec((half, rows, width), lambda i: (0, 0, 0))
    shape = jax.ShapeDtypeStruct
    return glue_call(
        sums_kernel,
        [shape((parts, rows, width), BF)] * 3 + [shape((half, rows, width), BF)] * 2,
        same,
        arrived,
        grid=(2,),
        in_specs=[both] * 2,
        out_specs=[one] * 3 + [fixed] * 2,
    )


def over_hops(sums):
    return hop(sums[3], 2), hop(sums[4], 4)


def join_kernel(by_x_ref, by_y_ref, over_x_ref, over_y_ref, new_x_ref, new_y_ref):
    new_y_ref[...] = total(by_y_ref[...], over_x_ref[...])
    new_x_ref[...] = total(by_x_ref[...], over_y_ref[...])


def join_call(sums, over):
    by_x, by_y = sums[1:3]
    half = (by_x.shape[0] // 2, *by_x.shape[1:])
    low = pl.BlockSpec(half, lambda i: (0, 0, 0))
    high = pl.BlockSpec(half, lambda i: (1, 0, 0))
    return glue_call(
        join_kernel,
        [jax.ShapeDtypeStruct(by_x.shape, BF)] * 2,
        by_x,
        by_y,
        *over,
        grid=(1,),
        in_specs=[high, low, low, low],
        out_specs=[high, low],
        input_output_aliases={0: 0, 1: 1},
    )


def both_kernel(x0_ref, x1_ref, y0_ref, y1_ref, over_x_ref, over_y_ref, new_x_ref, new_y_ref):
    half = over_x_ref.shape[0]
    by_x = x0_ref[...].astype(F32) + x1_ref[...].astype(F32)
    by_y = y0_ref[...].astype(F32) + y1_ref[...].astype(F32)
    new_x_ref[:half] = by_x[:half].astype(BF)
    new_x_ref[half:] = (by_x[half:] + over_y_ref[...].astype(F32)).astype(BF)
    new_y_ref[:half] = (by_y[:half] + over_x_ref[...].astype(F32)).astype(BF)
    new_y_ref[half:] = by_y[half:].astype(BF)


def both_call(by_x, x_core, by_y, y_core, over):
    return glue_call(
        both_kernel,
        [jax.ShapeDtypeStruct(by_x.shape, BF)] * 2,
        by_x,
        x_core,
        by_y,
        y_core,
        *over,
        scalars=0,
    )


def send_kernel(place_ref, *refs):
    groups, outs = (len(refs) - 4) // 3, refs[-4:]
    start = 0
    for g in range(groups):
        own_ref, last_x_ref, last_y_ref = refs[3 * g : 3 * g + 3]
        size = own_ref.shape[2]
        for step, out in enumerate(outs):
            at = lax.rem(place_ref[0] + step, 4)
            value = sum(ref[at].astype(F32) for ref in (own_ref, last_x_ref, last_y_ref))
            out[:, start : start + size] = value.astype(out.dtype)
        start += size


def send_call(*groups):
    rows, width = groups[0][0].shape[1], sum(group[0].shape[2] for group in groups)
    shape = jax.ShapeDtypeStruct
    own, *sent = glue_call(
        send_kernel,
        [shape((rows, width), F32)] + [shape((rows, width), BF)] * 3,
        lax.axis_index("dp")[None],
        *[part for group in groups for part in group],
    )
    return own, [
        lax.ppermute(value, "dp", [(i, (i + step) % 4) for i in range(4)])
        for step, value in enumerate(sent, 1)
    ]


def adam_kernel(pieces, step_rate, shrink, weight_ref, moment_ref, square_ref, *refs):
    grads, outs = refs[: len(pieces)], refs[len(pieces) :]
    for ref, (_, _, parts) in zip(grads, pieces):
        for source, target, size in parts:
            columns = slice(target, target + size)
            news = adam_update(
                weight_ref[:, columns],
                moment_ref[:, columns],
                square_ref[:, columns],
                ref[:, source : source + size].astype(F32),
                step_rate,
                shrink,
            )
            for out, new in zip(outs, news):
                out[:, columns] = new


def adam_call(weight, moment, square, pieces, step_rate, shrink, rows):
    width = weight.shape[2]
    state = pl.BlockSpec((None, rows, width), lambda i: (0, i, 0))
    return pl.pallas_call(
        lambda *refs: adam_kernel(pieces, step_rate, shrink, *refs),
        grid=(weight.shape[1] // rows,),
        in_specs=[state] * 3
        + [
            pl.BlockSpec((rows, piece.shape[1]), lambda i, first=first: (first + i, 0))
            for piece, first, _ in pieces
        ],
        out_specs=[state] * 3,
        out_shape=[jax.ShapeDtypeStruct(weight.shape, F32)] * 3,
        compiler_params=pltpu.CompilerParams(vmem_limit_bytes=VMEM_BYTES),
        cost_estimate=HINT,
    )(weight, moment, square, *[piece for piece, _, _ in pieces])


def owned_kernel(step_rate, weight_ref, moment_ref, square_ref, own_ref, *refs):
    arrived, outs, rest = refs[:3], refs[3:6], refs[6]
    total_grad = own_ref[...] + sum(ref[...].astype(F32) for ref in arrived)
    size = weight_ref.shape[1]
    weight, gradient = weight_ref[...], total_grad[:, :size]
    news = adam_update(
        weight, moment_ref[...], square_ref[...], gradient, step_rate, weight_decay
    )
    for out, new in zip(outs, news):
        out[...] = new
    if total_grad.shape[1] > size:
        rest[...] = total_grad[:, size:]
    else:
        products = jnp.sum(weight.astype(BF).astype(F32) * gradient, axis=1, keepdims=True)
        rest[...] = jnp.broadcast_to(products, rest.shape)


def owned_call(weight, moment, square, sums, step_rate):
    vmem = pl.BlockSpec(memory_space=pltpu.VMEM)
    state = jax.ShapeDtypeStruct(weight.shape, F32)
    return pl.pallas_call(
        lambda *refs: owned_kernel(step_rate, *refs),
        in_specs=[vmem] * 7,
        out_specs=[vmem] * 4,
        out_shape=[state] * 3 + [jax.ShapeDtypeStruct((weight.shape[0], EXTRA), F32)],
        compiler_params=pltpu.CompilerParams(vmem_limit_bytes=VMEM_BYTES),
        cost_estimate=HINT,
    )(weight, moment, square, *sums)


def input_kernel(query_ref, late_ref, weight_ref, tokens_ref, factor_ref, gain_ref, grad_ref, out_ref):
    gradient = dot(query_ref[...], weight_ref[:, :QW], 0, 1)
    gradient = gradient + dot(late_ref[...], weight_ref[:, QW:QKV], 0, 1)
    tokens, factor = tokens_ref[...].astype(F32), factor_ref[...]
    scaled = gradient * gain_ref[:1]
    inner_mean = jnp.mean(scaled * tokens, axis=-1, keepdims=True)
    part = factor * scaled - tokens * (factor * factor * factor * inner_mean)
    out_ref[...] = grad_ref[...] + part


def input_call(*operands):
    vmem = pl.BlockSpec(memory_space=pltpu.VMEM)
    return pl.pallas_call(
        input_kernel,
        in_specs=[vmem] * 7,
        out_specs=vmem,
        out_shape=jax.ShapeDtypeStruct(operands[-1].shape, F32),
        compiler_params=pltpu.CompilerParams(vmem_limit_bytes=VMEM_BYTES),
        cost_estimate=HINT,
    )(*operands)


def gated(gate, up):
    rate = (2.0 / jnp.pi) ** 0.5
    bend = 0.044715 * rate
    square = gate * gate
    part = 0.5 + 0.5 * jnp.tanh(gate * (rate + bend * square))
    gelu = gate * part
    slope = part + gelu * (1.0 - part) * (2.0 * rate + 6.0 * bend * square)
    return gelu * up, slope * up, gelu


def local(
    inputs,
    cotangent,
    routes,
    project_weight,
    project_moment,
    project_square,
    output_weight,
    output_moment,
    output_square,
    router_weight,
    router_moment,
    router_square,
    norm_gains,
    gains_moment,
    gains_square,
    expert_in,
    expert_in_moment,
    expert_in_square,
    expert_down,
    expert_down_moment,
    expert_down_square,
):
    seq_count, stretch, width = inputs.shape
    device_count = lax.axis_size("expert")
    expert_count = device_count
    rows = seq_count * stretch
    me = lax.axis_index("expert")
    others = me ^ jnp.arange(device_count, dtype=jnp.int32)
    shard = project_weight.shape[0]

    first_payload = jnp.concatenate(
        [
            project_weight.astype(BF),
            router_weight.astype(BF),
            norm_gains.T.astype(BF),
            jnp.zeros((shard, EXTRA - expert_count - 2), BF),
        ],
        axis=1,
    )
    first_hops = [first_payload] + [plane_hop(first_payload, step) for step in (1, 2, 3)]
    own_grad = cotangent.reshape(rows, width)
    grad_near = gather_near(own_grad)
    in_low, down_low = expert_in[0].astype(BF), expert_down[0].astype(BF)
    share_first, share_second = [
        jnp.concatenate([in_low[:, p * HALF : (p + 1) * HALF] for p in (h, h + 2)], axis=1)
        for h in range(2)
    ]
    share_first = jnp.concatenate(
        [share_first, down_low[:, : 2 * HALF], down_low[:, 2 * HALF :]], axis=0
    )
    first_hops, grad_near, inputs, routes, output_low, place = phase(
        first_hops, grad_near, inputs, routes, output_weight, me
    )

    first_plane = plane_end(first_hops)
    first_near = gather_near(first_plane)
    output_low = output_low.astype(BF)
    output_hops = [output_low] + [plane_hop(output_low, step) for step in (1, 2, 3)]
    positions = place * stretch + jnp.arange(stretch, dtype=jnp.int32)
    frequency = rope_base ** (-jnp.arange(HD // 2, dtype=F32) / (HD // 2))
    angles = frequency[:, None] * positions.astype(F32)[None, :]
    cosine = jnp.tile(jnp.cos(angles), (1, seq_count))
    sine = jnp.tile(jnp.sin(angles), (1, seq_count))
    route_rows = jnp.concatenate(
        [routes.reshape(rows, TOP).T.astype(BF), jnp.zeros((32 - TOP, rows), BF)], axis=0
    )
    first_near, output_hops, share_first, share_second, cosine, sine, route_rows = phase(
        first_near, output_hops, share_first, share_second, cosine, sine, route_rows
    )

    weights_first = lax.all_gather(share_first, "dp")
    weights_second = lax.all_gather(share_second, "dp")
    first_over, first_cores = gather_over(first_near), gather_cores(first_near)
    first_sibling = hop(first_plane, 1)
    output_plane = plane_end(output_hops)
    first_over, first_cores, first_sibling, output_plane = phase(
        first_over, first_cores, first_sibling, output_plane
    )

    first_far = hop(first_over[0], 1), hop(first_over[1], 1)
    output_near, output_sibling = gather_near(output_plane), hop(output_plane, 1)
    first_far = phase(first_far)[0]

    inputs = inputs.reshape(rows, width)
    shape = jax.ShapeDtypeStruct
    queries, pair_payload, normed_one, factor_one, gains, router, full_first = assembled_call(
        project_kernel,
        [
            shape((H, HD, rows), BF),
            shape((2 * KW + 32, rows), BF),
            shape((rows, width), BF),
            shape((rows, 1), F32),
            shape((8, D), F32),
            shape((D, EXTRA), BF),
        ],
        (D, QKV + EXTRA),
        me[None],
        [
            first_plane,
            first_sibling,
            first_near[0],
            first_cores[0],
            first_near[1],
            first_cores[1],
            *first_over,
            *first_far,
        ],
        inputs,
        cosine,
        sine,
        route_rows,
    )
    pair_payload, output_near, output_sibling, queries = phase(
        pair_payload, output_near, output_sibling, queries
    )

    key_positions = (others[:, None] * stretch + jnp.arange(stretch)[None, :]).reshape(-1)
    bias = jnp.where(key_positions[:, None] <= positions[None, :], 0.0, masked_score).astype(F32)
    pair_near, pair_sibling = gather_near(pair_payload), hop(pair_payload, 1)
    output_over = gather_over(output_near)
    pair_near, pair_sibling, output_over, bias = phase(pair_near, pair_sibling, output_over, bias)

    pair_over, pair_cores = gather_over(pair_near), gather_cores(pair_near)
    output_core_x = hop(output_near[0], 1)
    pair_over, pair_cores, output_core_x = phase(pair_over, pair_cores, output_core_x)

    pair_diagonal = jnp.concatenate(pair_over, axis=0)
    pair_core, output_core_y = hop(pair_diagonal, 1), hop(output_near[1], 1)
    output_far = hop(output_over[0], 1), hop(output_over[1], 1)
    pair_core, output_core_y, output_far = phase(pair_core, output_core_y, output_far)

    pair_blocks = gathered(
        pair_payload, pair_sibling, pair_near, pair_cores, pair_diagonal, pair_core
    )
    pairs = jnp.stack(pair_blocks)
    lanes = jnp.arange(EXTRA, dtype=jnp.int32)[None, :]
    grad_over, grad_cores = gather_over(grad_near), gather_cores(grad_near)
    grad_sibling = hop(own_grad, 1)
    mixed, lse = attention_call(
        forward_kernel,
        [shape((H, HD, rows), F32), shape((seq_count, H, stretch), F32)],
        ["head", "row"],
        queries,
        pairs,
        bias,
    )
    mixed, lse, grad_over, grad_cores, grad_sibling = phase(
        mixed, lse, grad_over, grad_cores, grad_sibling
    )

    hidden_one, normed_two, factor_two, mixed_rows, full_output = assembled_call(
        attended_kernel,
        [
            shape((rows, width), F32),
            shape((rows, width), BF),
            shape((rows, 1), F32),
            shape((QW, rows), BF),
        ],
        (QW, D),
        me[None],
        [
            output_plane,
            output_sibling,
            output_near[0],
            output_core_x,
            output_near[1],
            output_core_y,
            *output_over,
            *output_far,
        ],
        mixed,
        inputs,
        gains,
    )

    row_near, row_sibling = gather_near(normed_two), hop(normed_two, 1)
    grad_diagonal = jnp.concatenate(grad_over, axis=0)
    grad_core = hop(grad_diagonal, 1)
    row_near, row_sibling, grad_core = phase(row_near, row_sibling, grad_core)
    grad_blocks = gathered(
        own_grad, grad_sibling, grad_near, grad_cores, grad_diagonal, grad_core
    )
    row_over, row_cores = gather_over(row_near), gather_cores(row_near)
    all_routes = jnp.concatenate(
        [block[2 * KW : 2 * KW + TOP].T for block in pair_blocks], axis=0
    ).astype(jnp.int32)
    named = jnp.any(all_routes[:, :, None] == lanes[None], axis=1)
    route_bias = jnp.where(named, 0.0, masked_score).astype(F32)
    row_over, row_cores, route_bias = phase(row_over, row_cores, route_bias)
    row_diagonal = jnp.concatenate(row_over, axis=0)
    row_core = phase(hop(row_diagonal, 1))[0]
    row_blocks = gathered(normed_two, row_sibling, row_near, row_cores, row_diagonal, row_core)
    gates, gate_grad_first, up_first, hidden_first, in_grad_first = first_call(
        me[None], row_blocks, grad_blocks, route_bias, weights_first, router
    )
    grads_first = lax.psum_scatter(in_grad_first, "dp")

    def second_part(t, *others):
        return second_call(
            t,
            me[None],
            row_blocks,
            grad_blocks,
            gates,
            gate_grad_first,
            after(up_first, *others),
            hidden_first,
            weights_first,
            weights_second,
        )

    far = second_part(3)
    far_cores = hop(far[1], 1), hop(far[3], 1)
    by_y = second_part(2, far[0])
    far_cores, _ = phase(far_cores, by_y[0])
    diagonal = total(far[0], far_cores[0])
    copy_over = reduce_over(diagonal)
    by_y_cores = hop(by_y[1], 1), hop(by_y[3], 1)
    result_diagonal = total(far[2], far_cores[1])
    by_x = second_part(1, diagonal, result_diagonal)
    copy_over, by_y_cores, _, result_diagonal = phase(
        copy_over, by_y_cores, by_x[0], result_diagonal
    )
    result_over, by_x_cores = reduce_over(result_diagonal), (hop(by_x[1], 1), hop(by_x[3], 1))
    own = second_part(0, by_x[0])
    result_over, by_x_cores, _ = phase(result_over, by_x_cores, own[0])
    copy_last = both_call(by_x[0], by_x_cores[0], by_y[0], by_y_cores[0], copy_over)
    last = last_hops(*copy_last)
    own_cores = hop(own[1], 1), hop(own[3], 1)
    result_last = both_call(
        by_x[2], after(by_x_cores[1], *copy_last), by_y[2], by_y_cores[1], result_over
    )
    parts = (own, by_x, by_y, far)
    weight_grads = last_call(
        row_blocks,
        grad_blocks,
        [part[4] for part in parts],
        [part[5] for part in parts],
        after(hidden_first, *result_last, grads_first),
    )
    last, own_cores, weight_grads, result_last = phase(last, own_cores, weight_grads, result_last)
    grads_second = lax.psum_scatter(weight_grads, "dp")
    result_hops = last_hops(*result_last)

    hidden_grad_one, branch_grad, mixed_grad, extras = glue_call(
        token_kernel,
        [
            jax.ShapeDtypeStruct((rows, width), F32),
            jax.ShapeDtypeStruct((rows, width), BF),
            jax.ShapeDtypeStruct((QW, rows), BF),
            jax.ShapeDtypeStruct((EXTRA, D), F32),
        ],
        own[0],
        own_cores[0],
        *last,
        gates,
        router,
        hidden_one,
        factor_two,
        gains,
        own_grad,
        normed_two,
        full_output,
        scalars=0,
    )
    mixed_grad = mixed_grad.reshape(H, HD, rows)
    mixed_grad, branch_grad, extras, hidden_grad_one = phase(
        mixed_grad, branch_grad, extras, hidden_grad_one
    )

    query_grad, pairs_same, pairs_other = attention_call(
        backward_kernel,
        [
            jax.ShapeDtypeStruct((H, HD, rows), F32),
            jax.ShapeDtypeStruct((4, rows, 2 * KW), BF),
            jax.ShapeDtypeStruct((4, rows, 2 * KW), BF),
        ],
        ["head"] + [pl.BlockSpec((4, stretch, 2 * KW), lambda s: (0, s, 0))] * 2,
        queries,
        pairs,
        bias,
        mixed,
        lse,
        mixed_grad,
    )
    query_grad, pairs_same, pairs_other, cosine, sine, result_hops = phase(
        query_grad, pairs_same, pairs_other, cosine, sine, result_hops
    )

    pair_cores = hop(pairs_other, 1)
    output_same, output_other = glue_call(
        output_kernel,
        cut_shapes(shard, D + EXTRA),
        me[None],
        mixed_rows,
        branch_grad,
        extras,
        scratch_shapes=[pltpu.VMEM((QW, D + EXTRA), BF)],
    )
    pair_cores, output_same, output_other = phase(pair_cores, output_same, output_other)

    quarters = (4, 4, rows // 4, 2 * KW)
    pair_sums = sums_call(pairs_same.reshape(quarters), pair_cores.reshape(quarters))
    pair_over, output_cores = over_hops(pair_sums), hop(output_other, 1)
    query_part, query_same, query_other = glue_call(
        query_kernel,
        [jax.ShapeDtypeStruct((QW, rows), BF)] + cut_shapes(shard, QW),
        me[None],
        after(query_grad, *pair_sums),
        cosine,
        sine,
        normed_one,
        scratch_shapes=[pltpu.VMEM((D, QW), BF)],
    )
    pair_over, pair_sums, query_same, query_other, query_part, output_cores = phase(
        pair_over, pair_sums, query_same, query_other, query_part, output_cores
    )

    pair_last = join_call(pair_sums, pair_over)
    pair_hops, query_cores = last_hops(*pair_last), hop(query_other, 1)
    output_sums = sums_call(output_same, after(output_cores, *pair_last))
    output_over = over_hops(output_sums)
    pair_hops, query_cores, output_sums, output_over = phase(
        pair_hops, query_cores, output_sums, output_over
    )

    late_part, late_same, late_other = glue_call(
        late_kernel,
        [jax.ShapeDtypeStruct((2 * KW, rows), BF)] + cut_shapes(shard, 2 * KW),
        me[None],
        *[value.reshape(rows, 2 * KW) for value in (pair_sums[0], *pair_hops)],
        cosine,
        sine,
        normed_one,
        scratch_shapes=[pltpu.VMEM((D, 2 * KW), BF)],
    )
    late_cores = hop(late_other, 1)
    output_last = join_call(output_sums, after(output_over, late_other))
    output_hops = last_hops(*output_last)
    query_sums = sums_call(query_same, after(query_cores, *output_last))
    query_over = over_hops(query_sums)
    output_hops, late_cores, late_same, late_part, query_sums, query_over = phase(
        output_hops, late_cores, late_same, late_part, query_sums, query_over
    )

    late_sums = sums_call(late_same, late_cores)
    late_over = over_hops(late_sums)
    query_last = join_call(query_sums, after(query_over, *late_sums))
    query_hops = last_hops(*query_last)
    input_grad = input_call(
        query_part,
        after(late_part, *query_last),
        full_first,
        inputs,
        factor_one,
        gains,
        hidden_grad_one,
    )
    late_over, query_hops, late_sums, input_grad = phase(
        late_over, query_hops, late_sums, input_grad
    )

    late_last = join_call(late_sums, late_over)
    late_hops = last_hops(*late_last)
    output_own, output_arrived = send_call(
        (output_sums[0], *after(output_hops, *late_last))
    )
    grads_first, grads_second = phase(grads_first, grads_second, output_own, late_last)[:2]
    in_new = adam_call(
        expert_in,
        expert_in_moment,
        expert_in_square,
        [
            (grads_first, 0, [(0, 0, HALF), (HALF, FF, HALF)]),
            (grads_second, 0, [(0, HALF, HALF), (HALF, FF + HALF, HALF)]),
        ],
        3.0 / D**0.5,
        weight_decay,
        ROWS // 4,
    )
    down_new = adam_call(
        expert_down,
        expert_down_moment,
        expert_down_square,
        [
            (grads_second, 4, [(0, 0, 2 * HALF)]),
            (grads_second, 6, [(0, 2 * HALF, 2 * HALF)]),
        ],
        12.0 / FF**0.5,
        weight_decay,
        ROWS // 4,
    )
    late_hops, output_arrived, output_own, in_new, down_new = phase(
        late_hops, output_arrived, output_own, in_new, down_new
    )

    project_own, project_arrived = send_call(
        (query_sums[0], *query_hops), (late_sums[0], *late_hops)
    )
    output_own = after(output_own, project_own)
    sequence = stretch * device_count
    *output_new, output_rest = owned_call(
        output_weight,
        output_moment,
        output_square,
        [output_own, *output_arrived],
        3.0 * (sequence / (32.0 * H * HD)) ** 0.5,
    )
    outputs = hidden_one + reduced(
        total(own[2], after(own_cores[1], output_rest)), result_hops
    )
    project_arrived, output_new, output_rest, outputs = phase(
        project_arrived, output_new, output_rest, outputs
    )
    *project_new, products = owned_call(
        project_weight,
        project_moment,
        project_square,
        [project_own, *project_arrived],
        3.0 * (2.0 / D) ** 0.5,
    )
    rest = output_rest.T
    router_new = [
        new.T
        for new in adam_update(
            router_weight.T,
            router_moment.T,
            router_square.T,
            rest[:expert_count],
            1.5 / D**0.5,
            weight_decay,
        )
    ]
    own_gains = norm_gains.astype(BF).astype(F32)
    gains_sum = jnp.stack([products[:, 0] / own_gains[0], rest[expert_count]])
    gains_new = adam_update(norm_gains, gains_moment, gains_square, gains_sum, 0.8, 0.0)
    return (
        outputs.reshape(seq_count, stretch, width),
        input_grad.reshape(seq_count, stretch, width),
        *project_new,
        *output_new,
        *router_new,
        *gains_new,
        *in_new,
        *down_new,
    )


def rms_norm(values, gain_row):
    factor = lax.rsqrt(jnp.mean(values * values, axis=-1, keepdims=True) + norm_epsilon)
    return values * factor * gain_row


def rotate(values, positions):
    half_width = values.shape[-1] // 2
    frequency = rope_base ** (-jnp.arange(half_width, dtype=jnp.float32) / half_width)
    angles = positions.astype(jnp.float32)[:, None] * frequency[None, :]
    cosine = jnp.cos(angles)[:, None, :]
    sine_part = jnp.sin(angles)[:, None, :]
    first_half = values[..., :half_width]
    second_half = values[..., half_width:]
    return jnp.concatenate(
        [
            first_half * cosine - second_half * sine_part,
            second_half * cosine + first_half * sine_part,
        ],
        axis=-1,
    )


def gated_unit(gate_up):
    return jax.nn.gelu(gate_up[..., :FF], approximate=True) * gate_up[..., FF:]


def slot_tables(route_block, expert_count, capacity):
    flat_routes = route_block.reshape(-1)
    pick_count = flat_routes.shape[0]
    onehot = (flat_routes[:, None] == jnp.arange(expert_count, dtype=jnp.int32)[None, :]).astype(
        jnp.int32
    )
    earlier = jnp.cumsum(onehot, axis=0) - onehot
    rank_values = jnp.sum(earlier * onehot, axis=1)
    slot_index = flat_routes * capacity + rank_values
    slot_table = (
        jnp.full((expert_count * capacity,), pick_count, jnp.int32)
        .at[slot_index]
        .set(jnp.arange(pick_count, dtype=jnp.int32))
    )
    return (slot_index, slot_table)


def attention_blocks(step_fn, carried, key_values, last_query):
    key_count = key_values.shape[1]
    block_keys = 512

    def one_turn(turn_index, state_now):
        offset = turn_index * block_keys
        key_block = lax.dynamic_slice_in_dim(key_values, offset, block_keys, 1)
        return lax.cond(
            offset > last_query,
            lambda held_state: held_state,
            lambda held_state: step_fn(held_state, key_block, offset),
            state_now,
        )

    return lax.fori_loop(0, key_count // block_keys, one_turn, carried)


def general(
    inputs,
    cotangent,
    routes,
    project_weight,
    project_moment,
    project_square,
    output_weight,
    output_moment,
    output_square,
    router_weight,
    router_moment,
    router_square,
    norm_gains,
    gains_moment,
    gains_square,
    expert_in,
    expert_in_moment,
    expert_in_square,
    expert_down,
    expert_down_moment,
    expert_down_square,
):
    seq_count, stretch_len, model_width = inputs.shape
    expert_devices = lax.axis_size("expert")
    seq_length = stretch_len * expert_devices
    expert_count = EXP_DEV * expert_devices
    row_count = seq_count * stretch_len
    capacity = 2 * row_count * TOP // expert_count
    group_size = H // KVH
    query_width = H * HD
    key_width = KVH * HD
    group_rows = group_size * stretch_len
    score_scale = HD ** (-0.5)
    first_query = lax.axis_index("expert") * stretch_len
    last_query = first_query + stretch_len - 1
    full_project, full_output, full_router, full_gains = (
        lax.all_gather(project_weight.astype(jnp.bfloat16), ("dp", "expert"), axis=0, tiled=True),
        lax.all_gather(output_weight.astype(jnp.bfloat16), ("dp", "expert"), axis=0, tiled=True),
        lax.all_gather(router_weight.astype(jnp.bfloat16), ("dp", "expert"), axis=0, tiled=True),
        lax.all_gather(norm_gains.astype(jnp.bfloat16), ("dp", "expert"), axis=1, tiled=True),
    )
    full_in, full_down = (
        lax.all_gather(expert_in.astype(jnp.bfloat16), "dp", axis=1, tiled=True),
        lax.all_gather(expert_down.astype(jnp.bfloat16), "dp", axis=1, tiled=True),
    )
    gain_values = full_gains.astype(jnp.float32)
    tokens = inputs.astype(jnp.float32).reshape(row_count, model_width)
    normed_one = rms_norm(tokens, gain_values[0]).astype(jnp.bfloat16)
    projected = jnp.dot(normed_one, full_project, preferred_element_type=jnp.float32).reshape(
        seq_count, stretch_len, -1
    )
    positions = first_query + jnp.arange(stretch_len, dtype=jnp.int32)

    def rope_back(gradient):
        unused, pullback = jax.vjp(
            lambda values: rotate(values, positions), jnp.zeros_like(gradient)
        )
        return pullback(gradient)[0]

    queries = rotate(
        projected[..., :query_width].reshape(seq_count, stretch_len, H, HD), positions
    ).astype(jnp.bfloat16)
    rotated_keys = rotate(
        projected[..., query_width : query_width + key_width].reshape(
            seq_count, stretch_len, KVH, HD
        ),
        positions,
    ).astype(jnp.bfloat16)
    values = projected[..., query_width + key_width :].astype(jnp.bfloat16)
    local_pairs = jnp.concatenate(
        [rotated_keys.reshape(seq_count, stretch_len, key_width), values], axis=-1
    )
    all_pairs = lax.all_gather(local_pairs, "expert", axis=1, tiled=True)

    def to_grid(token_rows):
        return (
            token_rows.reshape(seq_count, stretch_len, KVH, group_size, HD)
            .transpose(0, 2, 3, 1, 4)
            .reshape(seq_count, KVH, group_rows, HD)
        )

    def from_grid(grid_rows):
        return (
            grid_rows.reshape(seq_count, KVH, group_size, stretch_len, HD)
            .transpose(0, 3, 1, 2, 4)
            .reshape(row_count, query_width)
        )

    query_grid = to_grid(queries)
    row_positions = first_query + jnp.arange(group_rows, dtype=jnp.int32) % stretch_len

    def scores_for(sequence, key_block, offset):
        key_part = key_block[sequence, :, :key_width].reshape(-1, KVH, HD)
        raw_scores = (
            jnp.einsum(
                "krd,nkd->krn", query_grid[sequence], key_part, preferred_element_type=jnp.float32
            )
            * score_scale
        )
        key_positions = offset + jnp.arange(key_block.shape[1], dtype=jnp.int32)
        allowed = (key_positions[None, :] <= row_positions[:, None])[None]
        return (raw_scores, allowed)

    def stats_step(carried, key_block, offset):
        top_now, total_now = carried
        new_tops = []
        new_totals = []
        for sequence in range(seq_count):
            raw_scores, allowed = scores_for(sequence, key_block, offset)
            masked = jnp.where(allowed, raw_scores, masked_score)
            top_new = jnp.maximum(top_now[sequence], jnp.max(masked, axis=-1))
            weights = jnp.where(allowed, jnp.exp(masked - top_new[..., None]), 0.0)
            new_totals.append(
                total_now[sequence] * jnp.exp(top_now[sequence] - top_new)
                + jnp.sum(weights, axis=-1)
            )
            new_tops.append(top_new)
        return (jnp.stack(new_tops), jnp.stack(new_totals))

    stats_shape = (seq_count, KVH, group_rows)
    top_all, total_all = attention_blocks(
        stats_step,
        (jnp.full(stats_shape, masked_score, jnp.float32), jnp.zeros(stats_shape, jnp.float32)),
        all_pairs,
        last_query,
    )
    log_total = top_all + jnp.log(total_all)

    def softmax_for(sequence, key_block, offset):
        raw_scores, allowed = scores_for(sequence, key_block, offset)
        return jnp.where(
            allowed,
            jnp.exp(jnp.where(allowed, raw_scores, masked_score) - log_total[sequence][..., None]),
            0.0,
        )

    def mix_step(carried, key_block, offset):
        new_rows = []
        for sequence in range(seq_count):
            softmax_rows = softmax_for(sequence, key_block, offset).astype(jnp.bfloat16)
            value_part = key_block[sequence, :, key_width:].reshape(-1, KVH, HD)
            new_rows.append(
                carried[sequence]
                + jnp.einsum(
                    "krn,nkd->krd", softmax_rows, value_part, preferred_element_type=jnp.float32
                )
            )
        return jnp.stack(new_rows)

    mixed_grid = attention_blocks(
        mix_step, jnp.zeros((seq_count, KVH, group_rows, HD), jnp.float32), all_pairs, last_query
    )
    mixed_rows = from_grid(mixed_grid).astype(jnp.bfloat16)
    hidden_one = tokens + jnp.dot(mixed_rows, full_output, preferred_element_type=jnp.float32)
    normed_two = rms_norm(hidden_one, gain_values[1]).astype(jnp.bfloat16)
    logits = jnp.dot(normed_two, full_router, preferred_element_type=jnp.float32)
    route_rows = routes.reshape(row_count, TOP)
    onehot = (
        route_rows[:, :, None] == jnp.arange(expert_count, dtype=jnp.int32)[None, None, :]
    ).astype(jnp.float32)
    gate_weights = jax.nn.softmax(
        jnp.einsum("rte,re->rt", onehot, logits, precision=lax.Precision.HIGHEST), axis=-1
    )
    slot_index, slot_table = slot_tables(route_rows, expert_count, capacity)
    padded = jnp.concatenate([normed_two, jnp.zeros((1, model_width), jnp.bfloat16)], axis=0)
    sent_rows = padded[slot_table // TOP].reshape(expert_count, capacity, model_width)
    arrived_rows = lax.all_to_all(sent_rows, "expert", split_axis=0, concat_axis=0, tiled=True)
    batched = arrived_rows.reshape(expert_devices, EXP_DEV, -1, model_width)
    gate_up = jnp.einsum("neid,edf->neif", batched, full_in, preferred_element_type=jnp.float32)
    hidden = gated_unit(gate_up).astype(jnp.bfloat16)
    result = jnp.einsum(
        "neif,efd->neid", hidden, full_down, preferred_element_type=jnp.float32
    ).astype(jnp.bfloat16)
    results = result.reshape(arrived_rows.shape)
    kept_gate_up = gate_up.reshape(arrived_rows.shape[0], arrived_rows.shape[1], 2 * FF)
    returned = lax.all_to_all(results, "expert", split_axis=0, concat_axis=0, tiled=True)
    picked = returned.reshape(expert_count * capacity, model_width)[slot_index].reshape(
        row_count, TOP, model_width
    )
    picked_wide = picked.astype(jnp.float32)
    mixture = jnp.sum(gate_weights[:, :, None] * picked_wide, axis=1)
    outputs = hidden_one + mixture
    grad_rows = cotangent.astype(jnp.float32).reshape(row_count, model_width)
    gate_grad = jnp.sum(grad_rows[:, None, :] * picked_wide, axis=-1)
    chosen_grad = gate_weights * (
        gate_grad - jnp.sum(gate_weights * gate_grad, axis=-1, keepdims=True)
    )
    logit_grad = jnp.einsum(
        "rte,rt->re", onehot, chosen_grad, precision=lax.Precision.HIGHEST
    ).astype(jnp.bfloat16)
    copy_out_grad = (
        (gate_weights[:, :, None] * grad_rows[:, None, :])
        .astype(jnp.bfloat16)
        .reshape(row_count * TOP, model_width)
    )
    grad_sent = jnp.concatenate([copy_out_grad, jnp.zeros((1, model_width), jnp.bfloat16)], axis=0)[
        slot_table
    ].reshape(expert_count, capacity, model_width)
    grad_arrived = lax.all_to_all(grad_sent, "expert", split_axis=0, concat_axis=0, tiled=True)
    batched_grad = grad_arrived.reshape(expert_devices, EXP_DEV, -1, model_width)
    batched_in = arrived_rows.reshape(expert_devices, EXP_DEV, -1, model_width)
    gate_up = kept_gate_up.reshape(expert_devices, EXP_DEV, -1, 2 * FF)
    hidden, unit_pull = jax.vjp(gated_unit, gate_up)
    grad_down = jnp.einsum(
        "neif,neid->efd",
        hidden.astype(jnp.bfloat16),
        batched_grad,
        preferred_element_type=jnp.float32,
    )
    hidden_grad = jnp.einsum(
        "neid,efd->neif", batched_grad, full_down, preferred_element_type=jnp.float32
    )
    gate_up_grad = unit_pull(hidden_grad)[0].astype(jnp.bfloat16)
    grad_in = jnp.einsum(
        "neid,neif->edf", batched_in, gate_up_grad, preferred_element_type=jnp.float32
    )
    copy_in_grad = (
        jnp.einsum("neif,edf->neid", gate_up_grad, full_in, preferred_element_type=jnp.float32)
        .astype(jnp.bfloat16)
        .reshape(arrived_rows.shape)
    )
    expert_in_grad, expert_down_grad = (
        lax.psum_scatter(
            grad_in.astype(jnp.bfloat16), "dp", scatter_dimension=1, tiled=True
        ).astype(jnp.float32),
        lax.psum_scatter(
            grad_down.astype(jnp.bfloat16), "dp", scatter_dimension=1, tiled=True
        ).astype(jnp.float32),
    )
    returned_grad = lax.all_to_all(copy_in_grad, "expert", split_axis=0, concat_axis=0, tiled=True)
    copies_grad = returned_grad.reshape(expert_count * capacity, model_width)[slot_index].reshape(
        row_count, TOP, model_width
    )
    normed_two_grad = jnp.sum(copies_grad.astype(jnp.float32), axis=1) + jnp.dot(
        logit_grad, full_router.T, preferred_element_type=jnp.float32
    )
    router_grad_full = jnp.einsum(
        "rd,re->de", normed_two, logit_grad, preferred_element_type=jnp.float32
    )
    unused_two, norm_two_pull = jax.vjp(rms_norm, hidden_one, gain_values[1])
    hidden_part, gain_two_grad = norm_two_pull(normed_two_grad)
    hidden_grad_one = grad_rows + hidden_part
    branch_grad = hidden_grad_one.astype(jnp.bfloat16)
    output_grad_full = jnp.einsum(
        "rh,rd->hd", mixed_rows, branch_grad, preferred_element_type=jnp.float32
    )
    mixed_grad = jnp.dot(branch_grad, full_output.T, preferred_element_type=jnp.float32).astype(
        jnp.bfloat16
    )
    mixed_grad_grid = to_grid(mixed_grad.reshape(seq_count, stretch_len, H, HD))
    row_delta = jnp.sum(mixed_grad_grid.astype(jnp.float32) * mixed_grid, axis=-1)

    def back_step(carried, key_block, offset):
        query_grad, pair_grad = carried
        new_query = []
        block_len = key_block.shape[1]
        for sequence in range(seq_count):
            softmax_rows = softmax_for(sequence, key_block, offset)
            key_part = key_block[sequence, :, :key_width].reshape(-1, KVH, HD)
            value_part = key_block[sequence, :, key_width:].reshape(-1, KVH, HD)
            softmax_grad = jnp.einsum(
                "krd,nkd->krn",
                mixed_grad_grid[sequence],
                value_part,
                preferred_element_type=jnp.float32,
            )
            score_grad = (softmax_rows * (softmax_grad - row_delta[sequence][..., None])).astype(
                jnp.bfloat16
            )
            new_query.append(
                query_grad[sequence]
                + jnp.einsum(
                    "krn,nkd->krd", score_grad, key_part, preferred_element_type=jnp.float32
                )
                * score_scale
            )
            key_grad = (
                jnp.einsum(
                    "krn,krd->nkd",
                    score_grad,
                    query_grid[sequence],
                    preferred_element_type=jnp.float32,
                )
                * score_scale
            )
            value_grad = jnp.einsum(
                "krn,krd->nkd",
                softmax_rows.astype(jnp.bfloat16),
                mixed_grad_grid[sequence],
                preferred_element_type=jnp.float32,
            )
            block_grad = jnp.concatenate(
                [key_grad.reshape(block_len, key_width), value_grad.reshape(block_len, key_width)],
                axis=-1,
            )
            current = lax.dynamic_slice(
                pair_grad,
                (jnp.int32(sequence), offset, jnp.int32(0)),
                (1, block_len, 2 * key_width),
            )
            pair_grad = lax.dynamic_update_slice(
                pair_grad, current + block_grad[None], (jnp.int32(sequence), offset, jnp.int32(0))
            )
        return (jnp.stack(new_query), pair_grad)

    query_start = jnp.zeros((seq_count, KVH, group_rows, HD), jnp.float32)
    pair_start = jnp.zeros((seq_count, seq_length, 2 * key_width), jnp.float32)
    query_grad_grid, pair_grad_all = attention_blocks(
        back_step, (query_start, pair_start), all_pairs, last_query
    )
    pair_grad_local = lax.psum_scatter(
        pair_grad_all.astype(jnp.bfloat16), "expert", scatter_dimension=1, tiled=True
    ).astype(jnp.float32)
    query_grad_rows = rope_back(from_grid(query_grad_grid).reshape(seq_count, stretch_len, H, HD))
    key_grad_rows = rope_back(
        pair_grad_local[..., :key_width].reshape(seq_count, stretch_len, KVH, HD)
    )
    projected_grad = jnp.concatenate(
        [
            query_grad_rows.reshape(row_count, query_width),
            key_grad_rows.reshape(row_count, key_width),
            pair_grad_local[..., key_width:].reshape(row_count, key_width),
        ],
        axis=-1,
    ).astype(jnp.bfloat16)
    project_grad_full = jnp.einsum(
        "rd,rf->df", normed_one, projected_grad, preferred_element_type=jnp.float32
    )
    normed_one_grad = jnp.dot(projected_grad, full_project.T, preferred_element_type=jnp.float32)
    unused_one, norm_one_pull = jax.vjp(rms_norm, tokens, gain_values[0])
    token_part, gain_one_grad = norm_one_pull(normed_one_grad)
    input_grad = hidden_grad_one + token_part
    gains_grad_full = jnp.stack([gain_one_grad, gain_two_grad])
    project_grad, output_grad, router_grad, gains_grad = (
        lax.psum_scatter(project_grad_full, ("dp", "expert"), scatter_dimension=0, tiled=True),
        lax.psum_scatter(output_grad_full, ("dp", "expert"), scatter_dimension=0, tiled=True),
        lax.psum_scatter(router_grad_full, ("dp", "expert"), scatter_dimension=0, tiled=True),
        lax.psum_scatter(gains_grad_full, ("dp", "expert"), scatter_dimension=1, tiled=True),
    )
    rate_project = 3.0 * (2.0 / D) ** 0.5
    rate_output = 3.0 * (seq_length / (32.0 * H * HD)) ** 0.5
    rate_router = 1.5 / D**0.5
    rate_gains = 0.8
    rate_in = 3.0 / D**0.5
    rate_down = 12.0 / FF**0.5
    project_new = adam_update(
        project_weight, project_moment, project_square, project_grad, rate_project, weight_decay
    )
    output_new = adam_update(
        output_weight, output_moment, output_square, output_grad, rate_output, weight_decay
    )
    router_new = adam_update(
        router_weight, router_moment, router_square, router_grad, rate_router, weight_decay
    )
    gains_new = adam_update(norm_gains, gains_moment, gains_square, gains_grad, rate_gains, 0.0)
    in_new = adam_update(
        expert_in, expert_in_moment, expert_in_square, expert_in_grad, rate_in, weight_decay
    )
    down_new = adam_update(
        expert_down,
        expert_down_moment,
        expert_down_square,
        expert_down_grad,
        rate_down,
        weight_decay,
    )
    return (
        outputs.reshape(seq_count, stretch_len, model_width),
        input_grad.reshape(seq_count, stretch_len, model_width),
        project_new[0],
        project_new[1],
        project_new[2],
        output_new[0],
        output_new[1],
        output_new[2],
        router_new[0],
        router_new[1],
        router_new[2],
        gains_new[0],
        gains_new[1],
        gains_new[2],
        in_new[0],
        in_new[1],
        in_new[2],
        down_new[0],
        down_new[1],
        down_new[2],
    )


def solution(mesh):
    token_spec = P("dp", "expert", None)
    row_spec = P(("dp", "expert"), None)
    gain_spec = P(None, ("dp", "expert"))
    expert_spec = P("expert", "dp", None)
    states = (row_spec,) * 9 + (gain_spec,) * 3 + (expert_spec,) * 6
    small = mesh.shape["dp"] == 4 and mesh.shape["expert"] == 8
    return jax.shard_map(
        local if small else general,
        mesh=mesh,
        in_specs=(token_spec, token_spec, P(("dp", "expert"), None, None)) + states,
        out_specs=(token_spec, token_spec) + states,
        check_vma=False,
    )
```

```python
import jax
import jax.numpy as jnp
from jax import lax
from jax.experimental import pallas as pl
from jax.experimental.pallas import tpu as pltpu
from jax.sharding import PartitionSpec as P

D = 1536
H = 12
KVH = 2
HD = 128
FF = 768
TOP = 4
STEP = 10
GROUP = H // KVH
QW = H * HD
KW = KVH * HD
QKV = QW + 2 * KW
EXP_DEV = 1
EXTRA = 128

norm_epsilon = 1e-06
adam_epsilon = 1e-08
beta_first = 0.9
beta_second = 0.95
weight_decay = 0.1
rope_base = 1000000.0
masked_score = -1e30
score_scale = HD ** (-0.5)
log_two = 0.6931471805599453
BF = jnp.bfloat16
F32 = jnp.float32
VMEM_BYTES = 50 * 1024 * 1024
HINT = pl.CostEstimate(flops=0, bytes_accessed=0, transcendentals=0)


def dot(a, b, da, db):
    return lax.dot_general(a, b, (((da,), (db,)), ((), ())), preferred_element_type=F32)


def after(value, *others):
    return lax.optimization_barrier((value, *others))[0]


def bring(pairs, sems):
    copies = [pltpu.make_async_copy(a, b, sems.at[n]) for n, (a, b) in enumerate(pairs)]
    for copy in copies:
        copy.start()
    return copies


def glue_call(kernel, out_shape, *operands, scalars=1, **options):
    vmem = pl.BlockSpec(memory_space=pltpu.VMEM)
    options.setdefault(
        "in_specs",
        [pl.BlockSpec(memory_space=pltpu.SMEM)] * scalars + [vmem] * (len(operands) - scalars),
    )
    options.setdefault("out_specs", [vmem] * len(out_shape))
    return pl.pallas_call(
        kernel,
        out_shape=out_shape,
        compiler_params=pltpu.CompilerParams(vmem_limit_bytes=VMEM_BYTES),
        cost_estimate=HINT,
        **options,
    )(*operands)


def plane_kernel(place_ref, *refs):
    blocks, out_ref, sems = refs[:4], refs[4], refs[5]
    moves = [
        (block, out_ref.at[lax.rem(place_ref[0] + step, 4)]) for step, block in enumerate(blocks)
    ]
    for copy in bring(moves, sems):
        copy.wait()


def plane_end(blocks):
    anywhere = pl.BlockSpec(memory_space=pl.ANY)
    return glue_call(
        plane_kernel,
        [jax.ShapeDtypeStruct((4,) + blocks[0].shape, BF)],
        lax.axis_index("dp")[None],
        *blocks,
        in_specs=[pl.BlockSpec(memory_space=pltpu.SMEM)] + [anywhere] * 4,
        out_specs=[anywhere],
        scratch_shapes=[pltpu.SemaphoreType.DMA((4,))],
    )[0]


def halves_kernel(by_x_ref, by_y_ref, low_ref, high_ref, sems):
    half = low_ref.shape[0]
    moves = [(by_x_ref.at[pl.ds(0, half)], low_ref), (by_y_ref.at[pl.ds(half, half)], high_ref)]
    for copy in bring(moves, sems):
        copy.wait()


def halves_call(near):
    anywhere = pl.BlockSpec(memory_space=pl.ANY)
    half = jax.ShapeDtypeStruct((near[0].shape[0] // 2, *near[0].shape[1:]), BF)
    return glue_call(
        halves_kernel,
        [half, half],
        *near,
        in_specs=[anywhere] * 2,
        out_specs=[anywhere] * 2,
        scratch_shapes=[pltpu.SemaphoreType.DMA((2,))],
    )


def hop(value, mask):
    return lax.ppermute(value, "expert", [(i, i ^ mask) for i in range(8)])


def total(one, two):
    return (one.astype(F32) + two.astype(F32)).astype(one.dtype)


def gather_near(value):
    return hop(value, 2), hop(value, 4)


def gather_over(near):
    low, high = halves_call(near)
    by_x, by_y, _, _ = phase(*near, low, high)
    return (hop(low, 4), hop(high, 2)), (by_x, by_y)


def gather_cores(near):
    return hop(near[0], 1), hop(near[1], 1)


def gathered(value, sibling, near, cores, diagonal, diagonal_core):
    return [value, sibling, near[0], cores[0], near[1], cores[1], diagonal, diagonal_core]


def reduce_over(diagonal):
    half = diagonal.shape[0] // 2
    return hop(diagonal[:half], 2), hop(diagonal[half:], 4)


def last_hops(by_x, by_y):
    return hop(by_x, 2), hop(by_y, 4)


def reduced(own, last):
    return own.astype(F32) + last[0].astype(F32) + last[1].astype(F32)


def phase(*values):
    return lax.optimization_barrier(values)


def plane_hop(shard, step):
    return lax.ppermute(shard, "dp", [((i + step) % 4, i) for i in range(4)])


def key_block(kv_ref, row):
    return jnp.concatenate(
        [kv_ref[n, row : row + HD, :].astype(F32).T for n in range(kv_ref.shape[0])], axis=0
    ).astype(BF)


def two(ref, h):
    return jnp.concatenate([ref[h], ref[h + 1]], axis=1)


def forward_kernel(q_ref, kv_ref, bias_ref, mixed_ref, lse_ref):
    stretch = bias_ref.shape[1]
    bias = jnp.concatenate([bias_ref[...]] * 2, axis=1)
    for g in range(KVH):
        keys = key_block(kv_ref, g * HD)
        values = jnp.concatenate(
            [kv_ref[n, KW + g * HD : KW + (g + 1) * HD, :] for n in range(kv_ref.shape[0])], axis=1
        )
        for h in range(g * GROUP, (g + 1) * GROUP, 2):
            scores = dot(keys, two(q_ref, h), 1, 0) + bias
            top = jnp.max(scores, axis=0, keepdims=True)
            weights = jnp.exp2((scores - top) * (score_scale / log_two))
            amount = jnp.sum(weights, axis=0, keepdims=True)
            mixed = dot(values, weights.astype(BF), 1, 0) / amount
            lse = top * score_scale + jnp.log(amount)
            for n in range(2):
                part = slice(n * stretch, (n + 1) * stretch)
                mixed_ref[h + n] = mixed[:, part]
                lse_ref[0, h + n : h + n + 1, :] = lse[:, part]


def backward_kernel(q_ref, kv_ref, bias_ref, mixed_ref, lse_ref, grad_ref, dq_ref, same_ref, other_ref):
    blocks, stretch = kv_ref.shape[0], kv_ref.shape[2]
    bias = jnp.concatenate([bias_ref[...]] * 2, axis=1)
    for g in range(KVH):
        keys, values = key_block(kv_ref, g * HD), key_block(kv_ref, KW + g * HD)
        keys_flat = jnp.concatenate(
            [kv_ref[n, g * HD : (g + 1) * HD, :] for n in range(blocks)], axis=1
        )
        key_grad = jnp.zeros(keys.shape, F32)
        value_grad = jnp.zeros(keys.shape, F32)
        for h in range(g * GROUP, (g + 1) * GROUP, 2):
            query, grad = two(q_ref, h), two(grad_ref, h)
            lse = jnp.concatenate([lse_ref[0, h : h + 1, :], lse_ref[0, h + 1 : h + 2, :]], axis=1)
            scores = dot(keys, query, 1, 0) + bias
            probs = jnp.exp2(scores * (score_scale / log_two) - lse * (1.0 / log_two))
            delta = jnp.sum(two(mixed_ref, h) * grad.astype(F32), axis=0, keepdims=True)
            score_grad = (probs * (dot(values, grad, 1, 0) - delta)).astype(BF)
            query_grad = dot(keys_flat, score_grad, 1, 0) * score_scale
            for n in range(2):
                dq_ref[h + n] = query_grad[:, n * stretch : (n + 1) * stretch]
            key_grad += dot(score_grad, query, 1, 1)
            value_grad += dot(probs.astype(BF), grad, 1, 1)
        key_grad = (key_grad * score_scale).astype(BF)
        value_grad = value_grad.astype(BF)
        for n in range(blocks):
            part, ref = slice(n * stretch, (n + 1) * stretch), (same_ref, other_ref)[n % 2]
            ref[n // 2, :, g * HD : (g + 1) * HD] = key_grad[part]
            ref[n // 2, :, KW + g * HD : KW + (g + 1) * HD] = value_grad[part]


def attention_call(kernel, outs, out_specs, queries, pairs, bias, *more):
    blocks, _, tokens = pairs.shape
    stretch = bias.shape[1]
    head = pl.BlockSpec((H, HD, stretch), lambda s: (0, 0, s))
    row = pl.BlockSpec((1, H, stretch), lambda s: (s, 0, 0))
    specs = [
        head,
        pl.BlockSpec((blocks, 2 * KW, stretch), lambda s: (0, 0, s)),
        pl.BlockSpec(bias.shape, lambda s: (0, 0)),
        head,
        row,
        head,
    ]
    keys = blocks * stretch
    return pl.pallas_call(
        kernel,
        grid=(tokens // stretch,),
        in_specs=specs[: 3 + len(more)],
        out_specs=[head if s == "head" else row if s == "row" else s for s in out_specs],
        out_shape=outs,
        compiler_params=pltpu.CompilerParams(vmem_limit_bytes=56 * 1024 * 1024),
        cost_estimate=HINT,
    )(queries, pairs, bias, *more)


HALF = FF // 2
ROWS = D // 4
DOWN = FF // 4


def inner(weight_ref):
    return jnp.concatenate([weight_ref[a, :ROWS] for a in range(4)], axis=0)


def outer(first_ref, half=None):
    owners = range(4) if half is None else (2 * half, 2 * half + 1)
    return jnp.concatenate(
        [
            jnp.concatenate(
                [first_ref[a, ROWS : ROWS + DOWN], first_ref[a, ROWS + DOWN :]], axis=1
            )
            for a in owners
        ],
        axis=0,
    )


def gates_for(me_ref, gates):
    lanes = lax.broadcasted_iota(jnp.int32, gates.shape, 1)
    return jnp.sum(jnp.where(lanes == me_ref[0], gates, 0.0), axis=1, keepdims=True)


def first_kernel(me_ref, *refs):
    rows_in, grads_in = refs[:8], refs[8:16]
    bias_ref, first_ref, router_ref = refs[16:19]
    gates_out, gate_grad_out, gate_up_out, hidden_out, weight_out = refs[19:24]
    rows_v, grads_v, gate_up_v, hidden_v, weight_v, in_sems, out_sems = refs[24:]
    count = rows_in[0].shape[0]
    moves = []
    for k in range(8):
        t, part = k // 2, pl.ds((k % 2) * count, count)
        moves += [(rows_in[k], rows_v.at[t, part]), (grads_in[k], grads_v.at[t, part])]
    arriving = bring(moves, in_sems)
    weight, back = inner(first_ref), outer(first_ref, 0)
    leaving = []
    for t in range(4):
        part = slice(t * 2 * count, (t + 1) * 2 * count)
        for copy in arriving[4 * t : 4 * t + 4]:
            copy.wait()
        rows, grads = rows_v[t], grads_v[t]
        logits = dot(rows, router_ref[...], 1, 0) + bias_ref[part]
        exps = jnp.exp(logits - jnp.max(logits, axis=1, keepdims=True))
        gates = exps / jnp.sum(exps, axis=1, keepdims=True)
        gates_out[part] = gates
        mine = gates_for(me_ref, gates)
        gate_up = dot(rows, weight, 1, 0)
        hidden, slope_gate, slope_up = gated(gate_up[:, :HALF], gate_up[:, HALF:])
        hidden_grad = dot(grads, back, 1, 1)
        hidden = hidden.astype(BF).astype(F32)
        gate_grad = jnp.sum(hidden * hidden_grad, axis=1, keepdims=True)
        gate_grad_out[part] = jnp.broadcast_to(gate_grad, (2 * count, EXTRA))
        hidden_grad = hidden_grad * mine
        gate_up_v[t, :, :HALF] = (hidden_grad * slope_gate).astype(BF)
        gate_up_v[t, :, HALF:] = (hidden_grad * slope_up).astype(BF)
        hidden_v[t] = (mine * hidden).astype(BF)
        pairs = [(gate_up_v.at[t], gate_up_out.at[t]), (hidden_v.at[t], hidden_out.at[t])]
        leaving += bring(pairs, out_sems.at[pl.ds(2 * t, 2)])
    gate_up = gate_up_v[...].reshape(8 * count, 2 * HALF)
    for a in range(4):
        rows = rows_v[:, :, a * ROWS : (a + 1) * ROWS].reshape(8 * count, ROWS)
        weight_v[a] = dot(rows, gate_up, 0, 0).astype(BF)
        leaving += bring([(weight_v.at[a], weight_out.at[a])], out_sems.at[pl.ds(8 + a, 1)])
    for copy in leaving:
        copy.wait()


def first_call(me, rows, grads, bias, first, router):
    count, width = rows[0].shape
    shape = jax.ShapeDtypeStruct
    vmem, anywhere = pl.BlockSpec(memory_space=pltpu.VMEM), pl.BlockSpec(memory_space=pl.ANY)
    return pl.pallas_call(
        first_kernel,
        in_specs=[pl.BlockSpec(memory_space=pltpu.SMEM)] + [anywhere] * 16 + [vmem] * 3,
        out_specs=[vmem] * 2 + [anywhere] * 3,
        out_shape=[shape((8 * count, EXTRA), F32)] * 2
        + [
            shape((4, 2 * count, 2 * HALF), BF),
            shape((4, 2 * count, HALF), BF),
            shape((4, ROWS, 2 * HALF), BF),
        ],
        scratch_shapes=[
            pltpu.VMEM((4, 2 * count, width), BF),
            pltpu.VMEM((4, 2 * count, width), BF),
            pltpu.VMEM((4, 2 * count, 2 * HALF), BF),
            pltpu.VMEM((4, 2 * count, HALF), BF),
            pltpu.VMEM((4, ROWS, 2 * HALF), BF),
            pltpu.SemaphoreType.DMA((16,)),
            pltpu.SemaphoreType.DMA((12,)),
        ],
        compiler_params=pltpu.CompilerParams(vmem_limit_bytes=VMEM_BYTES),
        cost_estimate=HINT,
    )(me, *rows, *grads, bias, first, router)


def second_kernel(t, me_ref, *refs):
    row0, row1, grad0, grad1, gates_in, gate_grad_in, up_in, hidden_in, first, second = refs[:10]
    outs = refs[10:16]
    rows_v, grads_v, gates_v, gate_grad_v, up_v, hidden_v, inner0_v, inner1_v, outer_v = refs[16:25]
    out_v, result_v, up_out, hidden_out, sems, out_sems = refs[25:]
    count = row0.shape[0]
    low, high, part = pl.ds(0, count), pl.ds(count, count), pl.ds(t * 2 * count, 2 * count)
    moves = [
        (row0, rows_v.at[low]),
        (row1, rows_v.at[high]),
        (second, inner1_v),
        (grad0, grads_v.at[low]),
        (grad1, grads_v.at[high]),
        (first.at[:, pl.ds(ROWS, 2 * DOWN)], outer_v),
        (gates_in.at[part], gates_v),
        (gate_grad_in.at[part], gate_grad_v),
        (up_in.at[t], up_v),
        (first.at[:, pl.ds(0, ROWS)], inner0_v),
        (hidden_in.at[t], hidden_v),
    ]
    arriving = bring(moves, sems)
    for copy in arriving[:3]:
        copy.wait()
    inner1 = inner1_v[...].reshape(D, 2 * HALF)
    gate_up = dot(rows_v[...], inner1, 1, 0)
    for copy in arriving[3:6]:
        copy.wait()
    outer0, outer1 = [
        jnp.concatenate(
            [jnp.concatenate([outer_v[a, :DOWN], outer_v[a, DOWN:]], axis=1) for a in owners], axis=0
        )
        for owners in ((0, 1), (2, 3))
    ]
    hidden_grad = dot(grads_v[...], outer1, 1, 1)
    for copy in arriving[6:]:
        copy.wait()
    copies = dot(up_v[...], inner0_v[...].reshape(D, 2 * HALF), 1, 1)
    result = dot(hidden_v[...], outer0, 1, 0)
    hidden, slope_gate, slope_up = gated(gate_up[:, :HALF], gate_up[:, HALF:])
    mine = gates_for(me_ref, gates_v[...])
    hidden = hidden.astype(BF).astype(F32)
    gate_grad = gate_grad_v[...] + jnp.sum(hidden * hidden_grad, axis=1, keepdims=True)
    hidden_grad = hidden_grad * mine
    up_out[:, :HALF] = (hidden_grad * slope_gate).astype(BF)
    up_out[:, HALF:] = (hidden_grad * slope_up).astype(BF)
    hidden_out[...] = (mine * hidden).astype(BF)
    leaving = bring([(up_out, outs[4]), (hidden_out, outs[5])], out_sems.at[pl.ds(0, 2)])
    copies = (copies + dot(up_out[...], inner1, 1, 1)).astype(BF)
    lanes = lax.broadcasted_iota(jnp.int32, (2 * count, EXTRA), 1)
    rounded = gate_grad.astype(BF).astype(F32)
    columns = (
        jnp.where(lanes == me_ref[0], rounded, 0.0)
        + jnp.where(lanes == me_ref[0] + 8, gate_grad - rounded, 0.0)
    ).astype(BF)
    for n in range(2):
        out_v[n, :, :D] = copies[n * count : (n + 1) * count]
        out_v[n, :, D:] = columns[n * count : (n + 1) * count]
    leaving += bring(
        [(out_v.at[1], outs[1]), (out_v.at[0], outs[0])], out_sems.at[pl.ds(2, 2)]
    )
    result = (result + dot(hidden_out[...], outer1, 1, 0)).astype(BF)
    for n in range(2):
        result_v[n] = result[n * count : (n + 1) * count]
    leaving += bring(
        [(result_v.at[1], outs[3]), (result_v.at[0], outs[2])], out_sems.at[pl.ds(4, 2)]
    )
    for copy in leaving:
        copy.wait()


def second_call(t, me, rows, grads, gates, gate_grad, up_first, hidden_first, first, second):
    count, width = rows[0].shape
    shape = jax.ShapeDtypeStruct
    anywhere = pl.BlockSpec(memory_space=pl.ANY)
    return pl.pallas_call(
        lambda *refs: second_kernel(t, *refs),
        in_specs=[pl.BlockSpec(memory_space=pltpu.SMEM)] + [anywhere] * 10,
        out_specs=[pl.BlockSpec(memory_space=pltpu.HBM)] * 6,
        out_shape=[shape((count, D + EXTRA), BF)] * 2
        + [shape((count, D), BF)] * 2
        + [shape((2 * count, 2 * HALF), BF), shape((2 * count, HALF), BF)],
        scratch_shapes=[
            pltpu.VMEM((2 * count, width), BF),
            pltpu.VMEM((2 * count, width), BF),
            pltpu.VMEM((2 * count, EXTRA), F32),
            pltpu.VMEM((2 * count, EXTRA), F32),
            pltpu.VMEM((2 * count, 2 * HALF), BF),
            pltpu.VMEM((2 * count, HALF), BF),
            pltpu.VMEM((4, ROWS, 2 * HALF), BF),
            pltpu.VMEM((4, ROWS, 2 * HALF), BF),
            pltpu.VMEM((4, 2 * DOWN, 2 * HALF), BF),
            pltpu.VMEM((2, count, D + EXTRA), BF),
            pltpu.VMEM((2, count, D), BF),
            pltpu.VMEM((2 * count, 2 * HALF), BF),
            pltpu.VMEM((2 * count, HALF), BF),
            pltpu.SemaphoreType.DMA((11,)),
            pltpu.SemaphoreType.DMA((6,)),
        ],
        compiler_params=pltpu.CompilerParams(vmem_limit_bytes=VMEM_BYTES),
        cost_estimate=HINT,
    )(
        me,
        *rows[2 * t : 2 * t + 2],
        *grads[2 * t : 2 * t + 2],
        gates,
        gate_grad,
        up_first,
        hidden_first,
        first,
        second,
    )


def last_kernel(*refs):
    rows_in, grads_in, ups, hiddens = refs[:8], refs[8:16], refs[16:20], refs[20:24]
    hidden0, out_ref, rows_v, grads_v, up_v, hidden0_v, hidden1_v, out_v, in_sems, out_sems = refs[24:]
    count = rows_in[0].shape[0]
    arriving = bring(
        [(ref, grads_v.at[pl.ds(k * count, count)]) for k, ref in enumerate(grads_in)]
        + [(hidden0, hidden0_v)]
        + [(ref, hidden1_v.at[t]) for t, ref in enumerate(hiddens)]
        + [(ref, rows_v.at[pl.ds(k * count, count)]) for k, ref in enumerate(rows_in)]
        + [(ref, up_v.at[t]) for t, ref in enumerate(ups)],
        in_sems,
    )
    for copy in arriving[:9]:
        copy.wait()
    grads = grads_v[...]
    for half, ref in enumerate((hidden0_v, hidden1_v)):
        if half:
            for copy in arriving[9:13]:
                copy.wait()
        sums = dot(ref[...].reshape(8 * count, HALF), grads, 0, 0).astype(BF)
        for n in range(2):
            for side in range(2):
                out_v[2 * half + n, ROWS + side * DOWN : ROWS + (side + 1) * DOWN] = sums[
                    n * DOWN : (n + 1) * DOWN, side * 2 * HALF : (side + 1) * 2 * HALF
                ]
    for copy in arriving[13:]:
        copy.wait()
    leaving = []
    gate_up = up_v[...].reshape(8 * count, 2 * HALF)
    for a in range(4):
        out_v[a, :ROWS] = dot(rows_v[:, a * ROWS : (a + 1) * ROWS], gate_up, 0, 0).astype(BF)
        leaving += bring([(out_v.at[a], out_ref.at[a])], out_sems.at[pl.ds(a, 1)])
    for copy in leaving:
        copy.wait()


def last_call(rows, grads, ups, hiddens, hidden0):
    count, width = rows[0].shape
    anywhere = pl.BlockSpec(memory_space=pl.ANY)
    whole = (4, ROWS + 2 * DOWN, 2 * HALF)
    return pl.pallas_call(
        last_kernel,
        in_specs=[anywhere] * 25,
        out_specs=anywhere,
        out_shape=jax.ShapeDtypeStruct(whole, BF),
        scratch_shapes=[
            pltpu.VMEM((8 * count, width), BF),
            pltpu.VMEM((8 * count, width), BF),
            pltpu.VMEM((4, 2 * count, 2 * HALF), BF),
            pltpu.VMEM((4, 2 * count, HALF), BF),
            pltpu.VMEM((4, 2 * count, HALF), BF),
            pltpu.VMEM(whole, BF),
            pltpu.SemaphoreType.DMA((25,)),
            pltpu.SemaphoreType.DMA((4,)),
        ],
        compiler_params=pltpu.CompilerParams(vmem_limit_bytes=VMEM_BYTES),
        cost_estimate=HINT,
    )(*rows, *grads, *ups, *hiddens, hidden0)


def rms_factor(values):
    return lax.rsqrt(jnp.mean(values * values, axis=-1, keepdims=True) + norm_epsilon)


def rms_back(gradient, values, factor, gain):
    scaled = gradient * gain
    inner = jnp.mean(scaled * values, axis=-1, keepdims=True)
    return (
        factor * scaled - values * (factor * factor * factor * inner),
        jnp.sum(gradient * values * factor, axis=0),
    )


def turn(heads, cosine, sine):
    half = HD // 2
    first, second = heads[:, :half], heads[:, half:]
    return jnp.concatenate(
        [first * cosine - second * sine, second * cosine + first * sine], axis=1
    )


def adam_update(weight, moment, square, gradient, step_rate, shrink):
    moment_new = beta_first * moment + (1.0 - beta_first) * gradient
    square_new = beta_second * square + (1.0 - beta_second) * gradient * gradient
    normalized = (
        moment_new
        / (1.0 - beta_first**STEP)
        / (jnp.sqrt(square_new / (1.0 - beta_second**STEP)) + adam_epsilon)
    )
    return (moment_new, square_new, weight - step_rate * (normalized + shrink * weight))


def assemble(me_ref, refs, weight_v, whole_ref, sems, out_sem):
    rows = refs[0].shape[1]
    moves = []
    for k in range(8):
        for a in range(4):
            if k < 6:
                source = refs[k].at[a]
            else:
                source = refs[2 * k - 6 + a // 2].at[a % 2]
            start = pl.multiple_of((a * 8 + (me_ref[0] ^ k)) * rows, 16)
            moves.append((source, weight_v.at[pl.ds(start, rows)]))
    for copy in bring(moves, sems):
        copy.wait()
    return bring([(weight_v, whole_ref)], out_sem)[0]


def project_kernel(me_ref, *refs):
    blocks, (inputs_ref, cosine_ref, sine_ref, routes_ref) = refs[:10], refs[10:14]
    query_ref, pair_ref, normed_ref, factor_ref, gains_ref, router_ref, whole_ref = refs[14:21]
    weight_v, sems, out_sem = refs[21:]
    leaving = assemble(me_ref, blocks, weight_v, whole_ref, sems, out_sem)
    extras = weight_v[:, QKV:]
    lanes = lax.broadcasted_iota(jnp.int32, extras.shape, 1)
    router_ref[...] = jnp.where(lanes < 8, extras.astype(F32), 0.0).astype(BF)
    gains = extras.astype(F32).T[8:16]
    gains_ref[...] = gains
    tokens = inputs_ref[...].astype(F32)
    factor = rms_factor(tokens)
    factor_ref[...] = factor
    normed = (tokens * factor * gains[:1]).astype(BF)
    normed_ref[...] = normed
    projected = dot(normed, weight_v[:, :QKV], 1, 0)
    half = HD // 2
    cosine, sine = cosine_ref[...], sine_ref[...]
    for h in range(H + KVH):
        head = projected[:, h * HD : (h + 1) * HD].T
        first, second = head[:half], head[half:]
        head = jnp.concatenate(
            [first * cosine - second * sine, second * cosine + first * sine], axis=0
        ).astype(BF)
        if h < H:
            query_ref[h] = head
        else:
            pair_ref[(h - H) * HD : (h - H + 1) * HD] = head
    for h in range(KVH):
        start = QW + KW + h * HD
        pair_ref[KW + h * HD : KW + (h + 1) * HD] = projected[:, start : start + HD].T.astype(BF)
    pair_ref[2 * KW :] = routes_ref[...]
    leaving.wait()


def attended_kernel(me_ref, *refs):
    blocks, (mixed_ref, inputs_ref, gains_ref) = refs[:10], refs[10:13]
    hidden_ref, normed_ref, factor_ref, rows_ref, whole_ref, weight_v, sems, out_sem = refs[13:]
    leaving = assemble(me_ref, blocks, weight_v, whole_ref, sems, out_sem)
    rows_ref[...] = mixed_ref[...].reshape(rows_ref.shape).astype(BF)
    hidden = inputs_ref[...].astype(F32) + dot(rows_ref[...], weight_v[...], 0, 0)
    factor = rms_factor(hidden)
    hidden_ref[...] = hidden
    factor_ref[...] = factor
    normed_ref[...] = (hidden * factor * gains_ref[1:2]).astype(BF)
    leaving.wait()


def assembled_call(kernel, out_shape, whole_shape, me, blocks, *operands):
    vmem, anywhere = pl.BlockSpec(memory_space=pltpu.VMEM), pl.BlockSpec(memory_space=pl.ANY)
    return glue_call(
        kernel,
        [*out_shape, jax.ShapeDtypeStruct(whole_shape, BF)],
        me,
        *blocks,
        *operands,
        in_specs=[pl.BlockSpec(memory_space=pltpu.SMEM)]
        + [anywhere] * len(blocks)
        + [vmem] * len(operands),
        out_specs=[vmem] * len(out_shape) + [anywhere],
        scratch_shapes=[
            pltpu.VMEM(whole_shape, BF),
            pltpu.SemaphoreType.DMA((32,)),
            pltpu.SemaphoreType.DMA((1,)),
        ],
    )


def token_kernel(
    own_ref,
    core_ref,
    last_x_ref,
    last_y_ref,
    gates_ref,
    router_ref,
    hidden_ref,
    factor_ref,
    gain_ref,
    grad_ref,
    normed_ref,
    weight_ref,
    hidden_grad_ref,
    branch_ref,
    mixed_grad_ref,
    extras_ref,
):
    copies = sum(ref[...].astype(F32) for ref in (own_ref, core_ref, last_x_ref, last_y_ref))
    columns, gates = copies[:, D:], gates_ref[: copies.shape[0]]
    gate_grad = columns + pltpu.roll(columns, EXTRA - 8, 1)
    inner_sum = jnp.sum(gates * gate_grad, axis=1, keepdims=True)
    logit_grad = (gates * (gate_grad - inner_sum)).astype(BF)
    gradient = copies[:, :D] + dot(logit_grad, router_ref[...], 1, 1)
    hidden, factor = hidden_ref[...], factor_ref[...]
    scaled = gradient * gain_ref[1:2]
    inner_mean = jnp.mean(scaled * hidden, axis=-1, keepdims=True)
    part = factor * scaled - hidden * (factor * factor * factor * inner_mean)
    hidden_grad = grad_ref[...].astype(F32) + part
    hidden_grad_ref[...] = hidden_grad
    branch = hidden_grad.astype(BF)
    branch_ref[...] = branch
    mixed_grad_ref[...] = dot(weight_ref[...], branch, 1, 1).astype(BF)
    gain_grad = jnp.sum(gradient * hidden * factor, axis=0, keepdims=True)
    router_grad = dot(logit_grad, normed_ref[...], 0, 0)
    row = lax.broadcasted_iota(jnp.int32, router_grad.shape, 0)
    extras_ref[...] = jnp.where(row == 8, gain_grad, router_grad)


def put_cut(me_ref, scratch, same_ref, other_ref):
    core, chip = lax.rem(me_ref[0], 2), lax.div(me_ref[0], 2)
    rows = same_ref.shape[2]
    for n in range(4):
        for side, ref in enumerate((same_ref, other_ref)):
            device = 2 * (chip ^ n) + (core ^ side)
            for a in range(4):
                start = pl.multiple_of((a * 8 + device) * rows, 16)
                ref[n, a] = scratch[pl.ds(start, rows), :]


def cut_shapes(rows, width):
    return [jax.ShapeDtypeStruct((4, 4, rows, width), BF)] * 2


def output_kernel(me_ref, mixed_ref, branch_ref, extras_ref, same_ref, other_ref, scratch):
    scratch[:, :D] = dot(mixed_ref[...], branch_ref[...], 1, 0).astype(BF)
    scratch[:, D:] = extras_ref[...].T.astype(BF)
    put_cut(me_ref, scratch, same_ref, other_ref)


def turned_back(value, cosine, sine):
    half = HD // 2
    first, second = value[:half], value[half:]
    return jnp.concatenate(
        [first * cosine + second * sine, second * cosine - first * sine], axis=0
    )


def query_kernel(
    me_ref, query_ref, cosine_ref, sine_ref, normed_ref, part_ref, same_ref, other_ref, scratch
):
    for h in range(H):
        part = turned_back(query_ref[h], cosine_ref[...], sine_ref[...])
        part_ref[h * HD : (h + 1) * HD] = part.astype(BF)
    scratch[...] = dot(normed_ref[...], part_ref[...], 0, 1).astype(BF)
    put_cut(me_ref, scratch, same_ref, other_ref)


def late_kernel(
    me_ref,
    own_ref,
    last_x_ref,
    last_y_ref,
    cosine_ref,
    sine_ref,
    normed_ref,
    part_ref,
    same_ref,
    other_ref,
    scratch,
):
    value = sum(ref[...].astype(F32) for ref in (own_ref, last_x_ref, last_y_ref)).T
    for h in range(KVH):
        part = turned_back(value[h * HD : (h + 1) * HD], cosine_ref[...], sine_ref[...])
        part_ref[h * HD : (h + 1) * HD] = part.astype(BF)
    part_ref[KW:] = value[KW:].astype(BF)
    scratch[...] = dot(normed_ref[...], part_ref[...], 0, 1).astype(BF)
    put_cut(me_ref, scratch, same_ref, other_ref)


def sums_kernel(same_ref, arrived_ref, own_ref, by_x_ref, by_y_ref, low_ref, high_ref):
    for n, ref in enumerate((own_ref, by_x_ref, by_y_ref)):
        ref[...] = total(same_ref[n], arrived_ref[n])
    for half, ref in enumerate((low_ref, high_ref)):

        @pl.when(pl.program_id(0) == half)
        def _():
            ref[...] = total(same_ref[3], arrived_ref[3])


def sums_call(same, arrived):
    _, parts, rows, width = same.shape
    half = parts // 2
    both = pl.BlockSpec((4, half, rows, width), lambda i: (0, i, 0, 0))
    one = pl.BlockSpec((half, rows, width), lambda i: (i, 0, 0))
    fixed = pl.BlockSpec((half, rows, width), lambda i: (0, 0, 0))
    shape = jax.ShapeDtypeStruct
    return glue_call(
        sums_kernel,
        [shape((parts, rows, width), BF)] * 3 + [shape((half, rows, width), BF)] * 2,
        same,
        arrived,
        grid=(2,),
        in_specs=[both] * 2,
        out_specs=[one] * 3 + [fixed] * 2,
    )


def over_hops(sums):
    return hop(sums[3], 2), hop(sums[4], 4)


def join_kernel(by_x_ref, by_y_ref, over_x_ref, over_y_ref, new_x_ref, new_y_ref):
    new_y_ref[...] = total(by_y_ref[...], over_x_ref[...])
    new_x_ref[...] = total(by_x_ref[...], over_y_ref[...])


def join_call(sums, over):
    by_x, by_y = sums[1:3]
    half = (by_x.shape[0] // 2, *by_x.shape[1:])
    low = pl.BlockSpec(half, lambda i: (0, 0, 0))
    high = pl.BlockSpec(half, lambda i: (1, 0, 0))
    return glue_call(
        join_kernel,
        [jax.ShapeDtypeStruct(by_x.shape, BF)] * 2,
        by_x,
        by_y,
        *over,
        grid=(1,),
        in_specs=[high, low, low, low],
        out_specs=[high, low],
        input_output_aliases={0: 0, 1: 1},
    )


def both_kernel(x0_ref, x1_ref, y0_ref, y1_ref, over_x_ref, over_y_ref, new_x_ref, new_y_ref):
    half = over_x_ref.shape[0]
    by_x = x0_ref[...].astype(F32) + x1_ref[...].astype(F32)
    by_y = y0_ref[...].astype(F32) + y1_ref[...].astype(F32)
    new_x_ref[:half] = by_x[:half].astype(BF)
    new_x_ref[half:] = (by_x[half:] + over_y_ref[...].astype(F32)).astype(BF)
    new_y_ref[:half] = (by_y[:half] + over_x_ref[...].astype(F32)).astype(BF)
    new_y_ref[half:] = by_y[half:].astype(BF)


def both_call(by_x, x_core, by_y, y_core, over):
    return glue_call(
        both_kernel,
        [jax.ShapeDtypeStruct(by_x.shape, BF)] * 2,
        by_x,
        x_core,
        by_y,
        y_core,
        *over,
        scalars=0,
    )


def send_kernel(place_ref, *refs):
    groups, outs = (len(refs) - 4) // 3, refs[-4:]
    start = 0
    for g in range(groups):
        own_ref, last_x_ref, last_y_ref = refs[3 * g : 3 * g + 3]
        size = own_ref.shape[2]
        for step, out in enumerate(outs):
            at = lax.rem(place_ref[0] + step, 4)
            value = sum(ref[at].astype(F32) for ref in (own_ref, last_x_ref, last_y_ref))
            out[:, start : start + size] = value.astype(out.dtype)
        start += size


def send_call(*groups):
    rows, width = groups[0][0].shape[1], sum(group[0].shape[2] for group in groups)
    shape = jax.ShapeDtypeStruct
    own, *sent = glue_call(
        send_kernel,
        [shape((rows, width), F32)] + [shape((rows, width), BF)] * 3,
        lax.axis_index("dp")[None],
        *[part for group in groups for part in group],
    )
    return own, [
        lax.ppermute(value, "dp", [(i, (i + step) % 4) for i in range(4)])
        for step, value in enumerate(sent, 1)
    ]


def adam_kernel(pieces, step_rate, shrink, weight_ref, moment_ref, square_ref, *refs):
    grads, outs = refs[: len(pieces)], refs[len(pieces) :]
    for ref, (_, _, parts) in zip(grads, pieces):
        for source, target, size in parts:
            columns = slice(target, target + size)
            news = adam_update(
                weight_ref[:, columns],
                moment_ref[:, columns],
                square_ref[:, columns],
                ref[:, source : source + size].astype(F32),
                step_rate,
                shrink,
            )
            for out, new in zip(outs, news):
                out[:, columns] = new


def adam_call(weight, moment, square, pieces, step_rate, shrink, rows):
    width = weight.shape[2]
    state = pl.BlockSpec((None, rows, width), lambda i: (0, i, 0))
    return pl.pallas_call(
        lambda *refs: adam_kernel(pieces, step_rate, shrink, *refs),
        grid=(weight.shape[1] // rows,),
        in_specs=[state] * 3
        + [
            pl.BlockSpec((rows, piece.shape[1]), lambda i, first=first: (first + i, 0))
            for piece, first, _ in pieces
        ],
        out_specs=[state] * 3,
        out_shape=[jax.ShapeDtypeStruct(weight.shape, F32)] * 3,
        compiler_params=pltpu.CompilerParams(vmem_limit_bytes=VMEM_BYTES),
        cost_estimate=HINT,
    )(weight, moment, square, *[piece for piece, _, _ in pieces])


def owned_kernel(step_rate, weight_ref, moment_ref, square_ref, own_ref, *refs):
    arrived, outs, rest = refs[:3], refs[3:6], refs[6]
    total_grad = own_ref[...] + sum(ref[...].astype(F32) for ref in arrived)
    size = weight_ref.shape[1]
    weight, gradient = weight_ref[...], total_grad[:, :size]
    news = adam_update(
        weight, moment_ref[...], square_ref[...], gradient, step_rate, weight_decay
    )
    for out, new in zip(outs, news):
        out[...] = new
    if total_grad.shape[1] > size:
        rest[...] = total_grad[:, size:]
    else:
        products = jnp.sum(weight.astype(BF).astype(F32) * gradient, axis=1, keepdims=True)
        rest[...] = jnp.broadcast_to(products, rest.shape)


def owned_call(weight, moment, square, sums, step_rate):
    vmem = pl.BlockSpec(memory_space=pltpu.VMEM)
    state = jax.ShapeDtypeStruct(weight.shape, F32)
    return pl.pallas_call(
        lambda *refs: owned_kernel(step_rate, *refs),
        in_specs=[vmem] * 7,
        out_specs=[vmem] * 4,
        out_shape=[state] * 3 + [jax.ShapeDtypeStruct((weight.shape[0], EXTRA), F32)],
        compiler_params=pltpu.CompilerParams(vmem_limit_bytes=VMEM_BYTES),
        cost_estimate=HINT,
    )(weight, moment, square, *sums)


def input_kernel(query_ref, late_ref, weight_ref, tokens_ref, factor_ref, gain_ref, grad_ref, out_ref):
    gradient = dot(query_ref[...], weight_ref[:, :QW], 0, 1)
    gradient = gradient + dot(late_ref[...], weight_ref[:, QW:QKV], 0, 1)
    tokens, factor = tokens_ref[...].astype(F32), factor_ref[...]
    scaled = gradient * gain_ref[:1]
    inner_mean = jnp.mean(scaled * tokens, axis=-1, keepdims=True)
    part = factor * scaled - tokens * (factor * factor * factor * inner_mean)
    out_ref[...] = grad_ref[...] + part


def input_call(*operands):
    vmem = pl.BlockSpec(memory_space=pltpu.VMEM)
    return pl.pallas_call(
        input_kernel,
        in_specs=[vmem] * 7,
        out_specs=vmem,
        out_shape=jax.ShapeDtypeStruct(operands[-1].shape, F32),
        compiler_params=pltpu.CompilerParams(vmem_limit_bytes=VMEM_BYTES),
        cost_estimate=HINT,
    )(*operands)


def gated(gate, up):
    rate = (2.0 / jnp.pi) ** 0.5
    bend = 0.044715 * rate
    square = gate * gate
    part = 0.5 + 0.5 * jnp.tanh(gate * (rate + bend * square))
    gelu = gate * part
    slope = part + gelu * (1.0 - part) * (2.0 * rate + 6.0 * bend * square)
    return gelu * up, slope * up, gelu


def local(
    inputs,
    cotangent,
    routes,
    project_weight,
    project_moment,
    project_square,
    output_weight,
    output_moment,
    output_square,
    router_weight,
    router_moment,
    router_square,
    norm_gains,
    gains_moment,
    gains_square,
    expert_in,
    expert_in_moment,
    expert_in_square,
    expert_down,
    expert_down_moment,
    expert_down_square,
):
    seq_count, stretch, width = inputs.shape
    device_count = lax.axis_size("expert")
    expert_count = device_count
    rows = seq_count * stretch
    me = lax.axis_index("expert")
    others = me ^ jnp.arange(device_count, dtype=jnp.int32)
    shard = project_weight.shape[0]

    first_payload = jnp.concatenate(
        [
            project_weight.astype(BF),
            router_weight.astype(BF),
            norm_gains.T.astype(BF),
            jnp.zeros((shard, EXTRA - expert_count - 2), BF),
        ],
        axis=1,
    )
    first_hops = [first_payload] + [plane_hop(first_payload, step) for step in (1, 2, 3)]
    own_grad = cotangent.reshape(rows, width)
    grad_near = gather_near(own_grad)
    in_low, down_low = expert_in[0].astype(BF), expert_down[0].astype(BF)
    share_first, share_second = [
        jnp.concatenate([in_low[:, p * HALF : (p + 1) * HALF] for p in (h, h + 2)], axis=1)
        for h in range(2)
    ]
    share_first = jnp.concatenate(
        [share_first, down_low[:, : 2 * HALF], down_low[:, 2 * HALF :]], axis=0
    )
    first_hops, grad_near, inputs, routes, output_low, place = phase(
        first_hops, grad_near, inputs, routes, output_weight, me
    )

    first_plane = plane_end(first_hops)
    first_near = gather_near(first_plane)
    output_low = output_low.astype(BF)
    output_hops = [output_low] + [plane_hop(output_low, step) for step in (1, 2, 3)]
    positions = place * stretch + jnp.arange(stretch, dtype=jnp.int32)
    frequency = rope_base ** (-jnp.arange(HD // 2, dtype=F32) / (HD // 2))
    angles = frequency[:, None] * positions.astype(F32)[None, :]
    cosine = jnp.tile(jnp.cos(angles), (1, seq_count))
    sine = jnp.tile(jnp.sin(angles), (1, seq_count))
    route_rows = jnp.concatenate(
        [routes.reshape(rows, TOP).T.astype(BF), jnp.zeros((32 - TOP, rows), BF)], axis=0
    )
    first_near, output_hops, share_first, share_second, cosine, sine, route_rows = phase(
        first_near, output_hops, share_first, share_second, cosine, sine, route_rows
    )

    weights_first = lax.all_gather(share_first, "dp")
    weights_second = lax.all_gather(share_second, "dp")
    first_over, first_later = gather_over(first_near)
    first_cores = gather_cores(first_later)
    first_sibling = hop(after(first_plane, *first_later), 1)
    output_plane = plane_end(output_hops)
    first_over, first_cores, first_sibling, output_plane = phase(
        first_over, first_cores, first_sibling, output_plane
    )

    first_far = hop(first_over[0], 1), hop(first_over[1], 1)
    output_near, output_sibling = gather_near(output_plane), hop(output_plane, 1)
    first_far = phase(first_far)[0]

    inputs = inputs.reshape(rows, width)
    shape = jax.ShapeDtypeStruct
    queries, pair_payload, normed_one, factor_one, gains, router, full_first = assembled_call(
        project_kernel,
        [
            shape((H, HD, rows), BF),
            shape((2 * KW + 32, rows), BF),
            shape((rows, width), BF),
            shape((rows, 1), F32),
            shape((8, D), F32),
            shape((D, EXTRA), BF),
        ],
        (D, QKV + EXTRA),
        me[None],
        [
            first_plane,
            first_sibling,
            first_near[0],
            first_cores[0],
            first_near[1],
            first_cores[1],
            *first_over,
            *first_far,
        ],
        inputs,
        cosine,
        sine,
        route_rows,
    )
    pair_payload, output_near, output_sibling, queries = phase(
        pair_payload, output_near, output_sibling, queries
    )

    key_positions = (others[:, None] * stretch + jnp.arange(stretch)[None, :]).reshape(-1)
    bias = jnp.where(key_positions[:, None] <= positions[None, :], 0.0, masked_score).astype(F32)
    pair_near, pair_sibling = gather_near(pair_payload), hop(pair_payload, 1)
    output_over, _ = gather_over(output_near)
    pair_near, pair_sibling, output_over, bias = phase(pair_near, pair_sibling, output_over, bias)

    pair_over, pair_later = gather_over(pair_near)
    pair_cores = gather_cores(pair_later)
    output_core_x = hop(after(output_near[0], *pair_later), 1)
    pair_over, pair_cores, output_core_x = phase(pair_over, pair_cores, output_core_x)

    pair_diagonal = jnp.concatenate(pair_over, axis=0)
    pair_core, output_core_y = hop(pair_diagonal, 1), hop(output_near[1], 1)
    output_far = hop(output_over[0], 1), hop(output_over[1], 1)
    pair_core, output_core_y, output_far = phase(pair_core, output_core_y, output_far)

    pair_blocks = gathered(
        pair_payload, pair_sibling, pair_near, pair_cores, pair_diagonal, pair_core
    )
    pairs = jnp.stack(pair_blocks)
    lanes = jnp.arange(EXTRA, dtype=jnp.int32)[None, :]
    grad_over, _ = gather_over(grad_near)
    grad_cores = gather_cores(grad_near)
    grad_sibling = hop(own_grad, 1)
    mixed, lse = attention_call(
        forward_kernel,
        [shape((H, HD, rows), F32), shape((seq_count, H, stretch), F32)],
        ["head", "row"],
        queries,
        pairs,
        bias,
    )
    mixed, lse, grad_over, grad_cores, grad_sibling = phase(
        mixed, lse, grad_over, grad_cores, grad_sibling
    )

    hidden_one, normed_two, factor_two, mixed_rows, full_output = assembled_call(
        attended_kernel,
        [
            shape((rows, width), F32),
            shape((rows, width), BF),
            shape((rows, 1), F32),
            shape((QW, rows), BF),
        ],
        (QW, D),
        me[None],
        [
            output_plane,
            output_sibling,
            output_near[0],
            output_core_x,
            output_near[1],
            output_core_y,
            *output_over,
            *output_far,
        ],
        mixed,
        inputs,
        gains,
    )

    row_near, row_sibling = gather_near(normed_two), hop(normed_two, 1)
    grad_diagonal = jnp.concatenate(grad_over, axis=0)
    grad_core = hop(grad_diagonal, 1)
    row_near, row_sibling, grad_core = phase(row_near, row_sibling, grad_core)
    grad_blocks = gathered(
        own_grad, grad_sibling, grad_near, grad_cores, grad_diagonal, grad_core
    )
    row_over, row_later = gather_over(row_near)
    row_cores = gather_cores(row_later)
    all_routes = jnp.concatenate(
        [block[2 * KW : 2 * KW + TOP].T for block in pair_blocks], axis=0
    ).astype(jnp.int32)
    named = jnp.any(all_routes[:, :, None] == lanes[None], axis=1)
    route_bias = jnp.where(named, 0.0, masked_score).astype(F32)
    row_over, row_cores, route_bias = phase(row_over, row_cores, route_bias)
    row_diagonal = jnp.concatenate(row_over, axis=0)
    row_core = phase(hop(row_diagonal, 1))[0]
    row_blocks = gathered(normed_two, row_sibling, row_near, row_cores, row_diagonal, row_core)
    gates, gate_grad_first, up_first, hidden_first, in_grad_first = first_call(
        me[None], row_blocks, grad_blocks, route_bias, weights_first, router
    )
    grads_first = lax.psum_scatter(in_grad_first, "dp")

    def second_part(t, *others):
        return second_call(
            t,
            me[None],
            row_blocks,
            grad_blocks,
            gates,
            gate_grad_first,
            after(up_first, *others),
            hidden_first,
            weights_first,
            weights_second,
        )

    far = second_part(3)
    far_cores = hop(far[1], 1), hop(far[3], 1)
    by_y = second_part(2, far[0])
    far_cores, _ = phase(far_cores, by_y[0])
    diagonal = total(far[0], far_cores[0])
    copy_over = reduce_over(diagonal)
    by_y_cores = hop(by_y[1], 1), hop(by_y[3], 1)
    result_diagonal = total(far[2], far_cores[1])
    by_x = second_part(1, diagonal, result_diagonal)
    copy_over, by_y_cores, _, result_diagonal = phase(
        copy_over, by_y_cores, by_x[0], result_diagonal
    )
    result_over, by_x_cores = reduce_over(result_diagonal), (hop(by_x[1], 1), hop(by_x[3], 1))
    own = second_part(0, by_x[0])
    result_over, by_x_cores, _ = phase(result_over, by_x_cores, own[0])
    copy_last = both_call(by_x[0], by_x_cores[0], by_y[0], by_y_cores[0], copy_over)
    last = last_hops(*copy_last)
    own_cores = hop(own[1], 1), hop(own[3], 1)
    result_last = both_call(
        by_x[2], after(by_x_cores[1], *copy_last), by_y[2], by_y_cores[1], result_over
    )
    parts = (own, by_x, by_y, far)
    weight_grads = last_call(
        row_blocks,
        grad_blocks,
        [part[4] for part in parts],
        [part[5] for part in parts],
        after(hidden_first, *result_last, grads_first),
    )
    last, own_cores, weight_grads, result_last = phase(last, own_cores, weight_grads, result_last)
    grads_second = lax.psum_scatter(weight_grads, "dp")
    result_hops = last_hops(*result_last)

    hidden_grad_one, branch_grad, mixed_grad, extras = glue_call(
        token_kernel,
        [
            jax.ShapeDtypeStruct((rows, width), F32),
            jax.ShapeDtypeStruct((rows, width), BF),
            jax.ShapeDtypeStruct((QW, rows), BF),
            jax.ShapeDtypeStruct((EXTRA, D), F32),
        ],
        own[0],
        own_cores[0],
        *last,
        gates,
        router,
        hidden_one,
        factor_two,
        gains,
        own_grad,
        normed_two,
        full_output,
        scalars=0,
    )
    mixed_grad = mixed_grad.reshape(H, HD, rows)
    mixed_grad, branch_grad, extras, hidden_grad_one = phase(
        mixed_grad, branch_grad, extras, hidden_grad_one
    )

    query_grad, pairs_same, pairs_other = attention_call(
        backward_kernel,
        [
            jax.ShapeDtypeStruct((H, HD, rows), F32),
            jax.ShapeDtypeStruct((4, rows, 2 * KW), BF),
            jax.ShapeDtypeStruct((4, rows, 2 * KW), BF),
        ],
        ["head"] + [pl.BlockSpec((4, stretch, 2 * KW), lambda s: (0, s, 0))] * 2,
        queries,
        pairs,
        bias,
        mixed,
        lse,
        mixed_grad,
    )
    query_grad, pairs_same, pairs_other, cosine, sine, result_hops = phase(
        query_grad, pairs_same, pairs_other, cosine, sine, result_hops
    )

    pair_cores = hop(pairs_other, 1)
    output_same, output_other = glue_call(
        output_kernel,
        cut_shapes(shard, D + EXTRA),
        me[None],
        mixed_rows,
        branch_grad,
        extras,
        scratch_shapes=[pltpu.VMEM((QW, D + EXTRA), BF)],
    )
    pair_cores, output_same, output_other = phase(pair_cores, output_same, output_other)

    quarters = (4, 4, rows // 4, 2 * KW)
    pair_sums = sums_call(pairs_same.reshape(quarters), pair_cores.reshape(quarters))
    pair_over, output_cores = over_hops(pair_sums), hop(output_other, 1)
    query_part, query_same, query_other = glue_call(
        query_kernel,
        [jax.ShapeDtypeStruct((QW, rows), BF)] + cut_shapes(shard, QW),
        me[None],
        after(query_grad, *pair_sums),
        cosine,
        sine,
        normed_one,
        scratch_shapes=[pltpu.VMEM((D, QW), BF)],
    )
    pair_over, pair_sums, query_same, query_other, query_part, output_cores = phase(
        pair_over, pair_sums, query_same, query_other, query_part, output_cores
    )

    pair_last = join_call(pair_sums, pair_over)
    pair_hops, query_cores = last_hops(*pair_last), hop(query_other, 1)
    output_sums = sums_call(output_same, after(output_cores, *pair_last))
    output_over = over_hops(output_sums)
    pair_hops, query_cores, output_sums, output_over = phase(
        pair_hops, query_cores, output_sums, output_over
    )

    late_part, late_same, late_other = glue_call(
        late_kernel,
        [jax.ShapeDtypeStruct((2 * KW, rows), BF)] + cut_shapes(shard, 2 * KW),
        me[None],
        *[value.reshape(rows, 2 * KW) for value in (pair_sums[0], *pair_hops)],
        cosine,
        sine,
        normed_one,
        scratch_shapes=[pltpu.VMEM((D, 2 * KW), BF)],
    )
    late_cores = hop(late_other, 1)
    output_last = join_call(output_sums, after(output_over, late_other))
    output_hops = last_hops(*output_last)
    query_sums = sums_call(query_same, after(query_cores, *output_last))
    query_over = over_hops(query_sums)
    output_hops, late_cores, late_same, late_part, query_sums, query_over = phase(
        output_hops, late_cores, late_same, late_part, query_sums, query_over
    )

    late_sums = sums_call(late_same, late_cores)
    late_over = over_hops(late_sums)
    query_last = join_call(query_sums, after(query_over, *late_sums))
    query_hops = last_hops(*query_last)
    input_grad = input_call(
        query_part,
        after(late_part, *query_last),
        full_first,
        inputs,
        factor_one,
        gains,
        hidden_grad_one,
    )
    late_over, query_hops, late_sums, input_grad = phase(
        late_over, query_hops, late_sums, input_grad
    )

    late_last = join_call(late_sums, late_over)
    late_hops = last_hops(*late_last)
    output_own, output_arrived = send_call(
        (output_sums[0], *after(output_hops, *late_last))
    )
    grads_first, grads_second = phase(grads_first, grads_second, output_own, late_last)[:2]
    in_new = adam_call(
        expert_in,
        expert_in_moment,
        expert_in_square,
        [
            (grads_first, 0, [(0, 0, HALF), (HALF, FF, HALF)]),
            (grads_second, 0, [(0, HALF, HALF), (HALF, FF + HALF, HALF)]),
        ],
        3.0 / D**0.5,
        weight_decay,
        ROWS // 4,
    )
    down_new = adam_call(
        expert_down,
        expert_down_moment,
        expert_down_square,
        [
            (grads_second, 4, [(0, 0, 2 * HALF)]),
            (grads_second, 6, [(0, 2 * HALF, 2 * HALF)]),
        ],
        12.0 / FF**0.5,
        weight_decay,
        ROWS // 4,
    )
    late_hops, output_arrived, output_own, in_new, down_new = phase(
        late_hops, output_arrived, output_own, in_new, down_new
    )

    project_own, project_arrived = send_call(
        (query_sums[0], *query_hops), (late_sums[0], *late_hops)
    )
    output_own = after(output_own, project_own)
    sequence = stretch * device_count
    *output_new, output_rest = owned_call(
        output_weight,
        output_moment,
        output_square,
        [output_own, *output_arrived],
        3.0 * (sequence / (32.0 * H * HD)) ** 0.5,
    )
    outputs = hidden_one + reduced(
        total(own[2], after(own_cores[1], output_rest)), result_hops
    )
    rest = output_rest.T
    router_new = [
        new.T
        for new in adam_update(
            router_weight.T,
            router_moment.T,
            router_square.T,
            rest[:expert_count],
            1.5 / D**0.5,
            weight_decay,
        )
    ]
    project_arrived, output_new, rest, outputs, router_new = phase(
        project_arrived, output_new, rest, outputs, router_new
    )
    *project_new, products = owned_call(
        project_weight,
        project_moment,
        project_square,
        [project_own, *project_arrived],
        3.0 * (2.0 / D) ** 0.5,
    )
    own_gains = norm_gains.astype(BF).astype(F32)
    gains_sum = jnp.stack([products[:, 0] / own_gains[0], rest[expert_count]])
    gains_new = adam_update(norm_gains, gains_moment, gains_square, gains_sum, 0.8, 0.0)
    return (
        outputs.reshape(seq_count, stretch, width),
        input_grad.reshape(seq_count, stretch, width),
        *project_new,
        *output_new,
        *router_new,
        *gains_new,
        *in_new,
        *down_new,
    )


def rms_norm(values, gain_row):
    factor = lax.rsqrt(jnp.mean(values * values, axis=-1, keepdims=True) + norm_epsilon)
    return values * factor * gain_row


def rotate(values, positions):
    half_width = values.shape[-1] // 2
    frequency = rope_base ** (-jnp.arange(half_width, dtype=jnp.float32) / half_width)
    angles = positions.astype(jnp.float32)[:, None] * frequency[None, :]
    cosine = jnp.cos(angles)[:, None, :]
    sine_part = jnp.sin(angles)[:, None, :]
    first_half = values[..., :half_width]
    second_half = values[..., half_width:]
    return jnp.concatenate(
        [
            first_half * cosine - second_half * sine_part,
            second_half * cosine + first_half * sine_part,
        ],
        axis=-1,
    )


def gated_unit(gate_up):
    return jax.nn.gelu(gate_up[..., :FF], approximate=True) * gate_up[..., FF:]


def slot_tables(route_block, expert_count, capacity):
    flat_routes = route_block.reshape(-1)
    pick_count = flat_routes.shape[0]
    onehot = (flat_routes[:, None] == jnp.arange(expert_count, dtype=jnp.int32)[None, :]).astype(
        jnp.int32
    )
    earlier = jnp.cumsum(onehot, axis=0) - onehot
    rank_values = jnp.sum(earlier * onehot, axis=1)
    slot_index = flat_routes * capacity + rank_values
    slot_table = (
        jnp.full((expert_count * capacity,), pick_count, jnp.int32)
        .at[slot_index]
        .set(jnp.arange(pick_count, dtype=jnp.int32))
    )
    return (slot_index, slot_table)


def attention_blocks(step_fn, carried, key_values, last_query):
    key_count = key_values.shape[1]
    block_keys = 512

    def one_turn(turn_index, state_now):
        offset = turn_index * block_keys
        key_block = lax.dynamic_slice_in_dim(key_values, offset, block_keys, 1)
        return lax.cond(
            offset > last_query,
            lambda held_state: held_state,
            lambda held_state: step_fn(held_state, key_block, offset),
            state_now,
        )

    return lax.fori_loop(0, key_count // block_keys, one_turn, carried)


def general(
    inputs,
    cotangent,
    routes,
    project_weight,
    project_moment,
    project_square,
    output_weight,
    output_moment,
    output_square,
    router_weight,
    router_moment,
    router_square,
    norm_gains,
    gains_moment,
    gains_square,
    expert_in,
    expert_in_moment,
    expert_in_square,
    expert_down,
    expert_down_moment,
    expert_down_square,
):
    seq_count, stretch_len, model_width = inputs.shape
    expert_devices = lax.axis_size("expert")
    seq_length = stretch_len * expert_devices
    expert_count = EXP_DEV * expert_devices
    row_count = seq_count * stretch_len
    capacity = 2 * row_count * TOP // expert_count
    group_size = H // KVH
    query_width = H * HD
    key_width = KVH * HD
    group_rows = group_size * stretch_len
    score_scale = HD ** (-0.5)
    first_query = lax.axis_index("expert") * stretch_len
    last_query = first_query + stretch_len - 1
    full_project, full_output, full_router, full_gains = (
        lax.all_gather(project_weight.astype(jnp.bfloat16), ("dp", "expert"), axis=0, tiled=True),
        lax.all_gather(output_weight.astype(jnp.bfloat16), ("dp", "expert"), axis=0, tiled=True),
        lax.all_gather(router_weight.astype(jnp.bfloat16), ("dp", "expert"), axis=0, tiled=True),
        lax.all_gather(norm_gains.astype(jnp.bfloat16), ("dp", "expert"), axis=1, tiled=True),
    )
    full_in, full_down = (
        lax.all_gather(expert_in.astype(jnp.bfloat16), "dp", axis=1, tiled=True),
        lax.all_gather(expert_down.astype(jnp.bfloat16), "dp", axis=1, tiled=True),
    )
    gain_values = full_gains.astype(jnp.float32)
    tokens = inputs.astype(jnp.float32).reshape(row_count, model_width)
    normed_one = rms_norm(tokens, gain_values[0]).astype(jnp.bfloat16)
    projected = jnp.dot(normed_one, full_project, preferred_element_type=jnp.float32).reshape(
        seq_count, stretch_len, -1
    )
    positions = first_query + jnp.arange(stretch_len, dtype=jnp.int32)

    def rope_back(gradient):
        unused, pullback = jax.vjp(
            lambda values: rotate(values, positions), jnp.zeros_like(gradient)
        )
        return pullback(gradient)[0]

    queries = rotate(
        projected[..., :query_width].reshape(seq_count, stretch_len, H, HD), positions
    ).astype(jnp.bfloat16)
    rotated_keys = rotate(
        projected[..., query_width : query_width + key_width].reshape(
            seq_count, stretch_len, KVH, HD
        ),
        positions,
    ).astype(jnp.bfloat16)
    values = projected[..., query_width + key_width :].astype(jnp.bfloat16)
    local_pairs = jnp.concatenate(
        [rotated_keys.reshape(seq_count, stretch_len, key_width), values], axis=-1
    )
    all_pairs = lax.all_gather(local_pairs, "expert", axis=1, tiled=True)

    def to_grid(token_rows):
        return (
            token_rows.reshape(seq_count, stretch_len, KVH, group_size, HD)
            .transpose(0, 2, 3, 1, 4)
            .reshape(seq_count, KVH, group_rows, HD)
        )

    def from_grid(grid_rows):
        return (
            grid_rows.reshape(seq_count, KVH, group_size, stretch_len, HD)
            .transpose(0, 3, 1, 2, 4)
            .reshape(row_count, query_width)
        )

    query_grid = to_grid(queries)
    row_positions = first_query + jnp.arange(group_rows, dtype=jnp.int32) % stretch_len

    def scores_for(sequence, key_block, offset):
        key_part = key_block[sequence, :, :key_width].reshape(-1, KVH, HD)
        raw_scores = (
            jnp.einsum(
                "krd,nkd->krn", query_grid[sequence], key_part, preferred_element_type=jnp.float32
            )
            * score_scale
        )
        key_positions = offset + jnp.arange(key_block.shape[1], dtype=jnp.int32)
        allowed = (key_positions[None, :] <= row_positions[:, None])[None]
        return (raw_scores, allowed)

    def stats_step(carried, key_block, offset):
        top_now, total_now = carried
        new_tops = []
        new_totals = []
        for sequence in range(seq_count):
            raw_scores, allowed = scores_for(sequence, key_block, offset)
            masked = jnp.where(allowed, raw_scores, masked_score)
            top_new = jnp.maximum(top_now[sequence], jnp.max(masked, axis=-1))
            weights = jnp.where(allowed, jnp.exp(masked - top_new[..., None]), 0.0)
            new_totals.append(
                total_now[sequence] * jnp.exp(top_now[sequence] - top_new)
                + jnp.sum(weights, axis=-1)
            )
            new_tops.append(top_new)
        return (jnp.stack(new_tops), jnp.stack(new_totals))

    stats_shape = (seq_count, KVH, group_rows)
    top_all, total_all = attention_blocks(
        stats_step,
        (jnp.full(stats_shape, masked_score, jnp.float32), jnp.zeros(stats_shape, jnp.float32)),
        all_pairs,
        last_query,
    )
    log_total = top_all + jnp.log(total_all)

    def softmax_for(sequence, key_block, offset):
        raw_scores, allowed = scores_for(sequence, key_block, offset)
        return jnp.where(
            allowed,
            jnp.exp(jnp.where(allowed, raw_scores, masked_score) - log_total[sequence][..., None]),
            0.0,
        )

    def mix_step(carried, key_block, offset):
        new_rows = []
        for sequence in range(seq_count):
            softmax_rows = softmax_for(sequence, key_block, offset).astype(jnp.bfloat16)
            value_part = key_block[sequence, :, key_width:].reshape(-1, KVH, HD)
            new_rows.append(
                carried[sequence]
                + jnp.einsum(
                    "krn,nkd->krd", softmax_rows, value_part, preferred_element_type=jnp.float32
                )
            )
        return jnp.stack(new_rows)

    mixed_grid = attention_blocks(
        mix_step, jnp.zeros((seq_count, KVH, group_rows, HD), jnp.float32), all_pairs, last_query
    )
    mixed_rows = from_grid(mixed_grid).astype(jnp.bfloat16)
    hidden_one = tokens + jnp.dot(mixed_rows, full_output, preferred_element_type=jnp.float32)
    normed_two = rms_norm(hidden_one, gain_values[1]).astype(jnp.bfloat16)
    logits = jnp.dot(normed_two, full_router, preferred_element_type=jnp.float32)
    route_rows = routes.reshape(row_count, TOP)
    onehot = (
        route_rows[:, :, None] == jnp.arange(expert_count, dtype=jnp.int32)[None, None, :]
    ).astype(jnp.float32)
    gate_weights = jax.nn.softmax(
        jnp.einsum("rte,re->rt", onehot, logits, precision=lax.Precision.HIGHEST), axis=-1
    )
    slot_index, slot_table = slot_tables(route_rows, expert_count, capacity)
    padded = jnp.concatenate([normed_two, jnp.zeros((1, model_width), jnp.bfloat16)], axis=0)
    sent_rows = padded[slot_table // TOP].reshape(expert_count, capacity, model_width)
    arrived_rows = lax.all_to_all(sent_rows, "expert", split_axis=0, concat_axis=0, tiled=True)
    batched = arrived_rows.reshape(expert_devices, EXP_DEV, -1, model_width)
    gate_up = jnp.einsum("neid,edf->neif", batched, full_in, preferred_element_type=jnp.float32)
    hidden = gated_unit(gate_up).astype(jnp.bfloat16)
    result = jnp.einsum(
        "neif,efd->neid", hidden, full_down, preferred_element_type=jnp.float32
    ).astype(jnp.bfloat16)
    results = result.reshape(arrived_rows.shape)
    kept_gate_up = gate_up.reshape(arrived_rows.shape[0], arrived_rows.shape[1], 2 * FF)
    returned = lax.all_to_all(results, "expert", split_axis=0, concat_axis=0, tiled=True)
    picked = returned.reshape(expert_count * capacity, model_width)[slot_index].reshape(
        row_count, TOP, model_width
    )
    picked_wide = picked.astype(jnp.float32)
    mixture = jnp.sum(gate_weights[:, :, None] * picked_wide, axis=1)
    outputs = hidden_one + mixture
    grad_rows = cotangent.astype(jnp.float32).reshape(row_count, model_width)
    gate_grad = jnp.sum(grad_rows[:, None, :] * picked_wide, axis=-1)
    chosen_grad = gate_weights * (
        gate_grad - jnp.sum(gate_weights * gate_grad, axis=-1, keepdims=True)
    )
    logit_grad = jnp.einsum(
        "rte,rt->re", onehot, chosen_grad, precision=lax.Precision.HIGHEST
    ).astype(jnp.bfloat16)
    copy_out_grad = (
        (gate_weights[:, :, None] * grad_rows[:, None, :])
        .astype(jnp.bfloat16)
        .reshape(row_count * TOP, model_width)
    )
    grad_sent = jnp.concatenate([copy_out_grad, jnp.zeros((1, model_width), jnp.bfloat16)], axis=0)[
        slot_table
    ].reshape(expert_count, capacity, model_width)
    grad_arrived = lax.all_to_all(grad_sent, "expert", split_axis=0, concat_axis=0, tiled=True)
    batched_grad = grad_arrived.reshape(expert_devices, EXP_DEV, -1, model_width)
    batched_in = arrived_rows.reshape(expert_devices, EXP_DEV, -1, model_width)
    gate_up = kept_gate_up.reshape(expert_devices, EXP_DEV, -1, 2 * FF)
    hidden, unit_pull = jax.vjp(gated_unit, gate_up)
    grad_down = jnp.einsum(
        "neif,neid->efd",
        hidden.astype(jnp.bfloat16),
        batched_grad,
        preferred_element_type=jnp.float32,
    )
    hidden_grad = jnp.einsum(
        "neid,efd->neif", batched_grad, full_down, preferred_element_type=jnp.float32
    )
    gate_up_grad = unit_pull(hidden_grad)[0].astype(jnp.bfloat16)
    grad_in = jnp.einsum(
        "neid,neif->edf", batched_in, gate_up_grad, preferred_element_type=jnp.float32
    )
    copy_in_grad = (
        jnp.einsum("neif,edf->neid", gate_up_grad, full_in, preferred_element_type=jnp.float32)
        .astype(jnp.bfloat16)
        .reshape(arrived_rows.shape)
    )
    expert_in_grad, expert_down_grad = (
        lax.psum_scatter(
            grad_in.astype(jnp.bfloat16), "dp", scatter_dimension=1, tiled=True
        ).astype(jnp.float32),
        lax.psum_scatter(
            grad_down.astype(jnp.bfloat16), "dp", scatter_dimension=1, tiled=True
        ).astype(jnp.float32),
    )
    returned_grad = lax.all_to_all(copy_in_grad, "expert", split_axis=0, concat_axis=0, tiled=True)
    copies_grad = returned_grad.reshape(expert_count * capacity, model_width)[slot_index].reshape(
        row_count, TOP, model_width
    )
    normed_two_grad = jnp.sum(copies_grad.astype(jnp.float32), axis=1) + jnp.dot(
        logit_grad, full_router.T, preferred_element_type=jnp.float32
    )
    router_grad_full = jnp.einsum(
        "rd,re->de", normed_two, logit_grad, preferred_element_type=jnp.float32
    )
    unused_two, norm_two_pull = jax.vjp(rms_norm, hidden_one, gain_values[1])
    hidden_part, gain_two_grad = norm_two_pull(normed_two_grad)
    hidden_grad_one = grad_rows + hidden_part
    branch_grad = hidden_grad_one.astype(jnp.bfloat16)
    output_grad_full = jnp.einsum(
        "rh,rd->hd", mixed_rows, branch_grad, preferred_element_type=jnp.float32
    )
    mixed_grad = jnp.dot(branch_grad, full_output.T, preferred_element_type=jnp.float32).astype(
        jnp.bfloat16
    )
    mixed_grad_grid = to_grid(mixed_grad.reshape(seq_count, stretch_len, H, HD))
    row_delta = jnp.sum(mixed_grad_grid.astype(jnp.float32) * mixed_grid, axis=-1)

    def back_step(carried, key_block, offset):
        query_grad, pair_grad = carried
        new_query = []
        block_len = key_block.shape[1]
        for sequence in range(seq_count):
            softmax_rows = softmax_for(sequence, key_block, offset)
            key_part = key_block[sequence, :, :key_width].reshape(-1, KVH, HD)
            value_part = key_block[sequence, :, key_width:].reshape(-1, KVH, HD)
            softmax_grad = jnp.einsum(
                "krd,nkd->krn",
                mixed_grad_grid[sequence],
                value_part,
                preferred_element_type=jnp.float32,
            )
            score_grad = (softmax_rows * (softmax_grad - row_delta[sequence][..., None])).astype(
                jnp.bfloat16
            )
            new_query.append(
                query_grad[sequence]
                + jnp.einsum(
                    "krn,nkd->krd", score_grad, key_part, preferred_element_type=jnp.float32
                )
                * score_scale
            )
            key_grad = (
                jnp.einsum(
                    "krn,krd->nkd",
                    score_grad,
                    query_grid[sequence],
                    preferred_element_type=jnp.float32,
                )
                * score_scale
            )
            value_grad = jnp.einsum(
                "krn,krd->nkd",
                softmax_rows.astype(jnp.bfloat16),
                mixed_grad_grid[sequence],
                preferred_element_type=jnp.float32,
            )
            block_grad = jnp.concatenate(
                [key_grad.reshape(block_len, key_width), value_grad.reshape(block_len, key_width)],
                axis=-1,
            )
            current = lax.dynamic_slice(
                pair_grad,
                (jnp.int32(sequence), offset, jnp.int32(0)),
                (1, block_len, 2 * key_width),
            )
            pair_grad = lax.dynamic_update_slice(
                pair_grad, current + block_grad[None], (jnp.int32(sequence), offset, jnp.int32(0))
            )
        return (jnp.stack(new_query), pair_grad)

    query_start = jnp.zeros((seq_count, KVH, group_rows, HD), jnp.float32)
    pair_start = jnp.zeros((seq_count, seq_length, 2 * key_width), jnp.float32)
    query_grad_grid, pair_grad_all = attention_blocks(
        back_step, (query_start, pair_start), all_pairs, last_query
    )
    pair_grad_local = lax.psum_scatter(
        pair_grad_all.astype(jnp.bfloat16), "expert", scatter_dimension=1, tiled=True
    ).astype(jnp.float32)
    query_grad_rows = rope_back(from_grid(query_grad_grid).reshape(seq_count, stretch_len, H, HD))
    key_grad_rows = rope_back(
        pair_grad_local[..., :key_width].reshape(seq_count, stretch_len, KVH, HD)
    )
    projected_grad = jnp.concatenate(
        [
            query_grad_rows.reshape(row_count, query_width),
            key_grad_rows.reshape(row_count, key_width),
            pair_grad_local[..., key_width:].reshape(row_count, key_width),
        ],
        axis=-1,
    ).astype(jnp.bfloat16)
    project_grad_full = jnp.einsum(
        "rd,rf->df", normed_one, projected_grad, preferred_element_type=jnp.float32
    )
    normed_one_grad = jnp.dot(projected_grad, full_project.T, preferred_element_type=jnp.float32)
    unused_one, norm_one_pull = jax.vjp(rms_norm, tokens, gain_values[0])
    token_part, gain_one_grad = norm_one_pull(normed_one_grad)
    input_grad = hidden_grad_one + token_part
    gains_grad_full = jnp.stack([gain_one_grad, gain_two_grad])
    project_grad, output_grad, router_grad, gains_grad = (
        lax.psum_scatter(project_grad_full, ("dp", "expert"), scatter_dimension=0, tiled=True),
        lax.psum_scatter(output_grad_full, ("dp", "expert"), scatter_dimension=0, tiled=True),
        lax.psum_scatter(router_grad_full, ("dp", "expert"), scatter_dimension=0, tiled=True),
        lax.psum_scatter(gains_grad_full, ("dp", "expert"), scatter_dimension=1, tiled=True),
    )
    rate_project = 3.0 * (2.0 / D) ** 0.5
    rate_output = 3.0 * (seq_length / (32.0 * H * HD)) ** 0.5
    rate_router = 1.5 / D**0.5
    rate_gains = 0.8
    rate_in = 3.0 / D**0.5
    rate_down = 12.0 / FF**0.5
    project_new = adam_update(
        project_weight, project_moment, project_square, project_grad, rate_project, weight_decay
    )
    output_new = adam_update(
        output_weight, output_moment, output_square, output_grad, rate_output, weight_decay
    )
    router_new = adam_update(
        router_weight, router_moment, router_square, router_grad, rate_router, weight_decay
    )
    gains_new = adam_update(norm_gains, gains_moment, gains_square, gains_grad, rate_gains, 0.0)
    in_new = adam_update(
        expert_in, expert_in_moment, expert_in_square, expert_in_grad, rate_in, weight_decay
    )
    down_new = adam_update(
        expert_down,
        expert_down_moment,
        expert_down_square,
        expert_down_grad,
        rate_down,
        weight_decay,
    )
    return (
        outputs.reshape(seq_count, stretch_len, model_width),
        input_grad.reshape(seq_count, stretch_len, model_width),
        project_new[0],
        project_new[1],
        project_new[2],
        output_new[0],
        output_new[1],
        output_new[2],
        router_new[0],
        router_new[1],
        router_new[2],
        gains_new[0],
        gains_new[1],
        gains_new[2],
        in_new[0],
        in_new[1],
        in_new[2],
        down_new[0],
        down_new[1],
        down_new[2],
    )


def solution(mesh):
    token_spec = P("dp", "expert", None)
    row_spec = P(("dp", "expert"), None)
    gain_spec = P(None, ("dp", "expert"))
    expert_spec = P("expert", "dp", None)
    states = (row_spec,) * 9 + (gain_spec,) * 3 + (expert_spec,) * 6
    small = mesh.shape["dp"] == 4 and mesh.shape["expert"] == 8
    return jax.shard_map(
        local if small else general,
        mesh=mesh,
        in_specs=(token_spec, token_spec, P(("dp", "expert"), None, None)) + states,
        out_specs=(token_spec, token_spec) + states,
        check_vma=False,
    )
```

```python
import jax
import jax.numpy as jnp
from jax import lax
from jax.experimental import pallas as pl
from jax.experimental.pallas import tpu as pltpu
from jax.sharding import PartitionSpec as P

D = 1536
H = 12
KVH = 2
HD = 128
FF = 768
TOP = 4
STEP = 10
GROUP = H // KVH
QW = H * HD
KW = KVH * HD
QKV = QW + 2 * KW
EXP_DEV = 1
EXTRA = 128

norm_epsilon = 1e-06
adam_epsilon = 1e-08
beta_first = 0.9
beta_second = 0.95
weight_decay = 0.1
rope_base = 1000000.0
masked_score = -1e30
score_scale = HD ** (-0.5)
BF = jnp.bfloat16
F32 = jnp.float32
VMEM_BYTES = 50 * 1024 * 1024
HINT = pl.CostEstimate(flops=0, bytes_accessed=0, transcendentals=0)


def dot(a, b, da, db):
    return lax.dot_general(a, b, (((da,), (db,)), ((), ())), preferred_element_type=F32)


def after(value, *others):
    return lax.optimization_barrier((value, *others))[0]


def bring(pairs, sems):
    copies = [pltpu.make_async_copy(a, b, sems.at[n]) for n, (a, b) in enumerate(pairs)]
    for copy in copies:
        copy.start()
    return copies


def glue_call(kernel, out_shape, *operands, scalars=1, **options):
    vmem = pl.BlockSpec(memory_space=pltpu.VMEM)
    options.setdefault(
        "in_specs",
        [pl.BlockSpec(memory_space=pltpu.SMEM)] * scalars + [vmem] * (len(operands) - scalars),
    )
    options.setdefault("out_specs", [vmem] * len(out_shape))
    return pl.pallas_call(
        kernel,
        out_shape=out_shape,
        compiler_params=pltpu.CompilerParams(vmem_limit_bytes=VMEM_BYTES),
        cost_estimate=HINT,
        **options,
    )(*operands)


def plane_kernel(place_ref, *refs):
    blocks, out_ref, sems = refs[:4], refs[4], refs[5]
    moves = [
        (block, out_ref.at[lax.rem(place_ref[0] + step, 4)]) for step, block in enumerate(blocks)
    ]
    for copy in bring(moves, sems):
        copy.wait()


def plane_end(blocks):
    anywhere = pl.BlockSpec(memory_space=pl.ANY)
    return glue_call(
        plane_kernel,
        [jax.ShapeDtypeStruct((4,) + blocks[0].shape, BF)],
        lax.axis_index("dp")[None],
        *blocks,
        in_specs=[pl.BlockSpec(memory_space=pltpu.SMEM)] + [anywhere] * 4,
        out_specs=[anywhere],
        scratch_shapes=[pltpu.SemaphoreType.DMA((4,))],
    )[0]


def halves_kernel(by_x_ref, by_y_ref, low_ref, high_ref, sems):
    half = low_ref.shape[0]
    moves = [(by_x_ref.at[pl.ds(0, half)], low_ref), (by_y_ref.at[pl.ds(half, half)], high_ref)]
    for copy in bring(moves, sems):
        copy.wait()


def halves_call(near):
    anywhere = pl.BlockSpec(memory_space=pl.ANY)
    half = jax.ShapeDtypeStruct((near[0].shape[0] // 2, *near[0].shape[1:]), BF)
    return glue_call(
        halves_kernel,
        [half, half],
        *near,
        in_specs=[anywhere] * 2,
        out_specs=[anywhere] * 2,
        scratch_shapes=[pltpu.SemaphoreType.DMA((2,))],
    )


def hop(value, mask):
    return lax.ppermute(value, "expert", [(i, i ^ mask) for i in range(8)])


def total(one, two):
    return (one.astype(F32) + two.astype(F32)).astype(one.dtype)


def gather_near(value):
    return hop(value, 2), hop(value, 4)


def gather_over(near):
    low, high = halves_call(near)
    by_x, by_y, _, _ = phase(*near, low, high)
    return (hop(low, 4), hop(high, 2)), (by_x, by_y)


def gather_cores(near):
    return hop(near[0], 1), hop(near[1], 1)


def gathered(value, sibling, near, cores, diagonal, diagonal_core):
    return [value, sibling, near[0], cores[0], near[1], cores[1], diagonal, diagonal_core]


def reduce_over(diagonal):
    half = diagonal.shape[0] // 2
    return hop(diagonal[:half], 2), hop(diagonal[half:], 4)


def last_hops(by_x, by_y):
    return hop(by_x, 2), hop(by_y, 4)


def reduced(own, last):
    return own.astype(F32) + last[0].astype(F32) + last[1].astype(F32)


def phase(*values):
    return lax.optimization_barrier(values)


def plane_hop(shard, step):
    return lax.ppermute(shard, "dp", [((i + step) % 4, i) for i in range(4)])


def key_block(kv_ref, row):
    return jnp.concatenate(
        [kv_ref[n, row : row + HD, :].astype(F32).T for n in range(kv_ref.shape[0])], axis=0
    ).astype(BF)


def two(ref, h):
    return jnp.concatenate([ref[h], ref[h + 1]], axis=1)


def forward_kernel(q_ref, kv_ref, bias_ref, mixed_ref, lse_ref):
    stretch = bias_ref.shape[1]
    bias = jnp.concatenate([bias_ref[...]] * 2, axis=1)
    for g in range(KVH):
        keys = key_block(kv_ref, g * HD)
        values = jnp.concatenate(
            [kv_ref[n, KW + g * HD : KW + (g + 1) * HD, :] for n in range(kv_ref.shape[0])], axis=1
        )
        for h in range(g * GROUP, (g + 1) * GROUP, 2):
            scores = dot(keys, two(q_ref, h), 1, 0) * score_scale + bias
            top = jnp.max(scores, axis=0, keepdims=True)
            weights = jnp.exp(scores - top)
            amount = jnp.sum(weights, axis=0, keepdims=True)
            mixed = dot(values, weights.astype(BF), 1, 0) / amount
            lse = top + jnp.log(amount)
            for n in range(2):
                part = slice(n * stretch, (n + 1) * stretch)
                mixed_ref[h + n] = mixed[:, part]
                lse_ref[0, h + n : h + n + 1, :] = lse[:, part]


def backward_kernel(q_ref, kv_ref, bias_ref, mixed_ref, lse_ref, grad_ref, dq_ref, same_ref, other_ref):
    blocks, stretch = kv_ref.shape[0], kv_ref.shape[2]
    bias = jnp.concatenate([bias_ref[...]] * 2, axis=1)
    for g in range(KVH):
        keys, values = key_block(kv_ref, g * HD), key_block(kv_ref, KW + g * HD)
        keys_flat = jnp.concatenate(
            [kv_ref[n, g * HD : (g + 1) * HD, :] for n in range(blocks)], axis=1
        )
        key_grad = jnp.zeros(keys.shape, F32)
        value_grad = jnp.zeros(keys.shape, F32)
        for h in range(g * GROUP, (g + 1) * GROUP, 2):
            query, grad = two(q_ref, h), two(grad_ref, h)
            lse = jnp.concatenate([lse_ref[0, h : h + 1, :], lse_ref[0, h + 1 : h + 2, :]], axis=1)
            scores = dot(keys, query, 1, 0) * score_scale + bias
            probs = jnp.exp(scores - lse)
            delta = jnp.sum(two(mixed_ref, h) * grad.astype(F32), axis=0, keepdims=True)
            score_grad = (probs * (dot(values, grad, 1, 0) - delta)).astype(BF)
            query_grad = dot(keys_flat, score_grad, 1, 0) * score_scale
            for n in range(2):
                dq_ref[h + n] = query_grad[:, n * stretch : (n + 1) * stretch]
            key_grad += dot(score_grad, query, 1, 1)
            value_grad += dot(probs.astype(BF), grad, 1, 1)
        key_grad = (key_grad * score_scale).astype(BF)
        value_grad = value_grad.astype(BF)
        for n in range(blocks):
            part, ref = slice(n * stretch, (n + 1) * stretch), (same_ref, other_ref)[n % 2]
            ref[n // 2, :, g * HD : (g + 1) * HD] = key_grad[part]
            ref[n // 2, :, KW + g * HD : KW + (g + 1) * HD] = value_grad[part]


def attention_call(kernel, outs, out_specs, queries, pairs, bias, *more):
    blocks, _, tokens = pairs.shape
    stretch = bias.shape[1]
    head = pl.BlockSpec((H, HD, stretch), lambda s: (0, 0, s))
    row = pl.BlockSpec((1, H, stretch), lambda s: (s, 0, 0))
    specs = [
        head,
        pl.BlockSpec((blocks, 2 * KW, stretch), lambda s: (0, 0, s)),
        pl.BlockSpec(bias.shape, lambda s: (0, 0)),
        head,
        row,
        head,
    ]
    keys = blocks * stretch
    return pl.pallas_call(
        kernel,
        grid=(tokens // stretch,),
        in_specs=specs[: 3 + len(more)],
        out_specs=[head if s == "head" else row if s == "row" else s for s in out_specs],
        out_shape=outs,
        compiler_params=pltpu.CompilerParams(vmem_limit_bytes=56 * 1024 * 1024),
        cost_estimate=HINT,
    )(queries, pairs, bias, *more)


HALF = FF // 2
ROWS = D // 4
DOWN = FF // 4


def inner(weight_ref):
    return jnp.concatenate([weight_ref[a, :ROWS] for a in range(4)], axis=0)


def outer(first_ref, half=None):
    owners = range(4) if half is None else (2 * half, 2 * half + 1)
    return jnp.concatenate(
        [
            jnp.concatenate(
                [first_ref[a, ROWS : ROWS + DOWN], first_ref[a, ROWS + DOWN :]], axis=1
            )
            for a in owners
        ],
        axis=0,
    )


def gates_for(me_ref, gates):
    lanes = lax.broadcasted_iota(jnp.int32, gates.shape, 1)
    return jnp.sum(jnp.where(lanes == me_ref[0], gates, 0.0), axis=1, keepdims=True)


def back_kernel(*refs):
    number = len(refs) - 7
    grads_in, (first, back_out, grads_v, outer_v, back_v, in_sems, out_sems) = (
        refs[:number],
        refs[number:],
    )
    count = grads_in[0].shape[0]
    moves = [(first.at[:, pl.ds(ROWS, 2 * DOWN)], outer_v)]
    for k in range(number):
        moves.append((grads_in[k], grads_v.at[k // 2, pl.ds((k % 2) * count, count)]))
    arriving = bring(moves, in_sems)
    arriving[0].wait()
    weight = jnp.concatenate(
        [jnp.concatenate([outer_v[a, :DOWN], outer_v[a, DOWN:]], axis=1) for a in range(4)], axis=0
    )
    leaving = []
    for t in range(number // 2):
        for copy in arriving[1 + 2 * t : 3 + 2 * t]:
            copy.wait()
        back_v[t] = dot(grads_v[t], weight, 1, 1).astype(BF)
        leaving += bring([(back_v.at[t], back_out.at[t])], out_sems.at[pl.ds(t, 1)])
    for copy in leaving:
        copy.wait()


def back_call(grads, first):
    count, width = grads[0].shape
    tiles = len(grads) // 2
    anywhere = pl.BlockSpec(memory_space=pl.ANY)
    return glue_call(
        back_kernel,
        [jax.ShapeDtypeStruct((tiles, 2 * count, FF), BF)],
        *grads,
        first,
        in_specs=[anywhere] * (len(grads) + 1),
        out_specs=[anywhere],
        scratch_shapes=[
            pltpu.VMEM((tiles, 2 * count, width), BF),
            pltpu.VMEM((4, 2 * DOWN, 2 * HALF), BF),
            pltpu.VMEM((tiles, 2 * count, FF), BF),
            pltpu.SemaphoreType.DMA((2 * tiles + 1,)),
            pltpu.SemaphoreType.DMA((tiles,)),
        ],
    )[0]


def first_kernel(me_ref, *refs):
    rows_in, back_near, back_far, bias_ref, first_in, router_ref = refs[:8], *refs[8:13]
    gates_out, gate_grad_out, gate_up_out, hidden_out, weight_out = refs[13:18]
    rows_v, back_v, inner_v, gate_up_v, hidden_v, weight_v, in_sems, out_sems = refs[18:]
    count = rows_in[0].shape[0]
    moves = [(first_in.at[:, pl.ds(0, ROWS)], inner_v)]
    for k in range(8):
        t, part = k // 2, pl.ds((k % 2) * count, count)
        moves.append((rows_in[k], rows_v.at[t, part]))
        if k % 2:
            source = back_near.at[t] if t < 3 else back_far.at[0]
            moves.append((source.at[:, pl.ds(0, HALF)], back_v.at[t]))
    arriving = bring(moves, in_sems)
    arriving.pop(0).wait()
    weight = inner_v[...].reshape(D, 2 * HALF)
    leaving = []
    for t in range(4):
        part = slice(t * 2 * count, (t + 1) * 2 * count)
        for copy in arriving[3 * t : 3 * t + 3]:
            copy.wait()
        rows = rows_v[t]
        logits = dot(rows, router_ref[...], 1, 0) + bias_ref[part]
        exps = jnp.exp(logits - jnp.max(logits, axis=1, keepdims=True))
        gates = exps / jnp.sum(exps, axis=1, keepdims=True)
        gates_out[part] = gates
        mine = gates_for(me_ref, gates)
        gate_up = dot(rows, weight, 1, 0)
        hidden, slope_gate, slope_up = gated(gate_up[:, :HALF], gate_up[:, HALF:])
        hidden_grad = back_v[t].astype(F32)
        hidden = hidden.astype(BF).astype(F32)
        gate_grad = jnp.sum(hidden * hidden_grad, axis=1, keepdims=True)
        gate_grad_out[part] = jnp.broadcast_to(gate_grad, (2 * count, EXTRA))
        hidden_grad = hidden_grad * mine
        gate_up_v[t, :, :HALF] = (hidden_grad * slope_gate).astype(BF)
        gate_up_v[t, :, HALF:] = (hidden_grad * slope_up).astype(BF)
        hidden_v[t] = (mine * hidden).astype(BF)
        pairs = [(gate_up_v.at[t], gate_up_out.at[t]), (hidden_v.at[t], hidden_out.at[t])]
        leaving += bring(pairs, out_sems.at[pl.ds(2 * t, 2)])
    gate_up = gate_up_v[...].reshape(8 * count, 2 * HALF)
    for a in range(4):
        rows = rows_v[:, :, a * ROWS : (a + 1) * ROWS].reshape(8 * count, ROWS)
        weight_v[a] = dot(rows, gate_up, 0, 0).astype(BF)
        leaving += bring([(weight_v.at[a], weight_out.at[a])], out_sems.at[pl.ds(8 + a, 1)])
    for copy in leaving:
        copy.wait()


def first_call(me, rows, back, bias, first, router):
    count, width = rows[0].shape
    shape = jax.ShapeDtypeStruct
    vmem, anywhere = pl.BlockSpec(memory_space=pltpu.VMEM), pl.BlockSpec(memory_space=pl.ANY)
    return pl.pallas_call(
        first_kernel,
        in_specs=[pl.BlockSpec(memory_space=pltpu.SMEM)]
        + [anywhere] * 10
        + [vmem, anywhere, vmem],
        out_specs=[vmem] * 2 + [anywhere] * 3,
        out_shape=[shape((8 * count, EXTRA), F32)] * 2
        + [
            shape((4, 2 * count, 2 * HALF), BF),
            shape((4, 2 * count, HALF), BF),
            shape((4, ROWS, 2 * HALF), BF),
        ],
        scratch_shapes=[
            pltpu.VMEM((4, 2 * count, width), BF),
            pltpu.VMEM((4, 2 * count, HALF), BF),
            pltpu.VMEM((4, ROWS, 2 * HALF), BF),
            pltpu.VMEM((4, 2 * count, 2 * HALF), BF),
            pltpu.VMEM((4, 2 * count, HALF), BF),
            pltpu.VMEM((4, ROWS, 2 * HALF), BF),
            pltpu.SemaphoreType.DMA((13,)),
            pltpu.SemaphoreType.DMA((12,)),
        ],
        compiler_params=pltpu.CompilerParams(vmem_limit_bytes=VMEM_BYTES),
        cost_estimate=HINT,
    )(me, *rows, *back, bias, first, router)


def second_kernel(t, me_ref, *refs):
    row0, row1, back, gates_in, gate_grad_in, up_in, hidden_in, first, second = refs[:9]
    outs = refs[9:15]
    rows_v, back_v, gates_v, gate_grad_v, up_v, hidden_v, inner0_v, inner1_v, outer_v = refs[15:24]
    out_v, result_v, up_out, hidden_out, sems, out_sems = refs[24:]
    count = row0.shape[0]
    low, high, part = pl.ds(0, count), pl.ds(count, count), pl.ds(t * 2 * count, 2 * count)
    moves = [
        (row0, rows_v.at[low]),
        (row1, rows_v.at[high]),
        (second, inner1_v),
        (back.at[t % 3, :, pl.ds(HALF, HALF)], back_v),
        (first.at[:, pl.ds(ROWS, 2 * DOWN)], outer_v),
        (gates_in.at[part], gates_v),
        (gate_grad_in.at[part], gate_grad_v),
        (up_in.at[t], up_v),
        (first.at[:, pl.ds(0, ROWS)], inner0_v),
        (hidden_in.at[t], hidden_v),
    ]
    arriving = bring(moves, sems)
    for copy in arriving[:3]:
        copy.wait()
    inner1 = inner1_v[...].reshape(D, 2 * HALF)
    gate_up = dot(rows_v[...], inner1, 1, 0)
    for copy in arriving[3:]:
        copy.wait()
    outer0, outer1 = [
        jnp.concatenate(
            [jnp.concatenate([outer_v[a, :DOWN], outer_v[a, DOWN:]], axis=1) for a in owners], axis=0
        )
        for owners in ((0, 1), (2, 3))
    ]
    hidden_grad = back_v[...].astype(F32)
    copies = dot(up_v[...], inner0_v[...].reshape(D, 2 * HALF), 1, 1)
    result = dot(hidden_v[...], outer0, 1, 0)
    hidden, slope_gate, slope_up = gated(gate_up[:, :HALF], gate_up[:, HALF:])
    mine = gates_for(me_ref, gates_v[...])
    hidden = hidden.astype(BF).astype(F32)
    gate_grad = gate_grad_v[...] + jnp.sum(hidden * hidden_grad, axis=1, keepdims=True)
    hidden_grad = hidden_grad * mine
    up_out[:, :HALF] = (hidden_grad * slope_gate).astype(BF)
    up_out[:, HALF:] = (hidden_grad * slope_up).astype(BF)
    hidden_out[...] = (mine * hidden).astype(BF)
    leaving = bring([(up_out, outs[4]), (hidden_out, outs[5])], out_sems.at[pl.ds(0, 2)])
    copies = (copies + dot(up_out[...], inner1, 1, 1)).astype(BF)
    lanes = lax.broadcasted_iota(jnp.int32, (2 * count, EXTRA), 1)
    rounded = gate_grad.astype(BF).astype(F32)
    columns = (
        jnp.where(lanes == me_ref[0], rounded, 0.0)
        + jnp.where(lanes == me_ref[0] + 8, gate_grad - rounded, 0.0)
    ).astype(BF)
    for n in range(2):
        out_v[n, :, :D] = copies[n * count : (n + 1) * count]
        out_v[n, :, D:] = columns[n * count : (n + 1) * count]
    leaving += bring(
        [(out_v.at[1], outs[1]), (out_v.at[0], outs[0])], out_sems.at[pl.ds(2, 2)]
    )
    result = (result + dot(hidden_out[...], outer1, 1, 0)).astype(BF)
    for n in range(2):
        result_v[n] = result[n * count : (n + 1) * count]
    leaving += bring(
        [(result_v.at[1], outs[3]), (result_v.at[0], outs[2])], out_sems.at[pl.ds(4, 2)]
    )
    for copy in leaving:
        copy.wait()


def second_call(t, me, rows, back, gates, gate_grad, up_first, hidden_first, first, second):
    count, width = rows[0].shape
    shape = jax.ShapeDtypeStruct
    anywhere = pl.BlockSpec(memory_space=pl.ANY)
    return pl.pallas_call(
        lambda *refs: second_kernel(t, *refs),
        in_specs=[pl.BlockSpec(memory_space=pltpu.SMEM)] + [anywhere] * 9,
        out_specs=[pl.BlockSpec(memory_space=pltpu.HBM)] * 6,
        out_shape=[shape((count, D + EXTRA), BF)] * 2
        + [shape((count, D), BF)] * 2
        + [shape((2 * count, 2 * HALF), BF), shape((2 * count, HALF), BF)],
        scratch_shapes=[
            pltpu.VMEM((2 * count, width), BF),
            pltpu.VMEM((2 * count, HALF), BF),
            pltpu.VMEM((2 * count, EXTRA), F32),
            pltpu.VMEM((2 * count, EXTRA), F32),
            pltpu.VMEM((2 * count, 2 * HALF), BF),
            pltpu.VMEM((2 * count, HALF), BF),
            pltpu.VMEM((4, ROWS, 2 * HALF), BF),
            pltpu.VMEM((4, ROWS, 2 * HALF), BF),
            pltpu.VMEM((4, 2 * DOWN, 2 * HALF), BF),
            pltpu.VMEM((2, count, D + EXTRA), BF),
            pltpu.VMEM((2, count, D), BF),
            pltpu.VMEM((2 * count, 2 * HALF), BF),
            pltpu.VMEM((2 * count, HALF), BF),
            pltpu.SemaphoreType.DMA((10,)),
            pltpu.SemaphoreType.DMA((6,)),
        ],
        compiler_params=pltpu.CompilerParams(vmem_limit_bytes=VMEM_BYTES),
        cost_estimate=HINT,
    )(
        me,
        *rows[2 * t : 2 * t + 2],
        back[t // 3],
        gates,
        gate_grad,
        up_first,
        hidden_first,
        first,
        second,
    )


def last_kernel(*refs):
    rows_in, grads_in, ups, hiddens = refs[:8], refs[8:16], refs[16:20], refs[20:24]
    hidden0, out_ref, rows_v, grads_v, up_v, hidden0_v, hidden1_v, out_v, in_sems, out_sems = refs[24:]
    count = rows_in[0].shape[0]
    arriving = bring(
        [(ref, grads_v.at[pl.ds(k * count, count)]) for k, ref in enumerate(grads_in)]
        + [(hidden0, hidden0_v)]
        + [(ref, hidden1_v.at[t]) for t, ref in enumerate(hiddens)]
        + [(ref, rows_v.at[pl.ds(k * count, count)]) for k, ref in enumerate(rows_in)]
        + [(ref, up_v.at[t]) for t, ref in enumerate(ups)],
        in_sems,
    )
    for copy in arriving[:9]:
        copy.wait()
    grads = grads_v[...]
    for half, ref in enumerate((hidden0_v, hidden1_v)):
        if half:
            for copy in arriving[9:13]:
                copy.wait()
        sums = dot(ref[...].reshape(8 * count, HALF), grads, 0, 0).astype(BF)
        for n in range(2):
            for side in range(2):
                out_v[2 * half + n, ROWS + side * DOWN : ROWS + (side + 1) * DOWN] = sums[
                    n * DOWN : (n + 1) * DOWN, side * 2 * HALF : (side + 1) * 2 * HALF
                ]
    for copy in arriving[13:]:
        copy.wait()
    leaving = []
    gate_up = up_v[...].reshape(8 * count, 2 * HALF)
    for a in range(4):
        out_v[a, :ROWS] = dot(rows_v[:, a * ROWS : (a + 1) * ROWS], gate_up, 0, 0).astype(BF)
        leaving += bring([(out_v.at[a], out_ref.at[a])], out_sems.at[pl.ds(a, 1)])
    for copy in leaving:
        copy.wait()


def last_call(rows, grads, ups, hiddens, hidden0):
    count, width = rows[0].shape
    anywhere = pl.BlockSpec(memory_space=pl.ANY)
    whole = (4, ROWS + 2 * DOWN, 2 * HALF)
    return pl.pallas_call(
        last_kernel,
        in_specs=[anywhere] * 25,
        out_specs=anywhere,
        out_shape=jax.ShapeDtypeStruct(whole, BF),
        scratch_shapes=[
            pltpu.VMEM((8 * count, width), BF),
            pltpu.VMEM((8 * count, width), BF),
            pltpu.VMEM((4, 2 * count, 2 * HALF), BF),
            pltpu.VMEM((4, 2 * count, HALF), BF),
            pltpu.VMEM((4, 2 * count, HALF), BF),
            pltpu.VMEM(whole, BF),
            pltpu.SemaphoreType.DMA((25,)),
            pltpu.SemaphoreType.DMA((4,)),
        ],
        compiler_params=pltpu.CompilerParams(vmem_limit_bytes=VMEM_BYTES),
        cost_estimate=HINT,
    )(*rows, *grads, *ups, *hiddens, hidden0)


def rms_factor(values):
    return lax.rsqrt(jnp.mean(values * values, axis=-1, keepdims=True) + norm_epsilon)


def rms_back(gradient, values, factor, gain):
    scaled = gradient * gain
    inner = jnp.mean(scaled * values, axis=-1, keepdims=True)
    return (
        factor * scaled - values * (factor * factor * factor * inner),
        jnp.sum(gradient * values * factor, axis=0),
    )


def turn(heads, cosine, sine):
    half = HD // 2
    first, second = heads[:, :half], heads[:, half:]
    return jnp.concatenate(
        [first * cosine - second * sine, second * cosine + first * sine], axis=1
    )


def adam_update(weight, moment, square, gradient, step_rate, shrink):
    moment_new = beta_first * moment + (1.0 - beta_first) * gradient
    square_new = beta_second * square + (1.0 - beta_second) * gradient * gradient
    normalized = (
        moment_new
        / (1.0 - beta_first**STEP)
        / (jnp.sqrt(square_new / (1.0 - beta_second**STEP)) + adam_epsilon)
    )
    return (moment_new, square_new, weight - step_rate * (normalized + shrink * weight))


def assemble(me_ref, refs, weight_v, whole_ref, sems, out_sem):
    rows = refs[0].shape[1]
    moves = []
    for k in range(8):
        for a in range(4):
            if k < 6:
                source = refs[k].at[a]
            else:
                source = refs[2 * k - 6 + a // 2].at[a % 2]
            start = pl.multiple_of((a * 8 + (me_ref[0] ^ k)) * rows, 16)
            moves.append((source, weight_v.at[pl.ds(start, rows)]))
    for copy in bring(moves, sems):
        copy.wait()
    return bring([(weight_v, whole_ref)], out_sem)[0]


def project_kernel(me_ref, *refs):
    blocks, (inputs_ref, cosine_ref, sine_ref, routes_ref) = refs[:10], refs[10:14]
    query_ref, pair_ref, normed_ref, factor_ref, gains_ref, router_ref, whole_ref = refs[14:21]
    weight_v, sems, out_sem = refs[21:]
    leaving = assemble(me_ref, blocks, weight_v, whole_ref, sems, out_sem)
    extras = weight_v[:, QKV:]
    lanes = lax.broadcasted_iota(jnp.int32, extras.shape, 1)
    router_ref[...] = jnp.where(lanes < 8, extras.astype(F32), 0.0).astype(BF)
    gains = extras.astype(F32).T[8:16]
    gains_ref[...] = gains
    tokens = inputs_ref[...].astype(F32)
    factor = rms_factor(tokens)
    factor_ref[...] = factor
    normed = (tokens * factor * gains[:1]).astype(BF)
    normed_ref[...] = normed
    projected = dot(normed, weight_v[:, :QKV], 1, 0)
    half = HD // 2
    cosine, sine = cosine_ref[...], sine_ref[...]
    for h in range(H + KVH):
        head = projected[:, h * HD : (h + 1) * HD].T
        first, second = head[:half], head[half:]
        head = jnp.concatenate(
            [first * cosine - second * sine, second * cosine + first * sine], axis=0
        ).astype(BF)
        if h < H:
            query_ref[h] = head
        else:
            pair_ref[(h - H) * HD : (h - H + 1) * HD] = head
    for h in range(KVH):
        start = QW + KW + h * HD
        pair_ref[KW + h * HD : KW + (h + 1) * HD] = projected[:, start : start + HD].T.astype(BF)
    pair_ref[2 * KW :] = routes_ref[...]
    leaving.wait()


def attended_kernel(me_ref, *refs):
    blocks, (mixed_ref, inputs_ref, gains_ref) = refs[:10], refs[10:13]
    hidden_ref, normed_ref, factor_ref, rows_ref, whole_ref, weight_v, sems, out_sem = refs[13:]
    leaving = assemble(me_ref, blocks, weight_v, whole_ref, sems, out_sem)
    rows_ref[...] = mixed_ref[...].reshape(rows_ref.shape).astype(BF)
    hidden = inputs_ref[...].astype(F32) + dot(rows_ref[...], weight_v[...], 0, 0)
    factor = rms_factor(hidden)
    hidden_ref[...] = hidden
    factor_ref[...] = factor
    normed_ref[...] = (hidden * factor * gains_ref[1:2]).astype(BF)
    leaving.wait()


def assembled_call(kernel, out_shape, whole_shape, me, blocks, *operands):
    vmem, anywhere = pl.BlockSpec(memory_space=pltpu.VMEM), pl.BlockSpec(memory_space=pl.ANY)
    return glue_call(
        kernel,
        [*out_shape, jax.ShapeDtypeStruct(whole_shape, BF)],
        me,
        *blocks,
        *operands,
        in_specs=[pl.BlockSpec(memory_space=pltpu.SMEM)]
        + [anywhere] * len(blocks)
        + [vmem] * len(operands),
        out_specs=[vmem] * len(out_shape) + [anywhere],
        scratch_shapes=[
            pltpu.VMEM(whole_shape, BF),
            pltpu.SemaphoreType.DMA((32,)),
            pltpu.SemaphoreType.DMA((1,)),
        ],
    )


def token_kernel(
    own_ref,
    core_ref,
    last_x_ref,
    last_y_ref,
    gates_ref,
    router_ref,
    hidden_ref,
    factor_ref,
    gain_ref,
    grad_ref,
    normed_ref,
    weight_ref,
    hidden_grad_ref,
    branch_ref,
    mixed_grad_ref,
    extras_ref,
):
    copies = sum(ref[...].astype(F32) for ref in (own_ref, core_ref, last_x_ref, last_y_ref))
    columns, gates = copies[:, D:], gates_ref[: copies.shape[0]]
    gate_grad = columns + pltpu.roll(columns, EXTRA - 8, 1)
    inner_sum = jnp.sum(gates * gate_grad, axis=1, keepdims=True)
    logit_grad = (gates * (gate_grad - inner_sum)).astype(BF)
    gradient = copies[:, :D] + dot(logit_grad, router_ref[...], 1, 1)
    hidden, factor = hidden_ref[...], factor_ref[...]
    scaled = gradient * gain_ref[1:2]
    inner_mean = jnp.mean(scaled * hidden, axis=-1, keepdims=True)
    part = factor * scaled - hidden * (factor * factor * factor * inner_mean)
    hidden_grad = grad_ref[...].astype(F32) + part
    hidden_grad_ref[...] = hidden_grad
    branch = hidden_grad.astype(BF)
    branch_ref[...] = branch
    mixed_grad_ref[...] = dot(weight_ref[...], branch, 1, 1).astype(BF)
    gain_grad = jnp.sum(gradient * hidden * factor, axis=0, keepdims=True)
    router_grad = dot(logit_grad, normed_ref[...], 0, 0)
    row = lax.broadcasted_iota(jnp.int32, router_grad.shape, 0)
    extras_ref[...] = jnp.where(row == 8, gain_grad, router_grad)


def put_cut(me_ref, scratch, same_ref, other_ref):
    core, chip = lax.rem(me_ref[0], 2), lax.div(me_ref[0], 2)
    rows = same_ref.shape[2]
    for n in range(4):
        for side, ref in enumerate((same_ref, other_ref)):
            device = 2 * (chip ^ n) + (core ^ side)
            for a in range(4):
                start = pl.multiple_of((a * 8 + device) * rows, 16)
                ref[n, a] = scratch[pl.ds(start, rows), :]


def cut_shapes(rows, width):
    return [jax.ShapeDtypeStruct((4, 4, rows, width), BF)] * 2


def output_kernel(me_ref, mixed_ref, branch_ref, extras_ref, same_ref, other_ref, scratch):
    scratch[:, :D] = dot(mixed_ref[...], branch_ref[...], 1, 0).astype(BF)
    scratch[:, D:] = extras_ref[...].T.astype(BF)
    put_cut(me_ref, scratch, same_ref, other_ref)


def turned_back(value, cosine, sine):
    half = HD // 2
    first, second = value[:half], value[half:]
    return jnp.concatenate(
        [first * cosine + second * sine, second * cosine - first * sine], axis=0
    )


def query_kernel(
    me_ref, query_ref, cosine_ref, sine_ref, normed_ref, part_ref, same_ref, other_ref, scratch
):
    for h in range(H):
        part = turned_back(query_ref[h], cosine_ref[...], sine_ref[...])
        part_ref[h * HD : (h + 1) * HD] = part.astype(BF)
    scratch[...] = dot(normed_ref[...], part_ref[...], 0, 1).astype(BF)
    put_cut(me_ref, scratch, same_ref, other_ref)


def late_kernel(
    me_ref,
    own_ref,
    last_x_ref,
    last_y_ref,
    cosine_ref,
    sine_ref,
    normed_ref,
    part_ref,
    same_ref,
    other_ref,
    scratch,
):
    value = sum(ref[...].astype(F32) for ref in (own_ref, last_x_ref, last_y_ref)).T
    for h in range(KVH):
        part = turned_back(value[h * HD : (h + 1) * HD], cosine_ref[...], sine_ref[...])
        part_ref[h * HD : (h + 1) * HD] = part.astype(BF)
    part_ref[KW:] = value[KW:].astype(BF)
    scratch[...] = dot(normed_ref[...], part_ref[...], 0, 1).astype(BF)
    put_cut(me_ref, scratch, same_ref, other_ref)


def sums_kernel(same_ref, arrived_ref, own_ref, by_x_ref, by_y_ref, low_ref, high_ref):
    for n, ref in enumerate((own_ref, by_x_ref, by_y_ref)):
        ref[...] = total(same_ref[n], arrived_ref[n])
    for half, ref in enumerate((low_ref, high_ref)):

        @pl.when(pl.program_id(0) == half)
        def _():
            ref[...] = total(same_ref[3], arrived_ref[3])


def sums_call(same, arrived):
    _, parts, rows, width = same.shape
    half = parts // 2
    both = pl.BlockSpec((4, half, rows, width), lambda i: (0, i, 0, 0))
    one = pl.BlockSpec((half, rows, width), lambda i: (i, 0, 0))
    fixed = pl.BlockSpec((half, rows, width), lambda i: (0, 0, 0))
    shape = jax.ShapeDtypeStruct
    return glue_call(
        sums_kernel,
        [shape((parts, rows, width), BF)] * 3 + [shape((half, rows, width), BF)] * 2,
        same,
        arrived,
        grid=(2,),
        in_specs=[both] * 2,
        out_specs=[one] * 3 + [fixed] * 2,
    )


def over_hops(sums):
    return hop(sums[3], 2), hop(sums[4], 4)


def join_kernel(by_x_ref, by_y_ref, over_x_ref, over_y_ref, new_x_ref, new_y_ref):
    new_y_ref[...] = total(by_y_ref[...], over_x_ref[...])
    new_x_ref[...] = total(by_x_ref[...], over_y_ref[...])


def join_call(sums, over):
    by_x, by_y = sums[1:3]
    half = (by_x.shape[0] // 2, *by_x.shape[1:])
    low = pl.BlockSpec(half, lambda i: (0, 0, 0))
    high = pl.BlockSpec(half, lambda i: (1, 0, 0))
    return glue_call(
        join_kernel,
        [jax.ShapeDtypeStruct(by_x.shape, BF)] * 2,
        by_x,
        by_y,
        *over,
        grid=(1,),
        in_specs=[high, low, low, low],
        out_specs=[high, low],
        input_output_aliases={0: 0, 1: 1},
    )


def both_kernel(x0_ref, x1_ref, y0_ref, y1_ref, over_x_ref, over_y_ref, new_x_ref, new_y_ref):
    half = over_x_ref.shape[0]
    by_x = x0_ref[...].astype(F32) + x1_ref[...].astype(F32)
    by_y = y0_ref[...].astype(F32) + y1_ref[...].astype(F32)
    new_x_ref[:half] = by_x[:half].astype(BF)
    new_x_ref[half:] = (by_x[half:] + over_y_ref[...].astype(F32)).astype(BF)
    new_y_ref[:half] = (by_y[:half] + over_x_ref[...].astype(F32)).astype(BF)
    new_y_ref[half:] = by_y[half:].astype(BF)


def both_call(by_x, x_core, by_y, y_core, over):
    return glue_call(
        both_kernel,
        [jax.ShapeDtypeStruct(by_x.shape, BF)] * 2,
        by_x,
        x_core,
        by_y,
        y_core,
        *over,
        scalars=0,
    )


def send_kernel(place_ref, *refs):
    groups, outs = (len(refs) - 4) // 3, refs[-4:]
    start = 0
    for g in range(groups):
        own_ref, last_x_ref, last_y_ref = refs[3 * g : 3 * g + 3]
        size = own_ref.shape[2]
        for step, out in enumerate(outs):
            at = lax.rem(place_ref[0] + step, 4)
            value = sum(ref[at].astype(F32) for ref in (own_ref, last_x_ref, last_y_ref))
            out[:, start : start + size] = value.astype(out.dtype)
        start += size


def send_call(*groups):
    rows, width = groups[0][0].shape[1], sum(group[0].shape[2] for group in groups)
    shape = jax.ShapeDtypeStruct
    own, *sent = glue_call(
        send_kernel,
        [shape((rows, width), F32)] + [shape((rows, width), BF)] * 3,
        lax.axis_index("dp")[None],
        *[part for group in groups for part in group],
    )
    return own, [
        lax.ppermute(value, "dp", [(i, (i + step) % 4) for i in range(4)])
        for step, value in enumerate(sent, 1)
    ]


def adam_kernel(pieces, step_rate, shrink, weight_ref, moment_ref, square_ref, *refs):
    grads, outs = refs[: len(pieces)], refs[len(pieces) :]
    for ref, (_, _, parts) in zip(grads, pieces):
        for source, target, size in parts:
            columns = slice(target, target + size)
            news = adam_update(
                weight_ref[:, columns],
                moment_ref[:, columns],
                square_ref[:, columns],
                ref[:, source : source + size].astype(F32),
                step_rate,
                shrink,
            )
            for out, new in zip(outs, news):
                out[:, columns] = new


def adam_call(weight, moment, square, pieces, step_rate, shrink, rows):
    width = weight.shape[2]
    state = pl.BlockSpec((None, rows, width), lambda i: (0, i, 0))
    return pl.pallas_call(
        lambda *refs: adam_kernel(pieces, step_rate, shrink, *refs),
        grid=(weight.shape[1] // rows,),
        in_specs=[state] * 3
        + [
            pl.BlockSpec((rows, piece.shape[1]), lambda i, first=first: (first + i, 0))
            for piece, first, _ in pieces
        ],
        out_specs=[state] * 3,
        out_shape=[jax.ShapeDtypeStruct(weight.shape, F32)] * 3,
        compiler_params=pltpu.CompilerParams(vmem_limit_bytes=VMEM_BYTES),
        cost_estimate=HINT,
    )(weight, moment, square, *[piece for piece, _, _ in pieces])


def owned_kernel(step_rate, weight_ref, moment_ref, square_ref, own_ref, *refs):
    arrived, outs, rest = refs[:3], refs[3:6], refs[6]
    total_grad = own_ref[...] + sum(ref[...].astype(F32) for ref in arrived)
    size = weight_ref.shape[1]
    weight, gradient = weight_ref[...], total_grad[:, :size]
    news = adam_update(
        weight, moment_ref[...], square_ref[...], gradient, step_rate, weight_decay
    )
    for out, new in zip(outs, news):
        out[...] = new
    if total_grad.shape[1] > size:
        rest[...] = total_grad[:, size:]
    else:
        products = jnp.sum(weight.astype(BF).astype(F32) * gradient, axis=1, keepdims=True)
        rest[...] = jnp.broadcast_to(products, rest.shape)


def owned_call(weight, moment, square, sums, step_rate):
    vmem = pl.BlockSpec(memory_space=pltpu.VMEM)
    state = jax.ShapeDtypeStruct(weight.shape, F32)
    return pl.pallas_call(
        lambda *refs: owned_kernel(step_rate, *refs),
        in_specs=[vmem] * 7,
        out_specs=[vmem] * 4,
        out_shape=[state] * 3 + [jax.ShapeDtypeStruct((weight.shape[0], EXTRA), F32)],
        compiler_params=pltpu.CompilerParams(vmem_limit_bytes=VMEM_BYTES),
        cost_estimate=HINT,
    )(weight, moment, square, *sums)


def input_kernel(query_ref, late_ref, weight_ref, tokens_ref, factor_ref, gain_ref, grad_ref, out_ref):
    gradient = dot(query_ref[...], weight_ref[:, :QW], 0, 1)
    gradient = gradient + dot(late_ref[...], weight_ref[:, QW:QKV], 0, 1)
    tokens, factor = tokens_ref[...].astype(F32), factor_ref[...]
    scaled = gradient * gain_ref[:1]
    inner_mean = jnp.mean(scaled * tokens, axis=-1, keepdims=True)
    part = factor * scaled - tokens * (factor * factor * factor * inner_mean)
    out_ref[...] = grad_ref[...] + part


def input_call(*operands):
    vmem = pl.BlockSpec(memory_space=pltpu.VMEM)
    return pl.pallas_call(
        input_kernel,
        in_specs=[vmem] * 7,
        out_specs=vmem,
        out_shape=jax.ShapeDtypeStruct(operands[-1].shape, F32),
        compiler_params=pltpu.CompilerParams(vmem_limit_bytes=VMEM_BYTES),
        cost_estimate=HINT,
    )(*operands)


def gated(gate, up):
    rate = (2.0 / jnp.pi) ** 0.5
    bend = 0.044715 * rate
    square = gate * gate
    part = 0.5 + 0.5 * jnp.tanh(gate * (rate + bend * square))
    gelu = gate * part
    slope = part + gelu * (1.0 - part) * (2.0 * rate + 6.0 * bend * square)
    return gelu * up, slope * up, gelu


def local(
    inputs,
    cotangent,
    routes,
    project_weight,
    project_moment,
    project_square,
    output_weight,
    output_moment,
    output_square,
    router_weight,
    router_moment,
    router_square,
    norm_gains,
    gains_moment,
    gains_square,
    expert_in,
    expert_in_moment,
    expert_in_square,
    expert_down,
    expert_down_moment,
    expert_down_square,
):
    seq_count, stretch, width = inputs.shape
    device_count = lax.axis_size("expert")
    expert_count = device_count
    rows = seq_count * stretch
    me = lax.axis_index("expert")
    others = me ^ jnp.arange(device_count, dtype=jnp.int32)
    shard = project_weight.shape[0]

    first_payload = jnp.concatenate(
        [
            project_weight.astype(BF),
            router_weight.astype(BF),
            norm_gains.T.astype(BF),
            jnp.zeros((shard, EXTRA - expert_count - 2), BF),
        ],
        axis=1,
    )
    first_hops = [first_payload] + [plane_hop(first_payload, step) for step in (1, 2, 3)]
    own_grad = cotangent.reshape(rows, width)
    grad_near = gather_near(own_grad)
    in_low, down_low = expert_in[0].astype(BF), expert_down[0].astype(BF)
    share_first, share_second = [
        jnp.concatenate([in_low[:, p * HALF : (p + 1) * HALF] for p in (h, h + 2)], axis=1)
        for h in range(2)
    ]
    share_first = jnp.concatenate(
        [share_first, down_low[:, : 2 * HALF], down_low[:, 2 * HALF :]], axis=0
    )
    first_hops, grad_near, inputs, routes, output_low, place = phase(
        first_hops, grad_near, inputs, routes, output_weight, me
    )

    first_plane = plane_end(first_hops)
    first_near = gather_near(first_plane)
    output_low = output_low.astype(BF)
    output_hops = [output_low] + [plane_hop(output_low, step) for step in (1, 2, 3)]
    positions = place * stretch + jnp.arange(stretch, dtype=jnp.int32)
    frequency = rope_base ** (-jnp.arange(HD // 2, dtype=F32) / (HD // 2))
    angles = frequency[:, None] * positions.astype(F32)[None, :]
    cosine = jnp.tile(jnp.cos(angles), (1, seq_count))
    sine = jnp.tile(jnp.sin(angles), (1, seq_count))
    route_rows = jnp.concatenate(
        [routes.reshape(rows, TOP).T.astype(BF), jnp.zeros((32 - TOP, rows), BF)], axis=0
    )
    first_near, output_hops, share_first, share_second, cosine, sine, route_rows = phase(
        first_near, output_hops, share_first, share_second, cosine, sine, route_rows
    )

    weights_first = lax.all_gather(share_first, "dp")
    weights_second = lax.all_gather(share_second, "dp")
    first_over, first_later = gather_over(first_near)
    first_cores = gather_cores(first_later)
    first_sibling = hop(after(first_plane, *first_later), 1)
    output_plane = plane_end(output_hops)
    first_over, first_cores, first_sibling, output_plane = phase(
        first_over, first_cores, first_sibling, output_plane
    )

    first_far = hop(first_over[0], 1), hop(first_over[1], 1)
    output_near, output_sibling = gather_near(output_plane), hop(output_plane, 1)
    first_far = phase(first_far)[0]

    inputs = inputs.reshape(rows, width)
    shape = jax.ShapeDtypeStruct
    queries, pair_payload, normed_one, factor_one, gains, router, full_first = assembled_call(
        project_kernel,
        [
            shape((H, HD, rows), BF),
            shape((2 * KW + 32, rows), BF),
            shape((rows, width), BF),
            shape((rows, 1), F32),
            shape((8, D), F32),
            shape((D, EXTRA), BF),
        ],
        (D, QKV + EXTRA),
        me[None],
        [
            first_plane,
            first_sibling,
            first_near[0],
            first_cores[0],
            first_near[1],
            first_cores[1],
            *first_over,
            *first_far,
        ],
        inputs,
        cosine,
        sine,
        route_rows,
    )
    pair_payload, output_near, output_sibling, queries = phase(
        pair_payload, output_near, output_sibling, queries
    )

    key_positions = (others[:, None] * stretch + jnp.arange(stretch)[None, :]).reshape(-1)
    bias = jnp.where(key_positions[:, None] <= positions[None, :], 0.0, masked_score).astype(F32)
    pair_near, pair_sibling = gather_near(pair_payload), hop(pair_payload, 1)
    output_over, _ = gather_over(output_near)
    pair_near, pair_sibling, output_over, bias = phase(pair_near, pair_sibling, output_over, bias)

    pair_over, pair_later = gather_over(pair_near)
    pair_cores = gather_cores(pair_later)
    output_core_x = hop(after(output_near[0], *pair_later), 1)
    pair_over, pair_cores, output_core_x = phase(pair_over, pair_cores, output_core_x)

    pair_diagonal = jnp.concatenate(pair_over, axis=0)
    pair_core, output_core_y = hop(pair_diagonal, 1), hop(output_near[1], 1)
    output_far = hop(output_over[0], 1), hop(output_over[1], 1)
    pair_core, output_core_y, output_far = phase(pair_core, output_core_y, output_far)

    pair_blocks = gathered(
        pair_payload, pair_sibling, pair_near, pair_cores, pair_diagonal, pair_core
    )
    pairs = jnp.stack(pair_blocks)
    lanes = jnp.arange(EXTRA, dtype=jnp.int32)[None, :]
    grad_over, _ = gather_over(grad_near)
    grad_cores = gather_cores(grad_near)
    grad_sibling = hop(own_grad, 1)
    mixed, lse = attention_call(
        forward_kernel,
        [shape((H, HD, rows), F32), shape((seq_count, H, stretch), F32)],
        ["head", "row"],
        queries,
        pairs,
        bias,
    )
    mixed, lse, grad_over, grad_cores, grad_sibling = phase(
        mixed, lse, grad_over, grad_cores, grad_sibling
    )

    hidden_one, normed_two, factor_two, mixed_rows, full_output = assembled_call(
        attended_kernel,
        [
            shape((rows, width), F32),
            shape((rows, width), BF),
            shape((rows, 1), F32),
            shape((QW, rows), BF),
        ],
        (QW, D),
        me[None],
        [
            output_plane,
            output_sibling,
            output_near[0],
            output_core_x,
            output_near[1],
            output_core_y,
            *output_over,
            *output_far,
        ],
        mixed,
        inputs,
        gains,
    )

    row_near, row_sibling = gather_near(normed_two), hop(normed_two, 1)
    grad_diagonal = jnp.concatenate(grad_over, axis=0)
    grad_core = hop(grad_diagonal, 1)
    back_near = back_call(
        [own_grad, grad_sibling, grad_near[0], grad_cores[0], grad_near[1], grad_cores[1]],
        after(weights_first, normed_two),
    )
    row_near, row_sibling, grad_core, back_near = phase(
        row_near, row_sibling, grad_core, back_near
    )
    grad_blocks = gathered(
        own_grad, grad_sibling, grad_near, grad_cores, grad_diagonal, grad_core
    )
    row_over, row_later = gather_over(row_near)
    row_cores = gather_cores(row_later)
    all_routes = jnp.concatenate(
        [block[2 * KW : 2 * KW + TOP].T for block in pair_blocks], axis=0
    ).astype(jnp.int32)
    named = jnp.any(all_routes[:, :, None] == lanes[None], axis=1)
    route_bias = jnp.where(named, 0.0, masked_score).astype(F32)
    back_far = back_call(grad_blocks[6:], weights_first)
    row_over, row_cores, route_bias, back_far = phase(row_over, row_cores, route_bias, back_far)
    back = (back_near, back_far)
    row_diagonal = jnp.concatenate(row_over, axis=0)
    row_core = phase(hop(row_diagonal, 1))[0]
    row_blocks = gathered(normed_two, row_sibling, row_near, row_cores, row_diagonal, row_core)
    gates, gate_grad_first, up_first, hidden_first, in_grad_first = first_call(
        me[None], row_blocks, back, route_bias, weights_first, router
    )
    grads_first = lax.psum_scatter(in_grad_first, "dp")

    def second_part(t, *others):
        return second_call(
            t,
            me[None],
            row_blocks,
            back,
            gates,
            gate_grad_first,
            after(up_first, *others),
            hidden_first,
            weights_first,
            weights_second,
        )

    far = second_part(3)
    far_cores = hop(far[1], 1), hop(far[3], 1)
    by_y = second_part(2, far[0])
    far_cores, _ = phase(far_cores, by_y[0])
    diagonal = total(far[0], far_cores[0])
    copy_over = reduce_over(diagonal)
    by_y_cores = hop(by_y[1], 1), hop(by_y[3], 1)
    result_diagonal = total(far[2], far_cores[1])
    by_x = second_part(1, diagonal, result_diagonal)
    copy_over, by_y_cores, _, result_diagonal = phase(
        copy_over, by_y_cores, by_x[0], result_diagonal
    )
    result_over, by_x_cores = reduce_over(result_diagonal), (hop(by_x[1], 1), hop(by_x[3], 1))
    own = second_part(0, by_x[0])
    result_over, by_x_cores, _ = phase(result_over, by_x_cores, own[0])
    copy_last = both_call(by_x[0], by_x_cores[0], by_y[0], by_y_cores[0], copy_over)
    last = last_hops(*copy_last)
    own_cores = hop(own[1], 1), hop(own[3], 1)
    result_last = both_call(
        by_x[2], after(by_x_cores[1], *copy_last), by_y[2], by_y_cores[1], result_over
    )
    parts = (own, by_x, by_y, far)
    weight_grads = last_call(
        row_blocks,
        grad_blocks,
        [part[4] for part in parts],
        [part[5] for part in parts],
        after(hidden_first, *result_last, grads_first),
    )
    last, own_cores, weight_grads, result_last = phase(last, own_cores, weight_grads, result_last)
    grads_second = lax.psum_scatter(weight_grads, "dp")
    result_hops = last_hops(*result_last)

    hidden_grad_one, branch_grad, mixed_grad, extras = glue_call(
        token_kernel,
        [
            jax.ShapeDtypeStruct((rows, width), F32),
            jax.ShapeDtypeStruct((rows, width), BF),
            jax.ShapeDtypeStruct((QW, rows), BF),
            jax.ShapeDtypeStruct((EXTRA, D), F32),
        ],
        own[0],
        own_cores[0],
        *last,
        gates,
        router,
        hidden_one,
        factor_two,
        gains,
        own_grad,
        normed_two,
        full_output,
        scalars=0,
    )
    mixed_grad = mixed_grad.reshape(H, HD, rows)
    mixed_grad, branch_grad, extras, hidden_grad_one = phase(
        mixed_grad, branch_grad, extras, hidden_grad_one
    )

    query_grad, pairs_same, pairs_other = attention_call(
        backward_kernel,
        [
            jax.ShapeDtypeStruct((H, HD, rows), F32),
            jax.ShapeDtypeStruct((4, rows, 2 * KW), BF),
            jax.ShapeDtypeStruct((4, rows, 2 * KW), BF),
        ],
        ["head"] + [pl.BlockSpec((4, stretch, 2 * KW), lambda s: (0, s, 0))] * 2,
        queries,
        pairs,
        bias,
        mixed,
        lse,
        mixed_grad,
    )
    query_grad, pairs_same, pairs_other, cosine, sine, result_hops = phase(
        query_grad, pairs_same, pairs_other, cosine, sine, result_hops
    )

    pair_cores = hop(pairs_other, 1)
    output_same, output_other = glue_call(
        output_kernel,
        cut_shapes(shard, D + EXTRA),
        me[None],
        mixed_rows,
        branch_grad,
        extras,
        scratch_shapes=[pltpu.VMEM((QW, D + EXTRA), BF)],
    )
    pair_cores, output_same, output_other = phase(pair_cores, output_same, output_other)

    quarters = (4, 4, rows // 4, 2 * KW)
    pair_sums = sums_call(pairs_same.reshape(quarters), pair_cores.reshape(quarters))
    pair_over, output_cores = over_hops(pair_sums), hop(output_other, 1)
    query_part, query_same, query_other = glue_call(
        query_kernel,
        [jax.ShapeDtypeStruct((QW, rows), BF)] + cut_shapes(shard, QW),
        me[None],
        after(query_grad, *pair_sums),
        cosine,
        sine,
        normed_one,
        scratch_shapes=[pltpu.VMEM((D, QW), BF)],
    )
    pair_over, pair_sums, query_same, query_other, query_part, output_cores = phase(
        pair_over, pair_sums, query_same, query_other, query_part, output_cores
    )

    pair_last = join_call(pair_sums, pair_over)
    pair_hops, query_cores = last_hops(*pair_last), hop(query_other, 1)
    output_sums = sums_call(output_same, after(output_cores, *pair_last))
    output_over = over_hops(output_sums)
    pair_hops, query_cores, output_sums, output_over = phase(
        pair_hops, query_cores, output_sums, output_over
    )

    late_part, late_same, late_other = glue_call(
        late_kernel,
        [jax.ShapeDtypeStruct((2 * KW, rows), BF)] + cut_shapes(shard, 2 * KW),
        me[None],
        *[value.reshape(rows, 2 * KW) for value in (pair_sums[0], *pair_hops)],
        cosine,
        sine,
        normed_one,
        scratch_shapes=[pltpu.VMEM((D, 2 * KW), BF)],
    )
    late_cores = hop(late_other, 1)
    output_last = join_call(output_sums, after(output_over, late_other))
    output_hops = last_hops(*output_last)
    query_sums = sums_call(query_same, after(query_cores, *output_last))
    query_over = over_hops(query_sums)
    output_hops, late_cores, late_same, late_part, query_sums, query_over = phase(
        output_hops, late_cores, late_same, late_part, query_sums, query_over
    )

    late_sums = sums_call(late_same, late_cores)
    late_over = over_hops(late_sums)
    query_last = join_call(query_sums, after(query_over, *late_sums))
    query_hops = last_hops(*query_last)
    input_grad = input_call(
        query_part,
        after(late_part, *query_last),
        full_first,
        inputs,
        factor_one,
        gains,
        hidden_grad_one,
    )
    late_over, query_hops, late_sums, input_grad = phase(
        late_over, query_hops, late_sums, input_grad
    )

    late_last = join_call(late_sums, late_over)
    late_hops = last_hops(*late_last)
    output_own, output_arrived = send_call(
        (output_sums[0], *after(output_hops, *late_last))
    )
    grads_first, grads_second = phase(grads_first, grads_second, output_own, late_last)[:2]
    in_new = adam_call(
        expert_in,
        expert_in_moment,
        expert_in_square,
        [
            (grads_first, 0, [(0, 0, HALF), (HALF, FF, HALF)]),
            (grads_second, 0, [(0, HALF, HALF), (HALF, FF + HALF, HALF)]),
        ],
        3.0 / D**0.5,
        weight_decay,
        ROWS // 4,
    )
    down_new = adam_call(
        expert_down,
        expert_down_moment,
        expert_down_square,
        [
            (grads_second, 4, [(0, 0, 2 * HALF)]),
            (grads_second, 6, [(0, 2 * HALF, 2 * HALF)]),
        ],
        12.0 / FF**0.5,
        weight_decay,
        ROWS // 4,
    )
    late_hops, output_arrived, output_own, in_new, down_new = phase(
        late_hops, output_arrived, output_own, in_new, down_new
    )

    project_own, project_arrived = send_call(
        (query_sums[0], *query_hops), (late_sums[0], *late_hops)
    )
    output_own = after(output_own, project_own)
    sequence = stretch * device_count
    *output_new, output_rest = owned_call(
        output_weight,
        output_moment,
        output_square,
        [output_own, *output_arrived],
        3.0 * (sequence / (32.0 * H * HD)) ** 0.5,
    )
    outputs = hidden_one + reduced(
        total(own[2], after(own_cores[1], output_rest)), result_hops
    )
    rest = output_rest.T
    router_new = [
        new.T
        for new in adam_update(
            router_weight.T,
            router_moment.T,
            router_square.T,
            rest[:expert_count],
            1.5 / D**0.5,
            weight_decay,
        )
    ]
    project_arrived, output_new, rest, outputs, router_new = phase(
        project_arrived, output_new, rest, outputs, router_new
    )
    *project_new, products = owned_call(
        project_weight,
        project_moment,
        project_square,
        [project_own, *project_arrived],
        3.0 * (2.0 / D) ** 0.5,
    )
    own_gains = norm_gains.astype(BF).astype(F32)
    gains_sum = jnp.stack([products[:, 0] / own_gains[0], rest[expert_count]])
    gains_new = adam_update(norm_gains, gains_moment, gains_square, gains_sum, 0.8, 0.0)
    return (
        outputs.reshape(seq_count, stretch, width),
        input_grad.reshape(seq_count, stretch, width),
        *project_new,
        *output_new,
        *router_new,
        *gains_new,
        *in_new,
        *down_new,
    )


def rms_norm(values, gain_row):
    factor = lax.rsqrt(jnp.mean(values * values, axis=-1, keepdims=True) + norm_epsilon)
    return values * factor * gain_row


def rotate(values, positions):
    half_width = values.shape[-1] // 2
    frequency = rope_base ** (-jnp.arange(half_width, dtype=jnp.float32) / half_width)
    angles = positions.astype(jnp.float32)[:, None] * frequency[None, :]
    cosine = jnp.cos(angles)[:, None, :]
    sine_part = jnp.sin(angles)[:, None, :]
    first_half = values[..., :half_width]
    second_half = values[..., half_width:]
    return jnp.concatenate(
        [
            first_half * cosine - second_half * sine_part,
            second_half * cosine + first_half * sine_part,
        ],
        axis=-1,
    )


def gated_unit(gate_up):
    return jax.nn.gelu(gate_up[..., :FF], approximate=True) * gate_up[..., FF:]


def slot_tables(route_block, expert_count, capacity):
    flat_routes = route_block.reshape(-1)
    pick_count = flat_routes.shape[0]
    onehot = (flat_routes[:, None] == jnp.arange(expert_count, dtype=jnp.int32)[None, :]).astype(
        jnp.int32
    )
    earlier = jnp.cumsum(onehot, axis=0) - onehot
    rank_values = jnp.sum(earlier * onehot, axis=1)
    slot_index = flat_routes * capacity + rank_values
    slot_table = (
        jnp.full((expert_count * capacity,), pick_count, jnp.int32)
        .at[slot_index]
        .set(jnp.arange(pick_count, dtype=jnp.int32))
    )
    return (slot_index, slot_table)


def attention_blocks(step_fn, carried, key_values, last_query):
    key_count = key_values.shape[1]
    block_keys = 512

    def one_turn(turn_index, state_now):
        offset = turn_index * block_keys
        key_block = lax.dynamic_slice_in_dim(key_values, offset, block_keys, 1)
        return lax.cond(
            offset > last_query,
            lambda held_state: held_state,
            lambda held_state: step_fn(held_state, key_block, offset),
            state_now,
        )

    return lax.fori_loop(0, key_count // block_keys, one_turn, carried)


def general(
    inputs,
    cotangent,
    routes,
    project_weight,
    project_moment,
    project_square,
    output_weight,
    output_moment,
    output_square,
    router_weight,
    router_moment,
    router_square,
    norm_gains,
    gains_moment,
    gains_square,
    expert_in,
    expert_in_moment,
    expert_in_square,
    expert_down,
    expert_down_moment,
    expert_down_square,
):
    seq_count, stretch_len, model_width = inputs.shape
    expert_devices = lax.axis_size("expert")
    seq_length = stretch_len * expert_devices
    expert_count = EXP_DEV * expert_devices
    row_count = seq_count * stretch_len
    capacity = 2 * row_count * TOP // expert_count
    group_size = H // KVH
    query_width = H * HD
    key_width = KVH * HD
    group_rows = group_size * stretch_len
    score_scale = HD ** (-0.5)
    first_query = lax.axis_index("expert") * stretch_len
    last_query = first_query + stretch_len - 1
    full_project, full_output, full_router, full_gains = (
        lax.all_gather(project_weight.astype(jnp.bfloat16), ("dp", "expert"), axis=0, tiled=True),
        lax.all_gather(output_weight.astype(jnp.bfloat16), ("dp", "expert"), axis=0, tiled=True),
        lax.all_gather(router_weight.astype(jnp.bfloat16), ("dp", "expert"), axis=0, tiled=True),
        lax.all_gather(norm_gains.astype(jnp.bfloat16), ("dp", "expert"), axis=1, tiled=True),
    )
    full_in, full_down = (
        lax.all_gather(expert_in.astype(jnp.bfloat16), "dp", axis=1, tiled=True),
        lax.all_gather(expert_down.astype(jnp.bfloat16), "dp", axis=1, tiled=True),
    )
    gain_values = full_gains.astype(jnp.float32)
    tokens = inputs.astype(jnp.float32).reshape(row_count, model_width)
    normed_one = rms_norm(tokens, gain_values[0]).astype(jnp.bfloat16)
    projected = jnp.dot(normed_one, full_project, preferred_element_type=jnp.float32).reshape(
        seq_count, stretch_len, -1
    )
    positions = first_query + jnp.arange(stretch_len, dtype=jnp.int32)

    def rope_back(gradient):
        unused, pullback = jax.vjp(
            lambda values: rotate(values, positions), jnp.zeros_like(gradient)
        )
        return pullback(gradient)[0]

    queries = rotate(
        projected[..., :query_width].reshape(seq_count, stretch_len, H, HD), positions
    ).astype(jnp.bfloat16)
    rotated_keys = rotate(
        projected[..., query_width : query_width + key_width].reshape(
            seq_count, stretch_len, KVH, HD
        ),
        positions,
    ).astype(jnp.bfloat16)
    values = projected[..., query_width + key_width :].astype(jnp.bfloat16)
    local_pairs = jnp.concatenate(
        [rotated_keys.reshape(seq_count, stretch_len, key_width), values], axis=-1
    )
    all_pairs = lax.all_gather(local_pairs, "expert", axis=1, tiled=True)

    def to_grid(token_rows):
        return (
            token_rows.reshape(seq_count, stretch_len, KVH, group_size, HD)
            .transpose(0, 2, 3, 1, 4)
            .reshape(seq_count, KVH, group_rows, HD)
        )

    def from_grid(grid_rows):
        return (
            grid_rows.reshape(seq_count, KVH, group_size, stretch_len, HD)
            .transpose(0, 3, 1, 2, 4)
            .reshape(row_count, query_width)
        )

    query_grid = to_grid(queries)
    row_positions = first_query + jnp.arange(group_rows, dtype=jnp.int32) % stretch_len

    def scores_for(sequence, key_block, offset):
        key_part = key_block[sequence, :, :key_width].reshape(-1, KVH, HD)
        raw_scores = (
            jnp.einsum(
                "krd,nkd->krn", query_grid[sequence], key_part, preferred_element_type=jnp.float32
            )
            * score_scale
        )
        key_positions = offset + jnp.arange(key_block.shape[1], dtype=jnp.int32)
        allowed = (key_positions[None, :] <= row_positions[:, None])[None]
        return (raw_scores, allowed)

    def stats_step(carried, key_block, offset):
        top_now, total_now = carried
        new_tops = []
        new_totals = []
        for sequence in range(seq_count):
            raw_scores, allowed = scores_for(sequence, key_block, offset)
            masked = jnp.where(allowed, raw_scores, masked_score)
            top_new = jnp.maximum(top_now[sequence], jnp.max(masked, axis=-1))
            weights = jnp.where(allowed, jnp.exp(masked - top_new[..., None]), 0.0)
            new_totals.append(
                total_now[sequence] * jnp.exp(top_now[sequence] - top_new)
                + jnp.sum(weights, axis=-1)
            )
            new_tops.append(top_new)
        return (jnp.stack(new_tops), jnp.stack(new_totals))

    stats_shape = (seq_count, KVH, group_rows)
    top_all, total_all = attention_blocks(
        stats_step,
        (jnp.full(stats_shape, masked_score, jnp.float32), jnp.zeros(stats_shape, jnp.float32)),
        all_pairs,
        last_query,
    )
    log_total = top_all + jnp.log(total_all)

    def softmax_for(sequence, key_block, offset):
        raw_scores, allowed = scores_for(sequence, key_block, offset)
        return jnp.where(
            allowed,
            jnp.exp(jnp.where(allowed, raw_scores, masked_score) - log_total[sequence][..., None]),
            0.0,
        )

    def mix_step(carried, key_block, offset):
        new_rows = []
        for sequence in range(seq_count):
            softmax_rows = softmax_for(sequence, key_block, offset).astype(jnp.bfloat16)
            value_part = key_block[sequence, :, key_width:].reshape(-1, KVH, HD)
            new_rows.append(
                carried[sequence]
                + jnp.einsum(
                    "krn,nkd->krd", softmax_rows, value_part, preferred_element_type=jnp.float32
                )
            )
        return jnp.stack(new_rows)

    mixed_grid = attention_blocks(
        mix_step, jnp.zeros((seq_count, KVH, group_rows, HD), jnp.float32), all_pairs, last_query
    )
    mixed_rows = from_grid(mixed_grid).astype(jnp.bfloat16)
    hidden_one = tokens + jnp.dot(mixed_rows, full_output, preferred_element_type=jnp.float32)
    normed_two = rms_norm(hidden_one, gain_values[1]).astype(jnp.bfloat16)
    logits = jnp.dot(normed_two, full_router, preferred_element_type=jnp.float32)
    route_rows = routes.reshape(row_count, TOP)
    onehot = (
        route_rows[:, :, None] == jnp.arange(expert_count, dtype=jnp.int32)[None, None, :]
    ).astype(jnp.float32)
    gate_weights = jax.nn.softmax(
        jnp.einsum("rte,re->rt", onehot, logits, precision=lax.Precision.HIGHEST), axis=-1
    )
    slot_index, slot_table = slot_tables(route_rows, expert_count, capacity)
    padded = jnp.concatenate([normed_two, jnp.zeros((1, model_width), jnp.bfloat16)], axis=0)
    sent_rows = padded[slot_table // TOP].reshape(expert_count, capacity, model_width)
    arrived_rows = lax.all_to_all(sent_rows, "expert", split_axis=0, concat_axis=0, tiled=True)
    batched = arrived_rows.reshape(expert_devices, EXP_DEV, -1, model_width)
    gate_up = jnp.einsum("neid,edf->neif", batched, full_in, preferred_element_type=jnp.float32)
    hidden = gated_unit(gate_up).astype(jnp.bfloat16)
    result = jnp.einsum(
        "neif,efd->neid", hidden, full_down, preferred_element_type=jnp.float32
    ).astype(jnp.bfloat16)
    results = result.reshape(arrived_rows.shape)
    kept_gate_up = gate_up.reshape(arrived_rows.shape[0], arrived_rows.shape[1], 2 * FF)
    returned = lax.all_to_all(results, "expert", split_axis=0, concat_axis=0, tiled=True)
    picked = returned.reshape(expert_count * capacity, model_width)[slot_index].reshape(
        row_count, TOP, model_width
    )
    picked_wide = picked.astype(jnp.float32)
    mixture = jnp.sum(gate_weights[:, :, None] * picked_wide, axis=1)
    outputs = hidden_one + mixture
    grad_rows = cotangent.astype(jnp.float32).reshape(row_count, model_width)
    gate_grad = jnp.sum(grad_rows[:, None, :] * picked_wide, axis=-1)
    chosen_grad = gate_weights * (
        gate_grad - jnp.sum(gate_weights * gate_grad, axis=-1, keepdims=True)
    )
    logit_grad = jnp.einsum(
        "rte,rt->re", onehot, chosen_grad, precision=lax.Precision.HIGHEST
    ).astype(jnp.bfloat16)
    copy_out_grad = (
        (gate_weights[:, :, None] * grad_rows[:, None, :])
        .astype(jnp.bfloat16)
        .reshape(row_count * TOP, model_width)
    )
    grad_sent = jnp.concatenate([copy_out_grad, jnp.zeros((1, model_width), jnp.bfloat16)], axis=0)[
        slot_table
    ].reshape(expert_count, capacity, model_width)
    grad_arrived = lax.all_to_all(grad_sent, "expert", split_axis=0, concat_axis=0, tiled=True)
    batched_grad = grad_arrived.reshape(expert_devices, EXP_DEV, -1, model_width)
    batched_in = arrived_rows.reshape(expert_devices, EXP_DEV, -1, model_width)
    gate_up = kept_gate_up.reshape(expert_devices, EXP_DEV, -1, 2 * FF)
    hidden, unit_pull = jax.vjp(gated_unit, gate_up)
    grad_down = jnp.einsum(
        "neif,neid->efd",
        hidden.astype(jnp.bfloat16),
        batched_grad,
        preferred_element_type=jnp.float32,
    )
    hidden_grad = jnp.einsum(
        "neid,efd->neif", batched_grad, full_down, preferred_element_type=jnp.float32
    )
    gate_up_grad = unit_pull(hidden_grad)[0].astype(jnp.bfloat16)
    grad_in = jnp.einsum(
        "neid,neif->edf", batched_in, gate_up_grad, preferred_element_type=jnp.float32
    )
    copy_in_grad = (
        jnp.einsum("neif,edf->neid", gate_up_grad, full_in, preferred_element_type=jnp.float32)
        .astype(jnp.bfloat16)
        .reshape(arrived_rows.shape)
    )
    expert_in_grad, expert_down_grad = (
        lax.psum_scatter(
            grad_in.astype(jnp.bfloat16), "dp", scatter_dimension=1, tiled=True
        ).astype(jnp.float32),
        lax.psum_scatter(
            grad_down.astype(jnp.bfloat16), "dp", scatter_dimension=1, tiled=True
        ).astype(jnp.float32),
    )
    returned_grad = lax.all_to_all(copy_in_grad, "expert", split_axis=0, concat_axis=0, tiled=True)
    copies_grad = returned_grad.reshape(expert_count * capacity, model_width)[slot_index].reshape(
        row_count, TOP, model_width
    )
    normed_two_grad = jnp.sum(copies_grad.astype(jnp.float32), axis=1) + jnp.dot(
        logit_grad, full_router.T, preferred_element_type=jnp.float32
    )
    router_grad_full = jnp.einsum(
        "rd,re->de", normed_two, logit_grad, preferred_element_type=jnp.float32
    )
    unused_two, norm_two_pull = jax.vjp(rms_norm, hidden_one, gain_values[1])
    hidden_part, gain_two_grad = norm_two_pull(normed_two_grad)
    hidden_grad_one = grad_rows + hidden_part
    branch_grad = hidden_grad_one.astype(jnp.bfloat16)
    output_grad_full = jnp.einsum(
        "rh,rd->hd", mixed_rows, branch_grad, preferred_element_type=jnp.float32
    )
    mixed_grad = jnp.dot(branch_grad, full_output.T, preferred_element_type=jnp.float32).astype(
        jnp.bfloat16
    )
    mixed_grad_grid = to_grid(mixed_grad.reshape(seq_count, stretch_len, H, HD))
    row_delta = jnp.sum(mixed_grad_grid.astype(jnp.float32) * mixed_grid, axis=-1)

    def back_step(carried, key_block, offset):
        query_grad, pair_grad = carried
        new_query = []
        block_len = key_block.shape[1]
        for sequence in range(seq_count):
            softmax_rows = softmax_for(sequence, key_block, offset)
            key_part = key_block[sequence, :, :key_width].reshape(-1, KVH, HD)
            value_part = key_block[sequence, :, key_width:].reshape(-1, KVH, HD)
            softmax_grad = jnp.einsum(
                "krd,nkd->krn",
                mixed_grad_grid[sequence],
                value_part,
                preferred_element_type=jnp.float32,
            )
            score_grad = (softmax_rows * (softmax_grad - row_delta[sequence][..., None])).astype(
                jnp.bfloat16
            )
            new_query.append(
                query_grad[sequence]
                + jnp.einsum(
                    "krn,nkd->krd", score_grad, key_part, preferred_element_type=jnp.float32
                )
                * score_scale
            )
            key_grad = (
                jnp.einsum(
                    "krn,krd->nkd",
                    score_grad,
                    query_grid[sequence],
                    preferred_element_type=jnp.float32,
                )
                * score_scale
            )
            value_grad = jnp.einsum(
                "krn,krd->nkd",
                softmax_rows.astype(jnp.bfloat16),
                mixed_grad_grid[sequence],
                preferred_element_type=jnp.float32,
            )
            block_grad = jnp.concatenate(
                [key_grad.reshape(block_len, key_width), value_grad.reshape(block_len, key_width)],
                axis=-1,
            )
            current = lax.dynamic_slice(
                pair_grad,
                (jnp.int32(sequence), offset, jnp.int32(0)),
                (1, block_len, 2 * key_width),
            )
            pair_grad = lax.dynamic_update_slice(
                pair_grad, current + block_grad[None], (jnp.int32(sequence), offset, jnp.int32(0))
            )
        return (jnp.stack(new_query), pair_grad)

    query_start = jnp.zeros((seq_count, KVH, group_rows, HD), jnp.float32)
    pair_start = jnp.zeros((seq_count, seq_length, 2 * key_width), jnp.float32)
    query_grad_grid, pair_grad_all = attention_blocks(
        back_step, (query_start, pair_start), all_pairs, last_query
    )
    pair_grad_local = lax.psum_scatter(
        pair_grad_all.astype(jnp.bfloat16), "expert", scatter_dimension=1, tiled=True
    ).astype(jnp.float32)
    query_grad_rows = rope_back(from_grid(query_grad_grid).reshape(seq_count, stretch_len, H, HD))
    key_grad_rows = rope_back(
        pair_grad_local[..., :key_width].reshape(seq_count, stretch_len, KVH, HD)
    )
    projected_grad = jnp.concatenate(
        [
            query_grad_rows.reshape(row_count, query_width),
            key_grad_rows.reshape(row_count, key_width),
            pair_grad_local[..., key_width:].reshape(row_count, key_width),
        ],
        axis=-1,
    ).astype(jnp.bfloat16)
    project_grad_full = jnp.einsum(
        "rd,rf->df", normed_one, projected_grad, preferred_element_type=jnp.float32
    )
    normed_one_grad = jnp.dot(projected_grad, full_project.T, preferred_element_type=jnp.float32)
    unused_one, norm_one_pull = jax.vjp(rms_norm, tokens, gain_values[0])
    token_part, gain_one_grad = norm_one_pull(normed_one_grad)
    input_grad = hidden_grad_one + token_part
    gains_grad_full = jnp.stack([gain_one_grad, gain_two_grad])
    project_grad, output_grad, router_grad, gains_grad = (
        lax.psum_scatter(project_grad_full, ("dp", "expert"), scatter_dimension=0, tiled=True),
        lax.psum_scatter(output_grad_full, ("dp", "expert"), scatter_dimension=0, tiled=True),
        lax.psum_scatter(router_grad_full, ("dp", "expert"), scatter_dimension=0, tiled=True),
        lax.psum_scatter(gains_grad_full, ("dp", "expert"), scatter_dimension=1, tiled=True),
    )
    rate_project = 3.0 * (2.0 / D) ** 0.5
    rate_output = 3.0 * (seq_length / (32.0 * H * HD)) ** 0.5
    rate_router = 1.5 / D**0.5
    rate_gains = 0.8
    rate_in = 3.0 / D**0.5
    rate_down = 12.0 / FF**0.5
    project_new = adam_update(
        project_weight, project_moment, project_square, project_grad, rate_project, weight_decay
    )
    output_new = adam_update(
        output_weight, output_moment, output_square, output_grad, rate_output, weight_decay
    )
    router_new = adam_update(
        router_weight, router_moment, router_square, router_grad, rate_router, weight_decay
    )
    gains_new = adam_update(norm_gains, gains_moment, gains_square, gains_grad, rate_gains, 0.0)
    in_new = adam_update(
        expert_in, expert_in_moment, expert_in_square, expert_in_grad, rate_in, weight_decay
    )
    down_new = adam_update(
        expert_down,
        expert_down_moment,
        expert_down_square,
        expert_down_grad,
        rate_down,
        weight_decay,
    )
    return (
        outputs.reshape(seq_count, stretch_len, model_width),
        input_grad.reshape(seq_count, stretch_len, model_width),
        project_new[0],
        project_new[1],
        project_new[2],
        output_new[0],
        output_new[1],
        output_new[2],
        router_new[0],
        router_new[1],
        router_new[2],
        gains_new[0],
        gains_new[1],
        gains_new[2],
        in_new[0],
        in_new[1],
        in_new[2],
        down_new[0],
        down_new[1],
        down_new[2],
    )


def solution(mesh):
    token_spec = P("dp", "expert", None)
    row_spec = P(("dp", "expert"), None)
    gain_spec = P(None, ("dp", "expert"))
    expert_spec = P("expert", "dp", None)
    states = (row_spec,) * 9 + (gain_spec,) * 3 + (expert_spec,) * 6
    small = mesh.shape["dp"] == 4 and mesh.shape["expert"] == 8
    return jax.shard_map(
        local if small else general,
        mesh=mesh,
        in_specs=(token_spec, token_spec, P(("dp", "expert"), None, None)) + states,
        out_specs=(token_spec, token_spec) + states,
        check_vma=False,
    )
```
